32 devices in a mesh: dp: 8 (over y, x, core), tensor: 4 (over z).
Axes of the slice: x: 2, y: 2, z: 4, core: 2. Of those that a mesh axis runs over, the one named last changes fastest.
Arguments:
- tokens: bfloat16 [15872, 768], P('dp'), may hold values from -6 to 6
- slot_kind: int32 [32], P('dp'), may hold values from 0 to 1
- offset_bucket: int32 [991], replicated, may hold values from 0 to 319
- w_query: bfloat16 [768, 768], P(None, 'tensor'), may hold values from -0.21875 to 0.21875
- b_query: bfloat16 [768], P('tensor'), may hold values from -2 to 2
- w_key: bfloat16 [768, 768], P(None, 'tensor'), may hold values from -0.21875 to 0.21875
- w_value: bfloat16 [768, 768], P(None, 'tensor'), may hold values from -0.21875 to 0.21875
- b_value: bfloat16 [768], P('tensor'), may hold values from -2 to 2
- w_out: bfloat16 [768, 768], P('tensor'), may hold values from -1.25 to 1.25
- b_out: bfloat16 [768], replicated, may hold values from -2 to 2
- gate_weight: bfloat16 [64, 8], replicated, may hold values from -0.75 to 0.75
- gate_bias: bfloat16 [8], replicated, may hold values from -2 to 2
- gate_scale: bfloat16 [12], P('tensor'), may hold values from 0.5 to 2
- rel_table: bfloat16 [320, 12], P(None, 'tensor'), may hold values from -4 to 4
- norm1_gain: bfloat16 [768], replicated, may hold values from 0.099609375 to 1.8984375
- norm1_bias: bfloat16 [768], replicated, may hold values from -2 to 2
- w_inner: bfloat16 [768, 3072], P(None, 'tensor'), may hold values from -0.21875 to 0.21875
- b_inner: bfloat16 [3072], P('tensor'), may hold values from -2 to 2
- w_outer: bfloat16 [3072, 768], P('tensor'), may hold values from -0.15625 to 0.15625
- b_outer: bfloat16 [768], replicated, may hold values from -2 to 2
- norm2_gain: bfloat16 [768], replicated, may hold values from 0.099609375 to 1.8984375
- norm2_bias: bfloat16 [768], replicated, may hold values from -2 to 2
- cotangent: bfloat16 [15872, 768], P('dp'), may hold values from -6 to 6
Outputs:
- output: bfloat16 [15872, 768], P('dp')
- grad_tokens: bfloat16 [15872, 768], P('dp')
- grad_w_query: float32 [768, 768], P(None, 'tensor')
- grad_b_query: float32 [768], P('tensor')
- grad_w_key: float32 [768, 768], P(None, 'tensor')
- grad_w_value: float32 [768, 768], P(None, 'tensor')
- grad_b_value: float32 [768], P('tensor')
- grad_w_out: float32 [768, 768], P('tensor')
- grad_b_out: float32 [768], replicated
- grad_gate_weight: float32 [64, 8], replicated
- grad_gate_bias: float32 [8], replicated
- grad_gate_scale: float32 [12], P('tensor')
- grad_rel_table: float32 [320, 12], P(None, 'tensor')
- grad_norm1_gain: float32 [768], replicated
- grad_norm1_bias: float32 [768], replicated
- grad_w_inner: float32 [768, 3072], P(None, 'tensor')
- grad_b_inner: float32 [3072], P('tensor')
- grad_w_outer: float32 [3072, 768], P('tensor')
- grad_b_outer: float32 [768], replicated
- grad_norm2_gain: float32 [768], replicated
- grad_norm2_bias: float32 [768], replicated
The draws below stay inside these ranges and needn't reach their ends.
Inputs may be any that keep to these rules, and one draw needn't show every extreme that they name: `slot_kind`: 0: the slot holds one clip of 496 patches; 1: it holds two clips of 248 patches, each attending only within itself. `offset_bucket`: entry d + 495 is the bucket of a key d positions after its query.
All inputs are finite; a program needn't handle non-finite values.
Results may differ from the reference program's by a relative error of at most 0.035.
Values may be sent and summed in bfloat16 or wider, within the bound.
A program may use at most 192 MiB of HBM per device.

```python
import math
import jax
import jax.numpy as jnp
from jax import lax

D = 768
HEADS = 12
HEAD = 64
FF = 3072
NB = 320
SEQ = 496
OFFSETS = 991
SLOTS = 32
TOKENS = 15872


def set_ends(entries, rng, low, high):
    longest = entries.shape.index(max(entries.shape))
    spots = []
    for shift in (0, 1):
        where = [jax.random.randint(jax.random.fold_in(rng, axis), (), 0, length) for axis, length in enumerate(entries.shape)]
        where[longest] = (where[longest] + shift) % entries.shape[longest]
        spots.append(tuple(where))
    return entries.at[spots[0]].set(low).at[spots[1]].set(high)


def shard_levels(key, dims, shards, smallest, high):
    level, own = 1.0, jax.random.fold_in(key, 6)
    for dim, blocks in shards:
        steps = jnp.exp(jax.random.uniform(jax.random.fold_in(own, dim), (blocks,), jnp.float32, smallest / len(shards), high / len(shards)))
        level = level * jnp.repeat(steps, dims[dim] // blocks).reshape([-1 if axis == dim else 1 for axis in range(len(dims))])
    return level


def centred(stream_key, dims, spread, limit, cuts=(), kind=jnp.bfloat16):
    level = shard_levels(stream_key, dims, cuts, -0.22, 0.18) if cuts else 1.0
    values = jax.random.normal(stream_key, dims, jnp.float32) * spread * level
    return jnp.minimum(jnp.maximum(values, -limit), limit).astype(kind)


def setup_inputs(seed: int = 0) -> dict:
    key_of = jax.random.split(jax.random.key(seed), 24)
    tokens = centred(key_of[0], (TOKENS, D), 1.0, 6.0, ((0, 8),))
    slot_kind = set_ends(jax.random.randint(key_of[1], (SLOTS,), 0, 2), jax.random.fold_in(key_of[1], 1), 0, 1).astype(jnp.int32)
    offset_bucket = set_ends(jax.random.randint(key_of[2], (OFFSETS,), 0, NB), jax.random.fold_in(key_of[2], 1), 0, NB - 1).astype(jnp.int32)
    w_query = centred(key_of[3], (D, D), D ** -0.5, 0.21875, ((1, 4),))
    b_query = centred(key_of[4], (D,), 0.3, 2.0, ((0, 4),))
    w_key = centred(key_of[5], (D, D), D ** -0.5, 0.21875, ((1, 4),))
    w_value = centred(key_of[6], (D, D), D ** -0.5, 0.21875, ((1, 4),))
    b_value = centred(key_of[7], (D,), 0.3, 2.0, ((0, 4),))
    w_out = centred(key_of[8], (D, D), (D // 32) ** -0.5, 1.25, ((0, 4),))
    b_out = centred(key_of[9], (D,), 0.3, 2.0)
    gate_weight = centred(key_of[10], (HEAD, 8), HEAD ** -0.5, 0.75)
    gate_bias = centred(key_of[11], (8,), 0.5, 2.0)
    gate_scale = jnp.clip(0.5 + 1.5 * jax.random.uniform(key_of[12], (HEADS,), jnp.float32) ** shard_levels(key_of[12], (HEADS,), ((0, 4),), -0.2, 0.2), 0.5, 2.0).astype(jnp.bfloat16)
    rel_table = centred(key_of[13], (NB, HEADS), 0.7, 4.0, ((1, 4),))
    norm1_gain = jnp.clip(1.0 + 0.18 * jax.random.normal(key_of[14], (D,), jnp.float32), 0.099609375, 1.8984375).astype(jnp.bfloat16)
    norm1_bias = centred(key_of[15], (D,), 0.3, 2.0)
    w_inner = centred(key_of[16], (D, FF), D ** -0.5, 0.21875, ((1, 4),))
    b_inner = centred(key_of[17], (FF,), 0.3, 2.0, ((0, 4),))
    w_outer = centred(key_of[18], (FF, D), (FF // 2) ** -0.5, 0.15625, ((0, 4),))
    b_outer = centred(key_of[19], (D,), 0.3, 2.0)
    norm2_gain = jnp.clip(1.0 + 0.18 * jax.random.normal(key_of[20], (D,), jnp.float32), 0.099609375, 1.8984375).astype(jnp.bfloat16)
    norm2_bias = centred(key_of[21], (D,), 0.3, 2.0)
    cotangent = centred(key_of[22], (TOKENS, D), 1.0, 6.0, ((0, 8),))
    return dict(tokens=tokens, slot_kind=slot_kind, offset_bucket=offset_bucket, w_query=w_query, b_query=b_query, w_key=w_key, w_value=w_value, b_value=b_value, w_out=w_out, b_out=b_out, gate_weight=gate_weight, gate_bias=gate_bias, gate_scale=gate_scale, rel_table=rel_table, norm1_gain=norm1_gain, norm1_bias=norm1_bias, w_inner=w_inner, b_inner=b_inner, w_outer=w_outer, b_outer=b_outer, norm2_gain=norm2_gain, norm2_bias=norm2_bias, cotangent=cotangent)


@jax.custom_vjp
def low(v):
    return lax.optimization_barrier(v.astype(jnp.bfloat16)).astype(jnp.float32)

@jax.custom_vjp
def low_back(v):
    return v

def low_keep(v):
    return (low(v), None)

def low_pass(kept, grad):
    return (grad,)

def back_keep(v):
    return (v, None)

def back_low(kept, grad):
    return (low(grad),)
low.defvjp(low_keep, low_pass)
low_back.defvjp(back_keep, back_low)
highest = lax.Precision.HIGHEST
residual_scale = 24.0 ** 0.25
norm_epsilon = 1e-05

def matmul(left, right):
    return jnp.dot(left, right, precision=highest)

def layer_norm(values, gain, shift):
    centered = values - lax.optimization_barrier(jnp.mean(values, -1, keepdims=True))
    inverse = lax.rsqrt(lax.optimization_barrier(jnp.mean(centered * centered, -1, keepdims=True)) + norm_epsilon)
    return centered * inverse * gain + shift

def block(params, inputs, kinds, buckets):
    w_query, b_query, w_key, w_value, b_value, w_out, b_out, gate_weight, gate_bias, gate_scale, rel_table, norm1_gain, norm1_bias, w_inner, b_inner, w_outer, b_outer, norm2_gain, norm2_bias = params
    groups, length, width = inputs.shape
    heads = gate_scale.shape[0]
    head_size = width // heads
    shape_four = (groups, length, heads, head_size)
    flat = inputs.reshape(groups * length, width)
    query_rows = low(low_back((matmul(flat, w_query) + b_query) * (1.0 / math.sqrt(head_size))))
    key_rows = low(low_back(matmul(flat, w_key)))
    value_rows = low(low_back(matmul(flat, w_value) + b_value))
    per_head = inputs.reshape(shape_four)
    gate_logits = jnp.einsum('gihd,de->gihe', per_head, gate_weight, precision=highest) + gate_bias
    first_gate = jax.nn.sigmoid(lax.optimization_barrier(jnp.sum(gate_logits[..., :4], -1)))
    second_gate = jax.nn.sigmoid(lax.optimization_barrier(jnp.sum(gate_logits[..., 4:], -1)))
    gate_value = first_gate * (second_gate * gate_scale - 1.0) + 2.0
    position = lax.iota(jnp.int32, length)
    offset_index = position[None, :] - position[:, None] + (length - 1)
    position_bias = jnp.transpose(rel_table[buckets[offset_index]], (2, 0, 1))
    scores = jnp.einsum('gihd,gjhd->ghij', query_rows.reshape(shape_four), key_rows.reshape(shape_four), precision=highest)
    scores = scores + jnp.transpose(gate_value, (0, 2, 1))[..., None] * position_bias[None]
    half_length = length // 2
    same_half = position[:, None] // half_length == position[None, :] // half_length
    allowed = (kinds[:, None, None] == 0) | same_half[None]
    scores = jnp.where(allowed[:, None], scores, -1e+30)
    weights = low(jax.nn.softmax(low_back(scores), axis=-1))
    mixed = jnp.einsum('ghij,gjhd->gihd', weights, value_rows.reshape(shape_four), precision=highest)
    mixed = low(low_back(mixed.reshape(groups * length, width)))
    attention = low_back(matmul(mixed, w_out) + b_out)
    hidden_one = layer_norm(residual_scale * flat + attention, norm1_gain, norm1_bias)
    inner = low_back(matmul(low(hidden_one), w_inner) + b_inner)
    activated = low(jax.nn.gelu(inner, approximate=False))
    branch = low_back(matmul(activated, w_outer) + b_outer)
    output = layer_norm(residual_scale * hidden_one + branch, norm2_gain, norm2_bias)
    return output.reshape(groups, length, width)

def reference(tokens, slot_kind, offset_bucket, w_query, b_query, w_key, w_value, b_value, w_out, b_out, gate_weight, gate_bias, gate_scale, rel_table, norm1_gain, norm1_bias, w_inner, b_inner, w_outer, b_outer, norm2_gain, norm2_bias, cotangent):
    params = tuple((weight_array.astype(jnp.float32) for weight_array in (w_query, b_query, w_key, w_value, b_value, w_out, b_out, gate_weight, gate_bias, gate_scale, rel_table, norm1_gain, norm1_bias, w_inner, b_inner, w_outer, b_outer, norm2_gain, norm2_bias)))
    slots = slot_kind.shape[0]
    per_group = 1
    for number in range(1, slots + 1):
        if slots % number == 0 and number * SEQ <= 4096:
            per_group = number
    blocks = slots // per_group
    kinds = slot_kind.reshape(blocks, per_group)
    stepper = jax.checkpoint(block)

    def forward(weights, inputs):
        stacked = inputs.reshape(blocks, per_group, SEQ, D)

        def one_group(pair):
            return stepper(weights, pair[0], pair[1], offset_bucket)
        result = lax.map(one_group, (stacked, kinds))
        return result.reshape(blocks * per_group * SEQ, D)
    output, pullback = jax.vjp(forward, params, tokens.astype(jnp.float32))
    grads, grad_tokens = pullback(cotangent.astype(jnp.float32))
    return (output.astype(jnp.bfloat16), grad_tokens.astype(jnp.bfloat16), grads[0], grads[1], grads[2], grads[3], grads[4], grads[5], grads[6], grads[7], grads[8], grads[9], grads[10], grads[11], grads[12], grads[13], grads[14], grads[15], grads[16], grads[17], grads[18])
```

```python
import functools
import math

import jax
import jax.numpy as jnp
from jax import lax
from jax.experimental import pallas as pl
from jax.experimental.pallas import tpu as pltpu
from jax.sharding import PartitionSpec as P

HEAD = 64
SEQ = 496
PAD = 512
D = 768
PAIRS = 6
HEADS = 12
BIAS = 1024
NB = 320
VMEM_LIMIT = 64 * 2**20 - 2**16
HALF = SEQ // 2
f32 = jnp.float32
bf16 = jnp.bfloat16
residual_scale = 24.0**0.25
norm_epsilon = 1e-05
highest = lax.Precision.HIGHEST


def dot(a, b, precision=None):
    return lax.dot_general(a, b, (((1,), (0,)), ((), ())), preferred_element_type=f32, precision=precision)


def dot_t(a, b, precision=None):
    return lax.dot_general(a, b, (((1,), (1,)), ((), ())), preferred_element_type=f32, precision=precision)


def dot_l(a, b):
    return lax.dot_general(a, b, (((0,), (0,)), ((), ())), preferred_element_type=f32)


def fold(x):
    return jnp.sum(x.reshape(x.shape[0] // 8, 8, x.shape[1]), axis=0)


def stats(r):
    c = r - jnp.mean(r, -1, keepdims=True)
    inv = lax.rsqrt(jnp.mean(c * c, -1, keepdims=True) + norm_epsilon)
    return c * inv, inv


def norm_back(g, n, inv):
    return inv * (g - jnp.mean(g, -1, keepdims=True) - n * jnp.mean(g * n, -1, keepdims=True))


def wide(ref, i):
    return ref[i].reshape(D, D)


def rows_loop(step, body, carry):
    def go(c, carry):
        return body(pl.ds(pl.multiple_of(c * step, step), step), carry)
    return lax.fori_loop(0, PAD // step, go, carry)


class K:
    pass


def head_mask(hh):
    lane = lax.broadcasted_iota(jnp.int32, (1, 128), 1)
    return jnp.where((lane // HEAD) == hh, 1.0, 0.0).astype(bf16)


def onehot(k):
    return jnp.where(lax.broadcasted_iota(jnp.int32, (NB, BIAS), 0) == k.bucket[...], 1.0, 0.0)


def own_small(k, z):
    table = dot(k.small[0:16, 0:NB], onehot(k).astype(bf16))
    k.sm[z, 0:3, :] = table[0:3]
    k.sm[z, 3:8, :] = k.small[3:8, :].astype(f32)


def mask_build(k, z):
    kind = k.kinds[z].astype(f32)
    def go(rows, _):
        j = lax.broadcasted_iota(jnp.int32, (32, PAD), 0) + rows.start
        i = lax.broadcasted_iota(jnp.int32, (32, PAD), 1)
        far = jnp.where(j < HALF, 0, 1) != jnp.where(i < HALF, 0, 1)
        k.mask[rows, :] = jnp.where(j < SEQ, 0.0, -1e30) + jnp.where(far, -1e30, 0.0) * kind
        return 0
    rows_loop(32, go, 0)


def gate_weights(k):
    gw = k.small[16:24, :].astype(f32)
    first = jnp.sum(gw[0:4], axis=0, keepdims=True)
    second = jnp.sum(gw[4:8], axis=0, keepdims=True)
    own = (lax.broadcasted_iota(jnp.int32, (16, D), 1) // HEAD) == lax.broadcasted_iota(jnp.int32, (16, D), 0)
    wide_first = jnp.where(own, first[:, 0:D], 0.0)
    wide_second = jnp.where(own, second[:, 0:D], 0.0)
    return jnp.concatenate([wide_first, wide_second], axis=0), first[:, D:], second[:, D:], own


def gates(k):
    weights, first_bias, second_bias, _ = gate_weights(k)
    logits = dot_t(weights, k.tok[...].astype(f32), precision=highest)
    spread = lambda b: jnp.concatenate([b, b], axis=1)
    first = jax.nn.sigmoid(logits[0:16] + spread(first_bias))
    second = jax.nn.sigmoid(logits[16:32] + spread(second_bias))
    k.first[...] = first
    k.second[...] = second
    for h in range(HEADS):
        k.factor[h : h + 1, :] = k.sm[h // 3, 5 + h % 3 : 6 + h % 3, 0:PAD]
    value = first * (second * k.factor[...] - 1.0) + 2.0
    for h in range(HEADS):
        k.gate[h] = value[h : h + 1, :]


def bias_tables(k):
    def go(p, _):
        for i in range(3):
            row = jnp.broadcast_to(k.sm[p, i : i + 1, :], (128, BIAS))
            k.bias[p * 3 + i] = pltpu.roll(row, 0, 1, stride=1, stride_axis=0)[:, 0:896].astype(bf16)
        return 0
    lax.fori_loop(0, 4, go, 0)


def small_row(k, row, start):
    return jnp.concatenate([k.sm[p, row : row + 1, start : start + 192] for p in range(4)], axis=1)


def project(k):
    bq = small_row(k, 3, 0)
    bv = small_row(k, 3, 192)
    for t, dest, bias, scale in ((0, k.q, bq, 0.125), (1, k.k, None, None), (2, k.v, bv, None)):
        r = dot_t(k.tok[...], wide(k.wa, t))
        if bias is not None:
            r = r + bias
        if scale is not None:
            r = r * scale
        r = r.astype(bf16)
        for pr in range(PAIRS):
            dest[pr] = r[:, 128 * pr : 128 * pr + 128]


def attend(k, pr):
    qp, kp, vp = k.q[pr], k.k[pr], k.v[pr]
    total = None
    for hh in range(2):
        h = pr * 2 + hh
        hm = head_mask(hh)
        km = kp * hm
        gate = k.gate[h]
        m8 = jnp.full((8, PAD), -3e38, f32)
        for c in range(4):
            s = dot_t(km[128 * c : 128 * c + 128], qp)
            k.s[128 * c : 128 * c + 128, :] = s
        for c in range(16):
            rows = slice(32 * c, 32 * c + 32)
            lane = 384 - 128 * (c // 4)
            t = k.bias[h, 32 * (c % 4) : 32 * (c % 4) + 32, lane : lane + PAD].astype(f32)
            s = k.s[rows, :] + t * gate + k.mask[rows, :]
            k.s[rows, :] = s
            m8 = jnp.maximum(m8, jnp.max(s.reshape(4, 8, PAD), axis=0))
        m = jnp.max(m8, axis=0, keepdims=True)
        l8 = jnp.zeros((8, PAD), f32)
        for c in range(16):
            rows = slice(32 * c, 32 * c + 32)
            e = jnp.exp(k.s[rows, :] - m)
            k.s[rows, :] = e
            l8 = l8 + fold(e)
        inv = 1.0 / jnp.sum(l8, axis=0, keepdims=True)
        for c in range(16):
            rows = slice(32 * c, 32 * c + 32)
            k.p[h, rows, :] = (k.s[rows, :] * inv).astype(bf16)
        part = dot_l(k.p[h], vp * hm)
        total = part if total is None else total + part
    k.mixed[pr] = total.astype(bf16)


def mixed_all(ref):
    return jnp.concatenate([ref[pr] for pr in range(PAIRS)], axis=1)


def vec(k, row):
    return k.small[row : row + 1, 0:D].astype(f32)


def norm_one(k):
    k.fa[...] = dot(mixed_all(k.mixed), wide(k.wa, 3))
    b_out, gain, shift = vec(k, 8), vec(k, 9), vec(k, 10)
    def go(rows, _):
        r = residual_scale * k.tok[rows, :].astype(f32) + k.fa[rows, :] + b_out
        n, inv = stats(r)
        k.n1[rows, :] = n
        k.inv1[rows, :] = jnp.broadcast_to(inv, (32, 128))
        k.hid[rows, :] = (n * gain + shift).astype(bf16)
        return 0
    rows_loop(32, go, 0)


def feed(k, p):
    k.fa[...] = dot(k.hid[...], wide(k.wi, p))
    b = k.sm[p, 4:5, 0:D]
    def go(rows, _):
        x = k.fa[rows, :] + b
        half = 0.5 * (1.0 + lax.erf(x * (1.0 / math.sqrt(2.0))))
        k.act[p, rows, :] = (x * half).astype(bf16)
        k.dg[p, rows, :] = (half + x * (jnp.exp(-0.5 * x * x) * (1.0 / math.sqrt(2.0 * math.pi)))).astype(bf16)
        return 0
    rows_loop(16, go, 0)
    k.fb[...] += dot(k.act[p], wide(k.wo, p))


def feed_init(k):
    k.fb[...] = jnp.zeros((PAD, D), f32)


def norm_two(k):
    b_outer, gain1, shift1, gain2, shift2 = vec(k, 11), vec(k, 9), vec(k, 10), vec(k, 12), vec(k, 13)
    def go(rows, carry):
        g_gain, g_shift, g_b = carry
        r = residual_scale * (k.n1[rows, :] * gain1 + shift1) + k.fb[rows, :] + b_outer
        n, inv = stats(r)
        k.out[rows, :] = (n * gain2 + shift2).astype(bf16)
        up = k.cot[rows, :].astype(f32)
        g2 = norm_back(up * gain2, n, inv)
        low = g2.astype(bf16)
        k.gb[rows, :] = low
        k.fb[rows, :] = residual_scale * g2
        return g_gain + fold(up * n), g_shift + fold(up), g_b + fold(low.astype(f32))
    zero = jnp.zeros((8, D), f32)
    g_gain, g_shift, g_b = rows_loop(32, go, (zero, zero, zero))
    for row, v in ((3, g_b), (4, g_gain), (5, g_shift)):
        k.sg[row : row + 1, 0:D] = jnp.sum(v, axis=0, keepdims=True)


def feed_back(k, p):
    k.fa[...] = dot_t(k.gb[...], wide(k.wo, p))
    def go(rows, acc):
        gi = (k.fa[rows, :] * k.dg[p, rows, :].astype(f32)).astype(bf16)
        k.dg[p, rows, :] = gi
        return acc + fold(gi.astype(f32))
    acc = rows_loop(32, go, jnp.zeros((8, D), f32))
    k.sg[pl.ds(6 + p, 1), 0:D] = jnp.sum(acc, axis=0, keepdims=True)
    k.fb[...] += dot_t(k.dg[p], wide(k.wi, p))
    k.wo[p] = dot_l(k.act[p], k.gb[...]).astype(bf16).reshape(8, 96, D)
    k.wi[p] = dot_l(k.hid[...], k.dg[p]).astype(bf16).reshape(8, 96, D)


def norm_one_back(k):
    gain = vec(k, 9)
    def go(rows, carry):
        g_gain, g_shift, g_b = carry
        gh = k.fb[rows, :]
        n = k.n1[rows, :]
        g1 = norm_back(gh * gain, n, k.inv1[rows, 0:1])
        low = g1.astype(bf16)
        k.gb[rows, :] = low
        k.fb[rows, :] = residual_scale * g1
        return g_gain + fold(gh * n), g_shift + fold(gh), g_b + fold(low.astype(f32))
    zero = jnp.zeros((8, D), f32)
    g_gain, g_shift, g_b = rows_loop(32, go, (zero, zero, zero))
    for row, v in ((0, g_b), (1, g_gain), (2, g_shift)):
        k.sg[row : row + 1, 0:D] = jnp.sum(v, axis=0, keepdims=True)
    gm = dot_t(k.gb[...], wide(k.wa, 3)).astype(bf16)
    for pr in range(PAIRS):
        k.gm[pr] = gm[:, 128 * pr : 128 * pr + 128]


def attend_back(k, pr):
    qp, kp, vp, gm = k.q[pr], k.k[pr], k.v[pr], k.gm[pr]
    tq = tk = tv = None
    for hh in range(2):
        h = pr * 2 + hh
        hm = head_mask(hh)
        vm = vp * hm
        gate = k.gate[h]
        for c in range(4):
            k.s[128 * c : 128 * c + 128, :] = dot_t(vm[128 * c : 128 * c + 128], gm)
        d8 = jnp.zeros((8, PAD), f32)
        for c in range(16):
            rows = slice(32 * c, 32 * c + 32)
            d8 = d8 + fold(k.s[rows, :] * k.p[h, rows, :].astype(f32))
        total = jnp.sum(d8, axis=0, keepdims=True)
        gg = jnp.zeros((8, PAD), f32)
        k.a[...] = jnp.zeros((128, BIAS), f32)
        for c in range(16):
            rows = slice(32 * c, 32 * c + 32)
            part = slice(32 * (c % 4), 32 * (c % 4) + 32)
            lane = 384 - 128 * (c // 4)
            low = (k.p[h, rows, :].astype(f32) * (k.s[rows, :] - total)).astype(bf16)
            k.gs[rows, :] = low
            g = low.astype(f32)
            gg = gg + fold(g * k.bias[h, part, lane : lane + PAD].astype(f32))
            k.a[part, lane : lane + PAD] += g * gate
        k.ggate[h] = jnp.sum(gg, axis=0, keepdims=True)
        acc = k.a[0:8, :]
        for c in range(1, 16):
            acc = acc + pltpu.roll(k.a[8 * c : 8 * c + 8, :], BIAS - 8 * c, 1)
        flat = acc[0:1]
        for b in range(1, 8):
            flat = flat + pltpu.roll(acc, BIAS - b, 1)[b : b + 1]
        k.goff[h] = flat
        gs = k.gs[...]
        pv = dot(k.p[h], gm * hm)
        pq = dot_l(gs, kp * hm)
        pk = dot(gs, qp * hm)
        tv, tq, tk = (pv, pq, pk) if tv is None else (tv + pv, tq + pq, tk + pk)
    k.q[pr] = (tq.astype(bf16) * 0.125).astype(bf16)
    k.k[pr] = tk.astype(bf16)
    k.v[pr] = tv.astype(bf16)


def gate_back(k):
    weights, _, _, own = gate_weights(k)
    ggate = jnp.concatenate([k.ggate[h] for h in range(HEADS)] + [jnp.zeros((4, PAD), f32)], axis=0)
    first, second, factor = k.first[...], k.second[...], k.factor[...]
    df = ggate * (second * factor - 1.0) * first * (1.0 - first)
    ds = ggate * first * factor * second * (1.0 - second)
    dz = jnp.concatenate([df, ds], axis=0)
    gscale = jnp.sum(ggate * first * second, axis=1, keepdims=True)
    gw = dot(dz, k.tok[...].astype(f32), precision=highest)
    pick = lambda v: jnp.sum(jnp.where(own, v, 0.0), axis=0, keepdims=True)
    k.sg[24:25, 0:D] = pick(gw[0:16])
    k.sg[25:26, 0:D] = pick(gw[16:32])
    k.sg[24:25, D:] = jnp.broadcast_to(jnp.sum(jnp.sum(df, axis=0, keepdims=True), axis=1, keepdims=True), (1, 256))
    k.sg[25:26, D:] = jnp.broadcast_to(jnp.sum(jnp.sum(ds, axis=0, keepdims=True), axis=1, keepdims=True), (1, 256))
    goff = jnp.concatenate([k.goff[h] for h in range(HEADS)] + [jnp.zeros((4, BIAS), f32)], axis=0)
    rel = dot_t(goff, onehot(k), precision=highest)
    k.sg[12:24, 0:NB] = rel[0:HEADS]
    k.sg[12:24, 512:640] = jnp.broadcast_to(gscale, (16, 128))[0:HEADS]
    return dot(dz.T, weights)


def grad_input(k):
    k.fa[...] = gate_back(k)
    for t, src in ((0, k.q), (1, k.k), (2, k.v)):
        k.fa[...] += dot(mixed_all(src), wide(k.wa, t))
    def go(rows, _):
        k.gtok[rows, :] = (k.fb[rows, :] + k.fa[rows, :]).astype(bf16)
        return 0
    rows_loop(32, go, 0)


def grad_projections(k):
    for t, src in ((0, k.q), (1, k.k), (2, k.v)):
        g = mixed_all(src)
        if t != 1:
            row = jnp.sum(fold(g.astype(f32)), axis=0, keepdims=True)
            k.sg[10 + t // 2 : 11 + t // 2, 0:D] = row
        k.wa[t] = dot_l(g, k.tok[...]).astype(bf16).reshape(4, 2, 96, D)
    k.wa[3] = dot_l(mixed_all(k.mixed), k.gb[...]).astype(bf16).reshape(4, 2, 96, D)


def each(n, fn, k):
    def go(i, _):
        fn(k, i)
        return 0
    lax.fori_loop(0, n, go, 0)


COMPUTE_SCRATCH = dict(
    tok=((PAD, D), bf16), cot=((PAD, D), bf16), sm=((4, 8, BIAS), f32), mask=((PAD, PAD), f32),
    first=((16, PAD), f32), second=((16, PAD), f32), factor=((16, PAD), f32), gate=((HEADS, 1, PAD), f32),
    bias=((HEADS, 128, 896), bf16), q=((PAIRS, PAD, 128), bf16), k=((PAIRS, PAD, 128), bf16),
    v=((PAIRS, PAD, 128), bf16), s=((PAD, PAD), f32), p=((HEADS, PAD, PAD), bf16), mixed=((PAIRS, PAD, 128), bf16),
    fa=((PAD, D), f32), fb=((PAD, D), f32), n1=((PAD, D), f32), inv1=((PAD, 128), f32), hid=((PAD, D), bf16),
    act=((4, PAD, D), bf16), dg=((4, PAD, D), bf16), out=((PAD, D), bf16), gb=((PAD, D), bf16),
    gm=((PAIRS, PAD, 128), bf16), gs=((PAD, PAD), bf16), a=((128, BIAS), f32), ggate=((HEADS, 1, PAD), f32),
    goff=((HEADS, 1, BIAS), f32), gtok=((PAD, D), bf16), sg=((32, BIAS), f32),
    wa=((4, 4, 2, 96, D), bf16), wi=((4, 8, 96, D), bf16), wo=((4, 8, 96, D), bf16),
)


MESH = pl.DeviceIdType.MESH
BLOCKS = (0, 1, 2)
SEMS = dict(
    wz=(3, 3), w1=(3, 3), w2=(3, 3, 2), w3=(3, 3), sm=(3,), ot=(3,), gt=(3,), r1=(3,), r2=(3, 2), r3=(3,),
    r4=(3, 3), a1=(3,), a2=(3, 2), a3=(3,), sg=(5,),
)
COMM_SCRATCH = dict(
    stage=((3, D, 192), bf16), rb1a=((2, 4, 2, 96, D), bf16), rb1i=((4, 4, 96, D), bf16), rb1o=((4, 4, 96, D), bf16),
    rb2=((3, 2, 4, 96, D), bf16), rb3=((3, 4, 96, D), bf16), rb4=((3, 3, 96, D), bf16), sgr=((5, 32, BIAS), f32),
)


class Net:
    def __init__(self, k):
        self.k = k
        dp, z = lax.axis_index("dp"), lax.axis_index("tensor")
        self.dp, self.z = dp, z
        c, x, y = dp % 2, (dp // 2) % 2, (dp // 4) % 2
        self.c = c
        across_x, across_y = dp + 2 * (1 - 2 * x), dp + 4 * (1 - 2 * y)
        self.core = (dp + 1 - 2 * c, z)
        self.x, self.y = (across_x, z), (across_y, z)
        self.one = ((1 - c) * across_x + c * across_y, z)
        self.two = (c * across_x + (1 - c) * across_y, z)
        at = lambda cc, yy, xx: 4 * cc + 2 * yy + xx
        ex, ey = at(c, y, 1 - x), at(c, 1 - y, x)
        self.e = at(c, y, x)
        self.e1 = (1 - c) * ex + c * ey
        self.e2 = c * ex + (1 - c) * ey
        self.e12 = at(c, 1 - y, 1 - x)

    def ahead(self, dz):
        return (self.z + dz) % 4

    def behind(self, dz):
        return (self.z + 4 - dz) % 4

    def copy(self, name, index, src, dst, device):
        sems = getattr(self.k, "sem_" + name)
        return pltpu.make_async_remote_copy(
            src_ref=src, dst_ref=dst, send_sem=sems.at[(0, *index)], recv_sem=sems.at[(1, *index)],
            device_id=device, device_id_type=MESH,
        )

    def greet(self):
        barrier = pltpu.get_barrier_semaphore()
        peers = [self.core, self.one, self.two] + [(self.dp, self.ahead(dz)) for dz in (1, 2, 3)]
        for peer in peers:
            pl.semaphore_signal(barrier, inc=1, device_id=peer, device_id_type=MESH)
        pl.semaphore_wait(barrier, len(peers))

    def block(self, b):
        return (self.k.wa, self.k.wi, self.k.wo)[b]

    def chunk(self, b, p, e):
        return self.block(b).at[e // 2, p, e % 2] if b == 0 else self.block(b).at[p, e]

    def chunk_all(self, b, e):
        return self.block(b).at[e // 2, :, e % 2] if b == 0 else self.block(b).at[:, e]

    def side(self, b, p, c):
        return self.block(b).at[pl.ds(2 * c, 2), p] if b == 0 else self.block(b).at[p, pl.ds(4 * c, 4)]

    def side_all(self, b, c):
        return self.block(b).at[pl.ds(2 * c, 2)] if b == 0 else self.block(b).at[:, pl.ds(4 * c, 4)]

    def wz(self, b, d):
        ref = self.chunk(b, self.z, self.e)
        return self.copy("wz", (b, d - 1), ref, ref, (self.dp, self.ahead(d)))

    def w1(self, b, d):
        ref = self.chunk(b, self.behind(d), self.e)
        return self.copy("w1", (b, d - 1), ref, ref, self.one)

    def w2(self, b, d, i):
        ref = self.chunk(b, self.behind(d), (self.e, self.e1)[i])
        return self.copy("w2", (b, d - 1, i), ref, ref, self.two)

    def w3(self, b, d):
        ref = self.side(b, self.behind(d), self.c)
        return self.copy("w3", (b, d - 1), ref, ref, self.core)

    def sm(self, d):
        ref = self.k.sm.at[self.z]
        return self.copy("sm", (d - 1,), ref, ref, (self.dp, self.ahead(d)))

    def rows(self, name, d):
        src, dst = (self.k.out, self.k.out_hbm) if name == "ot" else (self.k.gtok, self.k.gtok_hbm)
        at = pl.ds(pl.multiple_of(self.z * SEQ, 16), SEQ)
        return self.copy(name, (d - 1,), src.at[pl.ds(0, SEQ)], dst.at[at], (self.dp, self.ahead(d)))

    def r1(self, b):
        dst = (self.k.rb1a, self.k.rb1i, self.k.rb1o)[b]
        return self.copy("r1", (b,), self.side_all(b, 1 - self.c), dst, self.core)

    def r2(self, b, i):
        return self.copy("r2", (b, i), self.chunk_all(b, (self.e1, self.e12)[i]), self.k.rb2.at[b, i], self.one)

    def r3(self, b):
        return self.copy("r3", (b,), self.chunk_all(b, self.e2), self.k.rb3.at[b], self.two)

    def r4(self, b, d):
        to = self.ahead(d)
        return self.copy("r4", (b, d - 1), self.chunk(b, to, self.e), self.k.rb4.at[b, d - 1], (self.dp, to))

    def result(self, b, e):
        return (self.k.ra, self.k.ri, self.k.ro)[b].at[e]

    def keep(self, b):
        return pltpu.make_async_copy(self.chunk(b, self.z, self.e), self.result(b, self.e), self.k.sem_keep.at[b])

    def a1(self, b):
        return self.copy("a1", (b,), self.chunk(b, self.z, self.e), self.result(b, self.e), self.one)

    def a2(self, b, i):
        src = (self.chunk(b, self.z, self.e), self.result(b, self.e1))[i]
        return self.copy("a2", (b, i), src, self.result(b, (self.e, self.e1)[i]), self.two)

    def a3(self, b):
        ref = self.result(b, pl.ds(4 * self.c, 4))
        return self.copy("a3", (b,), ref, ref, self.core)

    def sg(self, i):
        device = (self.core, self.x, self.y, (self.dp, self.flip(1)), (self.dp, self.flip(2)))[i]
        return self.copy("sg", (i,), self.k.sg if i == 0 else self.k.sgs.at[i - 1], self.k.sgr.at[i], device)

    def flip(self, bit):
        return self.z + bit * (1 - 2 * ((self.z // bit) % 2))


def loop(n, fn):
    def go(i, _):
        fn(i)
        return 0
    lax.fori_loop(0, n, go, 0)


def weight_stage(net, b, stage):
    for d in (1, 3, 2):
        if stage == 1:
            net.wz(b, d).wait_recv()
            net.w1(b, d).start()
        elif stage == 2:
            net.w1(b, d).wait_recv()
            net.w2(b, d, 0).start()
            net.w2(b, d, 1).start()
        elif stage == 3:
            net.w2(b, d, 0).wait_recv()
            net.w2(b, d, 1).wait_recv()
            net.w3(b, d).start()
        else:
            net.w3(b, d).wait_recv()


def weights_sent(net):
    for b in BLOCKS:
        for d in (1, 2, 3):
            net.wz(b, d).wait_send()
            net.w1(b, d).wait_send()
            net.w2(b, d, 0).wait_send()
            net.w2(b, d, 1).wait_send()
            net.w3(b, d).wait_send()


def add_all(net, b, e, ref):
    def go(p):
        if b == 0:
            net.k.wa[e // 2, p, e % 2] = net.k.wa[e // 2, p, e % 2] + ref[p]
        else:
            net.block(b)[p, e] = net.block(b)[p, e] + ref[p]
    loop(4, go)


def reduce_stage(net, b, stage):
    k, c = net.k, net.c
    if stage == 0:
        net.r1(b).start()
    elif stage == 1:
        net.r1(b).wait_recv()
        def go(i):
            if b == 0:
                t, p = i // 4, i % 4
                for half in range(2):
                    k.wa[2 * c + t, p, half] = k.wa[2 * c + t, p, half] + k.rb1a[t, p, half]
            else:
                ref, src = net.block(b), (k.rb1i, k.rb1o)[b - 1]
                p, j = i // 2, 2 * (i % 2)
                for h in range(2):
                    ref[p, 4 * c + j + h] = ref[p, 4 * c + j + h] + src[p, j + h]
        loop(8, go)
        net.r2(b, 0).start()
        net.r2(b, 1).start()
    elif stage == 2:
        net.r2(b, 1).wait_recv()
        add_all(net, b, net.e2, k.rb2.at[b, 1])
        net.r3(b).start()
        net.r2(b, 0).wait_recv()
        add_all(net, b, net.e, k.rb2.at[b, 0])
    elif stage == 3:
        net.r3(b).wait_recv()
        add_all(net, b, net.e, k.rb3.at[b])
        for d in (1, 3, 2):
            net.r4(b, d).start()
    elif stage == 4:
        for d in (1, 3, 2):
            net.r4(b, d).wait_recv()
        if b == 0:
            own = k.wa[net.e // 2, net.z, net.e % 2]
        else:
            own = net.block(b)[net.z, net.e]
        total = (own.astype(f32) + k.rb4[b, 0].astype(f32)) + (k.rb4[b, 1].astype(f32) + k.rb4[b, 2].astype(f32))
        if b == 0:
            k.wa[net.e // 2, net.z, net.e % 2] = total.astype(bf16)
        else:
            net.block(b)[net.z, net.e] = total.astype(bf16)
        net.keep(b).start()
        net.a1(b).start()
        net.a2(b, 0).start()
    elif stage == 5:
        net.a1(b).wait_recv()
        net.a2(b, 1).start()
    elif stage == 6:
        net.keep(b).wait()
        net.a2(b, 0).wait_recv()
        net.a2(b, 1).wait_recv()
        net.a3(b).start()
    else:
        net.a3(b).wait_recv()
        net.r1(b).wait_send()
        for i in (0, 1):
            net.r2(b, i).wait_send()
            net.a2(b, i).wait_send()
        net.r3(b).wait_send()
        for d in (1, 2, 3):
            net.r4(b, d).wait_send()
        net.a1(b).wait_send()
        net.a3(b).wait_send()


def small_stage(net, i):
    k = net.k
    if i > 0:
        net.sg(i - 1).wait_recv()
        mine = k.sg[...] if i == 1 else k.sgs[i - 2]
        k.sgs[i - 1] = mine + k.sgr[i - 1]
    if i < 5:
        net.sg(i).start()


def kernel(names, *refs):
    k = K()
    for name, ref in zip(names, refs):
        setattr(k, name, ref)
    net = Net(k)
    z = net.z
    own_rows = pl.ds(pl.multiple_of(z * SEQ, 16), SEQ)
    local = [
        pltpu.make_async_copy(k.wq_hbm, k.stage.at[0], k.sem_in.at[0]),
        pltpu.make_async_copy(k.wk_hbm, k.stage.at[1], k.sem_in.at[1]),
        pltpu.make_async_copy(k.wv_hbm, k.stage.at[2], k.sem_in.at[2]),
        pltpu.make_async_copy(k.wout_hbm, k.wa.at[3, z], k.sem_in.at[3]),
        pltpu.make_async_copy(k.wi_hbm, k.wi.at[z], k.sem_in.at[4]),
        pltpu.make_async_copy(k.wo_hbm, k.wo.at[z], k.sem_in.at[5]),
        pltpu.make_async_copy(k.tok_hbm.at[own_rows], k.tok.at[pl.ds(0, SEQ)], k.sem_in.at[6]),
        pltpu.make_async_copy(k.cot_hbm.at[own_rows], k.cot.at[pl.ds(0, SEQ)], k.sem_in.at[7]),
    ]
    for c in local:
        c.start()
    k.tok[SEQ:PAD] = jnp.zeros((PAD - SEQ, D), bf16)
    k.cot[SEQ:PAD] = jnp.zeros((PAD - SEQ, D), bf16)
    k.sg[...] = jnp.zeros((32, BIAS), f32)
    k.factor[...] = jnp.zeros((16, PAD), f32)
    own_small(k, z)
    for t in range(3):
        local[t].wait()
        k.wa[t, z] = k.stage[t].T.reshape(2, 96, D)
    net.greet()
    for d in (1, 3, 2):
        net.sm(d).start()
    local[3].wait()
    for d in (1, 3, 2):
        net.wz(0, d).start()
    local[4].wait()
    local[5].wait()
    for b in (1, 2):
        for d in (1, 3, 2):
            net.wz(b, d).start()
    local[6].wait()
    local[7].wait()
    mask_build(k, z)
    weight_stage(net, 0, 1)
    for d in (1, 2, 3):
        net.sm(d).wait_recv()
    gates(k)
    weight_stage(net, 0, 2)
    bias_tables(k)
    weight_stage(net, 1, 1)
    weight_stage(net, 0, 3)
    weight_stage(net, 1, 2)
    weight_stage(net, 2, 1)
    weight_stage(net, 0, 4)
    project(k)

    def forward(pr):
        attend(k, pr)
        @pl.when(pr == 0)
        def _():
            weight_stage(net, 1, 3)
            weight_stage(net, 2, 2)
        @pl.when(pr == 3)
        def _():
            weight_stage(net, 2, 3)
    loop(PAIRS, forward)
    norm_one(k)
    weight_stage(net, 1, 4)
    weight_stage(net, 2, 4)
    feed_init(k)
    loop(4, lambda p: feed(k, p))
    norm_two(k)
    here = [
        pltpu.make_async_copy(k.out.at[pl.ds(0, SEQ)], k.out_hbm.at[own_rows], k.sem_in.at[0]),
        pltpu.make_async_copy(k.gtok.at[pl.ds(0, SEQ)], k.gtok_hbm.at[own_rows], k.sem_in.at[1]),
    ]
    here[0].start()
    for d in (1, 3, 2):
        net.rows("ot", d).start()
    weights_sent(net)
    loop(4, lambda p: feed_back(k, p))
    reduce_stage(net, 2, 0)
    reduce_stage(net, 1, 0)
    norm_one_back(k)
    reduce_stage(net, 2, 1)
    reduce_stage(net, 1, 1)

    def backward(pr):
        attend_back(k, pr)
        for step, stage in ((1, 2), (3, 3), (4, 4), (5, 5)):
            @pl.when(pr == step)
            def _():
                reduce_stage(net, 2, stage)
                reduce_stage(net, 1, stage)
    loop(PAIRS, backward)
    grad_input(k)
    here[1].start()
    for d in (1, 3, 2):
        net.rows("gt", d).start()
    grad_projections(k)
    reduce_stage(net, 0, 0)
    small_stage(net, 0)
    reduce_stage(net, 2, 6)
    reduce_stage(net, 1, 6)
    reduce_stage(net, 0, 1)
    small_stage(net, 1)
    reduce_stage(net, 0, 2)
    small_stage(net, 2)
    reduce_stage(net, 0, 3)
    small_stage(net, 3)
    reduce_stage(net, 0, 4)
    small_stage(net, 4)
    reduce_stage(net, 0, 5)
    small_stage(net, 5)
    reduce_stage(net, 0, 6)
    finish = pltpu.make_async_copy(k.sgs.at[4], k.sg_hbm, k.sem_in.at[2])
    finish.start()
    for b in (2, 1, 0):
        reduce_stage(net, b, 7)
    for i in range(5):
        net.sg(i).wait_send()
    for d in (1, 2, 3):
        net.sm(d).wait_send()
        for name in ("ot", "gt"):
            net.rows(name, d).wait_send()
            net.rows(name, d).wait_recv()
    here[0].wait()
    here[1].wait()
    finish.wait()


def pack(offset_bucket, b_query, b_value, gate_scale, rel_table, b_inner, shared, gate_weight, gate_bias):
    def row(v):
        return jnp.pad(v, (0, BIAS - v.shape[0]))
    rows = [row(rel_table[:, i]) for i in range(3)]
    rows += [row(jnp.concatenate([b_query, b_value])), row(b_inner)]
    rows += [jnp.broadcast_to(gate_scale[i], (BIAS,)) for i in range(3)]
    rows += [row(v) for v in shared] + [jnp.zeros(BIAS, bf16)] * 2
    gw = jnp.concatenate([jnp.tile(gate_weight.T, (1, HEADS)), jnp.broadcast_to(gate_bias[:, None], (8, BIAS - D))], 1)
    small = jnp.concatenate([jnp.stack(rows), gw])
    rev = offset_bucket[::-1]
    bucket = jnp.concatenate([rev[111:991], jnp.full((33,), -1, jnp.int32), rev[0:111]])[None]
    return small, bucket


def body(
    tokens, slot_kind, offset_bucket, w_query, b_query, w_key, w_value, b_value, w_out, b_out, gate_weight, gate_bias,
    gate_scale, rel_table, norm1_gain, norm1_bias, w_inner, b_inner, w_outer, b_outer, norm2_gain, norm2_bias, cotangent,
):
    shared = (b_out, norm1_gain, norm1_bias, b_outer, norm2_gain, norm2_bias)
    small, bucket = pack(offset_bucket, b_query, b_value, gate_scale, rel_table, b_inner, shared, gate_weight, gate_bias)
    z = lax.axis_index("tensor")
    n_dp = lax.axis_size("dp")
    rows = tokens.shape[0]
    shape = jax.ShapeDtypeStruct
    names = ["kinds", "bucket", "small", "tok_hbm", "cot_hbm", "wq_hbm", "wk_hbm", "wv_hbm", "wout_hbm", "wi_hbm", "wo_hbm"]
    names += ["out_hbm", "gtok_hbm", "ra", "ri", "ro", "sg_hbm"]
    scratch = []
    for name, (dims, dtype) in (COMPUTE_SCRATCH | COMM_SCRATCH).items():
        names.append(name)
        scratch.append(pltpu.VMEM(dims, dtype))
    names.append("sgs")
    scratch.append(pltpu.VMEM((5, 32, BIAS), f32))
    for name, dims in SEMS.items():
        names.append("sem_" + name)
        scratch.append(pltpu.SemaphoreType.DMA((2, *dims)))
    for name, count in (("sem_in", 8), ("sem_keep", 3)):
        names.append(name)
        scratch.append(pltpu.SemaphoreType.DMA((count,)))
    anywhere = pl.BlockSpec(memory_space=pl.ANY)
    vmem = pl.BlockSpec(memory_space=pltpu.VMEM)
    smem = pl.BlockSpec(memory_space=pltpu.SMEM)
    out, gtok, ra, ri, ro, sg = pl.pallas_call(
        functools.partial(kernel, names),
        in_specs=[smem, vmem, vmem] + [anywhere] * 8,
        out_specs=[anywhere] * 6,
        out_shape=[
            shape((rows, D), bf16), shape((rows, D), bf16), shape((8, 96, D), bf16), shape((8, 96, D), bf16),
            shape((8, 96, D), bf16), shape((32, BIAS), f32),
        ],
        scratch_shapes=scratch,
        compiler_params=pltpu.CompilerParams(collective_id=0, has_side_effects=True, vmem_limit_bytes=VMEM_LIMIT),
    )(
        slot_kind, bucket, small, tokens, cotangent, w_query, w_key, w_value, w_out.reshape(2, 96, D),
        w_inner.reshape(8, 96, D), w_outer.reshape(8, 96, D),
    )
    if n_dp > 8:
        groups = [list(range(g, n_dp, 8)) for g in range(8)]
        ra, ri, ro, sg = lax.psum((ra.astype(f32), ri.astype(f32), ro.astype(f32), sg), "dp", axis_index_groups=groups)
    ra = ra.reshape(4, 192, D).astype(f32)
    pick = lambda v, size: lax.dynamic_slice_in_dim(v, z * size, size, 0)
    return (
        out,
        gtok,
        ra[0].T,
        pick(sg[10], 192),
        ra[1].T,
        ra[2].T,
        pick(sg[11], 192),
        ra[3],
        sg[0, :D],
        jnp.concatenate([jnp.broadcast_to(jnp.sum(sg[24 + i, :D].reshape(HEADS, HEAD), 0)[:, None], (HEAD, 4)) for i in (0, 1)], 1),
        jnp.concatenate([jnp.broadcast_to(sg[24 + i, D], (4,)) for i in (0, 1)]),
        pick(sg[12:24, 512], 3),
        pick(sg[12:24, :NB], 3).T,
        sg[1, :D],
        sg[2, :D],
        ri.reshape(D, D).astype(f32),
        lax.dynamic_index_in_dim(sg[6:10, :D], z, 0, False),
        ro.reshape(D, D).astype(f32),
        sg[3, :D],
        sg[4, :D],
        sg[5, :D],
    )


def solution(mesh):
    in_specs = (
        P("dp", None),
        P("dp"),
        P(),
        P(None, "tensor"),
        P("tensor"),
        P(None, "tensor"),
        P(None, "tensor"),
        P("tensor"),
        P("tensor", None),
        P(),
        P(),
        P(),
        P("tensor"),
        P(None, "tensor"),
        P(),
        P(),
        P(None, "tensor"),
        P("tensor"),
        P("tensor", None),
        P(),
        P(),
        P(),
        P("dp", None),
    )
    out_specs = (
        P("dp", None),
        P("dp", None),
        P(None, "tensor"),
        P("tensor"),
        P(None, "tensor"),
        P(None, "tensor"),
        P("tensor"),
        P("tensor", None),
        P(),
        P(),
        P(),
        P("tensor"),
        P(None, "tensor"),
        P(),
        P(),
        P(None, "tensor"),
        P("tensor"),
        P("tensor", None),
        P(),
        P(),
        P(),
    )
    return jax.shard_map(body, mesh=mesh, in_specs=in_specs, out_specs=out_specs, check_vma=False)
```

```python
import functools
import math

import jax
import jax.numpy as jnp
from jax import lax
from jax.experimental import pallas as pl
from jax.experimental.pallas import tpu as pltpu
from jax.sharding import PartitionSpec as P

HEAD = 64
SEQ = 496
PAD = 512
D = 768
PAIRS = 6
HEADS = 12
BIAS = 1024
NB = 320
VMEM_LIMIT = 64 * 2**20 - 2**16
OFFSETS = 991
HALF = SEQ // 2
f32 = jnp.float32
bf16 = jnp.bfloat16
residual_scale = 24.0**0.25
norm_epsilon = 1e-05
highest = lax.Precision.HIGHEST


def dot(a, b, precision=None):
    return lax.dot_general(a, b, (((1,), (0,)), ((), ())), preferred_element_type=f32, precision=precision)


def dot_t(a, b, precision=None):
    return lax.dot_general(a, b, (((1,), (1,)), ((), ())), preferred_element_type=f32, precision=precision)


def dot_l(a, b):
    return lax.dot_general(a, b, (((0,), (0,)), ((), ())), preferred_element_type=f32)


def fold(x):
    return jnp.sum(x.reshape(x.shape[0] // 8, 8, x.shape[1]), axis=0)


def stats(r):
    c = r - jnp.mean(r, -1, keepdims=True)
    inv = lax.rsqrt(jnp.mean(c * c, -1, keepdims=True) + norm_epsilon)
    return c * inv, inv


def norm_back(g, n, inv):
    return inv * (g - jnp.mean(g, -1, keepdims=True) - n * jnp.mean(g * n, -1, keepdims=True))


def wide(ref, i):
    return ref[i].reshape(D, D)


def rows_loop(step, body, carry):
    def go(c, carry):
        return body(pl.ds(pl.multiple_of(c * step, step), step), carry)
    return lax.fori_loop(0, PAD // step, go, carry)


class K:
    pass


def head_mask(hh):
    lane = lax.broadcasted_iota(jnp.int32, (1, 128), 1)
    return jnp.where((lane // HEAD) == hh, 1.0, 0.0).astype(bf16)


def line(ref):
    return ref[...].astype(f32).reshape(1, ref.shape[0])


def one_hot(k):
    k.row[...] = jnp.full((1, BIAS), -1, jnp.int32)
    k.row[:, 0:OFFSETS] = k.bucket[...]
    hot = jnp.where(lax.broadcasted_iota(jnp.int32, (NB, BIAS), 0) == k.row[...], 1.0, 0.0).astype(bf16)
    for n in range(4):
        m = lax.broadcasted_iota(jnp.int32, (BIAS, 256), 0) + lax.broadcasted_iota(jnp.int32, (BIAS, 256), 1) + 256 * n
        turn = jnp.where((m == 879) | (m == 1903), 1.0, 0.0).astype(bf16)
        k.hot[:, 256 * n : 256 * n + 256] = dot(hot, turn).astype(bf16)


def own_small(k, z):
    one_hot(k)
    k.sm[z, 0:3, :] = dot(k.rel[...], k.hot[...])
    k.sm[z, 3:4, 0:192] = line(k.b_query)
    k.sm[z, 3:4, 192:384] = line(k.b_value)
    k.sm[z, 4:5, 0:D] = line(k.b_inner)
    for i in range(3):
        k.sm[z, 5 + i : 6 + i, :] = jnp.broadcast_to(k.scale[:, i : i + 1].astype(f32), (1, BIAS))


def mask_build(k, z):
    kind = k.kinds[z].astype(f32)
    def go(rows, _):
        j = lax.broadcasted_iota(jnp.int32, (32, PAD), 0) + rows.start
        i = lax.broadcasted_iota(jnp.int32, (32, PAD), 1)
        far = jnp.where(j < HALF, 0, 1) != jnp.where(i < HALF, 0, 1)
        k.mask[rows, :] = jnp.where(j < SEQ, 0.0, -1e30) + jnp.where(far, -1e30, 0.0) * kind
        return 0
    rows_loop(32, go, 0)


def gate_weights(k):
    gw = k.gw[...].astype(f32)
    tile = lambda v: jnp.concatenate([jnp.concatenate([v, v], axis=1)] * PAIRS, axis=1)
    first = tile(jnp.sum(gw[0:4], axis=0, keepdims=True))
    second = tile(jnp.sum(gw[4:8], axis=0, keepdims=True))
    bias = line(k.gate_bias)
    own = (lax.broadcasted_iota(jnp.int32, (16, D), 1) // HEAD) == lax.broadcasted_iota(jnp.int32, (16, D), 0)
    both = jnp.concatenate([jnp.where(own, first, 0.0), jnp.where(own, second, 0.0)], axis=0)
    add = lambda v: jnp.sum(v, axis=1, keepdims=True)
    return both, add(bias[:, 0:4]), add(bias[:, 4:8]), own


def gates(k):
    weights, first_bias, second_bias, _ = gate_weights(k)
    logits = dot_t(weights, k.tok[...].astype(f32), precision=highest)
    first = jax.nn.sigmoid(logits[0:16] + first_bias)
    second = jax.nn.sigmoid(logits[16:32] + second_bias)
    k.first[...] = first
    k.second[...] = second
    for h in range(HEADS):
        k.factor[h : h + 1, :] = k.sm[h // 3, 5 + h % 3 : 6 + h % 3, 0:PAD]
    value = first * (second * k.factor[...] - 1.0) + 2.0
    for h in range(HEADS):
        k.gate[h] = value[h : h + 1, :]


def bias_tables(k):
    def go(p, _):
        for i in range(3):
            row = jnp.broadcast_to(k.sm[p, i : i + 1, :], (128, BIAS))
            k.bias[p * 3 + i] = pltpu.roll(row, 0, 1, stride=1, stride_axis=0)[:, 0:896].astype(bf16)
        return 0
    lax.fori_loop(0, 4, go, 0)


def small_row(k, row, start):
    return jnp.concatenate([k.sm[p, row : row + 1, start : start + 192] for p in range(4)], axis=1)


def project(k):
    bq = small_row(k, 3, 0)
    bv = small_row(k, 3, 192)
    for t, dest, bias, scale in ((0, k.q, bq, 0.125), (1, k.k, None, None), (2, k.v, bv, None)):
        r = dot_t(k.tok[...], wide(k.wa, t))
        if bias is not None:
            r = r + bias
        if scale is not None:
            r = r * scale
        r = r.astype(bf16)
        for pr in range(PAIRS):
            dest[pr] = r[:, 128 * pr : 128 * pr + 128]


def attend(k, pr):
    qp, kp, vp = k.q[pr], k.k[pr], k.v[pr]
    total = None
    for hh in range(2):
        h = pr * 2 + hh
        hm = head_mask(hh)
        km = kp * hm
        gate = k.gate[h]
        m8 = jnp.full((8, PAD), -3e38, f32)
        for c in range(4):
            s = dot_t(km[128 * c : 128 * c + 128], qp)
            k.s[128 * c : 128 * c + 128, :] = s
        for c in range(16):
            rows = slice(32 * c, 32 * c + 32)
            lane = 384 - 128 * (c // 4)
            t = k.bias[h, 32 * (c % 4) : 32 * (c % 4) + 32, lane : lane + PAD].astype(f32)
            s = k.s[rows, :] + t * gate + k.mask[rows, :]
            k.s[rows, :] = s
            m8 = jnp.maximum(m8, jnp.max(s.reshape(4, 8, PAD), axis=0))
        m = jnp.max(m8, axis=0, keepdims=True)
        l8 = jnp.zeros((8, PAD), f32)
        for c in range(16):
            rows = slice(32 * c, 32 * c + 32)
            e = jnp.exp(k.s[rows, :] - m)
            k.s[rows, :] = e
            l8 = l8 + fold(e)
        inv = 1.0 / jnp.sum(l8, axis=0, keepdims=True)
        for c in range(16):
            rows = slice(32 * c, 32 * c + 32)
            k.p[h, rows, :] = (k.s[rows, :] * inv).astype(bf16)
        part = dot_l(k.p[h], vp * hm)
        total = part if total is None else total + part
    k.mixed[pr] = total.astype(bf16)


def mixed_all(ref):
    return jnp.concatenate([ref[pr] for pr in range(PAIRS)], axis=1)


def norm_one(k):
    k.fa[...] = dot(mixed_all(k.mixed), wide(k.wa, 3))
    b_out, gain, shift = line(k.b_out), line(k.norm1_gain), line(k.norm1_bias)
    def go(rows, _):
        r = residual_scale * k.tok[rows, :].astype(f32) + k.fa[rows, :] + b_out
        n, inv = stats(r)
        k.n1[rows, :] = n
        k.inv1[rows, :] = jnp.broadcast_to(inv, (32, 128))
        k.hid[rows, :] = (n * gain + shift).astype(bf16)
        return 0
    rows_loop(32, go, 0)


def feed(k, p):
    k.fa[...] = dot(k.hid[...], wide(k.wi, p))
    b = k.sm[p, 4:5, 0:D]
    def go(rows, _):
        x = k.fa[rows, :] + b
        half = 0.5 * (1.0 + lax.erf(x * (1.0 / math.sqrt(2.0))))
        k.act[p, rows, :] = (x * half).astype(bf16)
        k.dg[p, rows, :] = (half + x * (jnp.exp(-0.5 * x * x) * (1.0 / math.sqrt(2.0 * math.pi)))).astype(bf16)
        return 0
    rows_loop(16, go, 0)
    k.fb[...] += dot(k.act[p], wide(k.wo, p))


def feed_init(k):
    k.fb[...] = jnp.zeros((PAD, D), f32)


def norm_two(k):
    b_outer, gain1, shift1 = line(k.b_outer), line(k.norm1_gain), line(k.norm1_bias)
    gain2, shift2 = line(k.norm2_gain), line(k.norm2_bias)
    def go(rows, carry):
        g_gain, g_shift, g_b = carry
        r = residual_scale * (k.n1[rows, :] * gain1 + shift1) + k.fb[rows, :] + b_outer
        n, inv = stats(r)
        k.out[rows, :] = (n * gain2 + shift2).astype(bf16)
        up = k.cot[rows, :].astype(f32)
        g2 = norm_back(up * gain2, n, inv)
        low = g2.astype(bf16)
        k.gb[rows, :] = low
        k.fb[rows, :] = residual_scale * g2
        return g_gain + fold(up * n), g_shift + fold(up), g_b + fold(low.astype(f32))
    zero = jnp.zeros((8, D), f32)
    g_gain, g_shift, g_b = rows_loop(32, go, (zero, zero, zero))
    for row, v in ((3, g_b), (4, g_gain), (5, g_shift)):
        k.sg[row : row + 1, 0:D] = jnp.sum(v, axis=0, keepdims=True)


def feed_back(k, p):
    k.fa[...] = dot_t(k.gb[...], wide(k.wo, p))
    def go(rows, acc):
        gi = (k.fa[rows, :] * k.dg[p, rows, :].astype(f32)).astype(bf16)
        k.dg[p, rows, :] = gi
        return acc + fold(gi.astype(f32))
    acc = rows_loop(32, go, jnp.zeros((8, D), f32))
    k.sg[pl.ds(6 + p, 1), 0:D] = jnp.sum(acc, axis=0, keepdims=True)
    k.fb[...] += dot_t(k.dg[p], wide(k.wi, p))
    k.wo[p] = dot_l(k.act[p], k.gb[...]).astype(bf16).reshape(8, 96, D)
    k.wi[p] = dot_l(k.hid[...], k.dg[p]).astype(bf16).reshape(8, 96, D)


def norm_one_back(k):
    gain = line(k.norm1_gain)
    def go(rows, carry):
        g_gain, g_shift, g_b = carry
        gh = k.fb[rows, :]
        n = k.n1[rows, :]
        g1 = norm_back(gh * gain, n, k.inv1[rows, 0:1])
        low = g1.astype(bf16)
        k.gb[rows, :] = low
        k.fb[rows, :] = residual_scale * g1
        return g_gain + fold(gh * n), g_shift + fold(gh), g_b + fold(low.astype(f32))
    zero = jnp.zeros((8, D), f32)
    g_gain, g_shift, g_b = rows_loop(32, go, (zero, zero, zero))
    for row, v in ((0, g_b), (1, g_gain), (2, g_shift)):
        k.sg[row : row + 1, 0:D] = jnp.sum(v, axis=0, keepdims=True)
    gm = dot_t(k.gb[...], wide(k.wa, 3)).astype(bf16)
    for pr in range(PAIRS):
        k.gm[pr] = gm[:, 128 * pr : 128 * pr + 128]


def attend_back(k, pr):
    qp, kp, vp, gm = k.q[pr], k.k[pr], k.v[pr], k.gm[pr]
    tq = tk = tv = None
    for hh in range(2):
        h = pr * 2 + hh
        hm = head_mask(hh)
        vm = vp * hm
        gate = k.gate[h]
        for c in range(4):
            k.s[128 * c : 128 * c + 128, :] = dot_t(vm[128 * c : 128 * c + 128], gm)
        d8 = jnp.zeros((8, PAD), f32)
        for c in range(16):
            rows = slice(32 * c, 32 * c + 32)
            d8 = d8 + fold(k.s[rows, :] * k.p[h, rows, :].astype(f32))
        total = jnp.sum(d8, axis=0, keepdims=True)
        gg = jnp.zeros((8, PAD), f32)
        k.a[...] = jnp.zeros((128, BIAS), f32)
        for c in range(16):
            rows = slice(32 * c, 32 * c + 32)
            part = slice(32 * (c % 4), 32 * (c % 4) + 32)
            lane = 384 - 128 * (c // 4)
            low = (k.p[h, rows, :].astype(f32) * (k.s[rows, :] - total)).astype(bf16)
            k.gs[rows, :] = low
            g = low.astype(f32)
            gg = gg + fold(g * k.bias[h, part, lane : lane + PAD].astype(f32))
            k.a[part, lane : lane + PAD] += g * gate
        k.ggate[h] = jnp.sum(gg, axis=0, keepdims=True)
        acc = k.a[0:8, :]
        for c in range(1, 16):
            acc = acc + pltpu.roll(k.a[8 * c : 8 * c + 8, :], BIAS - 8 * c, 1)
        flat = acc[0:1]
        for b in range(1, 8):
            flat = flat + pltpu.roll(acc, BIAS - b, 1)[b : b + 1]
        k.goff[h] = flat
        gs = k.gs[...]
        pv = dot(k.p[h], gm * hm)
        pq = dot_l(gs, kp * hm)
        pk = dot(gs, qp * hm)
        tv, tq, tk = (pv, pq, pk) if tv is None else (tv + pv, tq + pq, tk + pk)
    k.q[pr] = (tq.astype(bf16) * 0.125).astype(bf16)
    k.k[pr] = tk.astype(bf16)
    k.v[pr] = tv.astype(bf16)


def gate_back(k):
    weights, _, _, own = gate_weights(k)
    ggate = jnp.concatenate([k.ggate[h] for h in range(HEADS)] + [jnp.zeros((4, PAD), f32)], axis=0)
    first, second, factor = k.first[...], k.second[...], k.factor[...]
    df = ggate * (second * factor - 1.0) * first * (1.0 - first)
    ds = ggate * first * factor * second * (1.0 - second)
    dz = jnp.concatenate([df, ds], axis=0)
    gscale = jnp.sum(ggate * first * second, axis=1, keepdims=True)
    gw = dot(dz, k.tok[...].astype(f32), precision=highest)
    pick = lambda v: jnp.sum(jnp.where(own, v, 0.0), axis=0, keepdims=True)
    k.sg[24:25, 0:D] = pick(gw[0:16])
    k.sg[25:26, 0:D] = pick(gw[16:32])
    k.sg[24:25, D:] = jnp.broadcast_to(jnp.sum(jnp.sum(df, axis=0, keepdims=True), axis=1, keepdims=True), (1, 256))
    k.sg[25:26, D:] = jnp.broadcast_to(jnp.sum(jnp.sum(ds, axis=0, keepdims=True), axis=1, keepdims=True), (1, 256))
    goff = jnp.concatenate([k.goff[h] for h in range(HEADS)] + [jnp.zeros((4, BIAS), f32)], axis=0)
    rel = dot_t(goff, k.hot[...].astype(f32), precision=highest)
    k.sg[12:24, 0:NB] = rel[0:HEADS]
    k.sg[12:24, 512:640] = jnp.broadcast_to(gscale, (16, 128))[0:HEADS]
    return dot(dz.T, weights)


def grad_input(k):
    k.fa[...] = gate_back(k)
    for t, src in ((0, k.q), (1, k.k), (2, k.v)):
        k.fa[...] += dot(mixed_all(src), wide(k.wa, t))
    def go(rows, _):
        k.gtok[rows, :] = (k.fb[rows, :] + k.fa[rows, :]).astype(bf16)
        return 0
    rows_loop(32, go, 0)


def grad_projections(k):
    for t, src in ((0, k.q), (1, k.k), (2, k.v)):
        g = mixed_all(src)
        if t != 1:
            row = jnp.sum(fold(g.astype(f32)), axis=0, keepdims=True)
            for p in range(4):
                at, lane = (6 + p, D) if t == 0 else (12 + 3 * p, 640)
                k.sg[at : at + 1, lane : lane + 192] = row[:, 192 * p : 192 * p + 192]
        k.wa[t] = dot_l(g, k.tok[...]).astype(bf16).reshape(4, 2, 96, D)
    k.wa[3] = dot_l(mixed_all(k.mixed), k.gb[...]).astype(bf16).reshape(4, 2, 96, D)


def each(n, fn, k):
    def go(i, _):
        fn(k, i)
        return 0
    lax.fori_loop(0, n, go, 0)


COMPUTE_SCRATCH = dict(
    row=((1, BIAS), jnp.int32), hot=((NB, BIAS), bf16), tok=((PAD, D), bf16), cot=((PAD, D), bf16), sm=((4, 8, BIAS), f32), mask=((PAD, PAD), f32),
    first=((16, PAD), f32), second=((16, PAD), f32), factor=((16, PAD), f32), gate=((HEADS, 1, PAD), f32),
    bias=((HEADS, 128, 896), bf16), q=((PAIRS, PAD, 128), bf16), k=((PAIRS, PAD, 128), bf16),
    v=((PAIRS, PAD, 128), bf16), s=((PAD, PAD), f32), p=((HEADS, PAD, PAD), bf16), mixed=((PAIRS, PAD, 128), bf16),
    fa=((PAD, D), f32), fb=((PAD, D), f32), n1=((PAD, D), f32), inv1=((PAD, 128), f32), hid=((PAD, D), bf16),
    act=((4, PAD, D), bf16), dg=((4, PAD, D), bf16), out=((PAD, D), bf16), gb=((PAD, D), bf16),
    gm=((PAIRS, PAD, 128), bf16), gs=((PAD, PAD), bf16), a=((128, BIAS), f32), ggate=((HEADS, 1, PAD), f32),
    goff=((HEADS, 1, BIAS), f32), gtok=((PAD, D), bf16), sg=((32, BIAS), f32),
    wa=((4, 4, 2, 96, D), bf16), wi=((4, 8, 96, D), bf16), wo=((4, 8, 96, D), bf16),
)


MESH = pl.DeviceIdType.MESH
BLOCKS = (0, 1, 2)
SEMS = dict(
    wz=(3, 3), w1=(3, 3), w2=(3, 3, 2), w3=(3, 3), sm=(3,), rows=(2, 2, 3), r1=(3, 4), r2=(3, 4, 2), r3=(3, 4),
    r4=(3, 3), a1=(3,), a2=(3, 2), a3=(3,), sg=(5,),
)
COMM_SCRATCH = dict(
    rb1a=((4, 2, 2, 96, D), bf16), rb1=((2, 4, 4, 96, D), bf16), rb2=((3, 4, 2, 96, D), bf16),
    rb3=((3, 4, 96, D), bf16), rb4=((3, 3, 96, D), bf16), sgr=((5, 32, BIAS), f32), sgs=((5, 32, BIAS), f32), fin=((16, BIAS), f32),
)


class Net:
    def __init__(self, k):
        self.k = k
        dp, z = lax.axis_index("dp"), lax.axis_index("tensor")
        self.dp, self.z = dp, z
        c, x, y = dp % 2, (dp // 2) % 2, (dp // 4) % 2
        self.c = c
        across_x, across_y = dp + 2 * (1 - 2 * x), dp + 4 * (1 - 2 * y)
        self.core = (dp + 1 - 2 * c, z)
        self.x, self.y = (across_x, z), (across_y, z)
        self.one = ((1 - c) * across_x + c * across_y, z)
        self.two = (c * across_x + (1 - c) * across_y, z)
        at = lambda cc, yy, xx: 4 * cc + 2 * yy + xx
        ex, ey = at(c, y, 1 - x), at(c, 1 - y, x)
        self.e = at(c, y, x)
        self.e1 = (1 - c) * ex + c * ey
        self.e2 = c * ex + (1 - c) * ey
        self.e12 = at(c, 1 - y, 1 - x)

    def ahead(self, dz):
        return (self.z + dz) % 4

    def behind(self, dz):
        return (self.z + 4 - dz) % 4

    def copy(self, name, index, src, dst, device):
        sems = getattr(self.k, "sem_" + name)
        return pltpu.make_async_remote_copy(
            src_ref=src, dst_ref=dst, send_sem=sems.at[(0, *index)], recv_sem=sems.at[(1, *index)],
            device_id=device, device_id_type=MESH,
        )

    def greet(self):
        barrier = pltpu.get_barrier_semaphore()
        peers = [self.core, self.one, self.two] + [(self.dp, self.ahead(dz)) for dz in (1, 2, 3)]
        for peer in peers:
            pl.semaphore_signal(barrier, inc=1, device_id=peer, device_id_type=MESH)
        pl.semaphore_wait(barrier, len(peers))

    def block(self, b):
        return (self.k.wa, self.k.wi, self.k.wo)[b]

    def chunk(self, b, p, e):
        return self.block(b).at[e // 2, p, e % 2] if b == 0 else self.block(b).at[p, e]

    def side(self, b, p, c):
        return self.block(b).at[pl.ds(2 * c, 2), p] if b == 0 else self.block(b).at[p, pl.ds(4 * c, 4)]

    def wz(self, b, d):
        ref = self.chunk(b, self.z, self.e)
        return self.copy("wz", (b, d - 1), ref, ref, (self.dp, self.ahead(d)))

    def w1(self, b, d):
        ref = self.chunk(b, self.behind(d), self.e)
        return self.copy("w1", (b, d - 1), ref, ref, self.one)

    def w2(self, b, d, i):
        ref = self.chunk(b, self.behind(d), (self.e, self.e1)[i])
        return self.copy("w2", (b, d - 1, i), ref, ref, self.two)

    def w3(self, b, d):
        ref = self.side(b, self.behind(d), self.c)
        return self.copy("w3", (b, d - 1), ref, ref, self.core)

    def sm(self, d):
        ref = self.k.sm.at[self.z]
        return self.copy("sm", (d - 1,), ref, ref, (self.dp, self.ahead(d)))

    def rows(self, a, way, j):
        source, result = ((self.k.out, self.k.out_hbm), (self.k.gtok, self.k.gtok_hbm))[a]
        slot = self.z - j if way == 0 else self.z + j
        to = self.z + 1 if way == 0 else self.z - 1
        at = result.at[pl.ds(pl.multiple_of(slot * SEQ, 16), SEQ)]
        return self.copy("rows", (a, way, j), source.at[pl.ds(0, SEQ)] if j == 0 else at, at, (self.dp, to))

    def sends(self, way, j):
        z = self.z
        return (z <= 2) & (z >= j) if way == 0 else (z >= 1) & (z + j <= 3)

    def receives(self, way, j):
        z = self.z
        return z >= 1 + j if way == 0 else z + 1 + j <= 3

    def r1(self, b, p):
        dst = self.k.rb1a.at[p] if b == 0 else self.k.rb1.at[b - 1, p]
        return self.copy("r1", (b, p), self.side(b, p, 1 - self.c), dst, self.core)

    def r2(self, b, p, i):
        return self.copy("r2", (b, p, i), self.chunk(b, p, (self.e1, self.e12)[i]), self.k.rb2.at[b, p, i], self.one)

    def r3(self, b, p):
        return self.copy("r3", (b, p), self.chunk(b, p, self.e2), self.k.rb3.at[b, p], self.two)

    def r4(self, b, d):
        to = self.ahead(d)
        return self.copy("r4", (b, d - 1), self.chunk(b, to, self.e), self.k.rb4.at[b, d - 1], (self.dp, to))

    def result(self, b, e):
        return (self.k.ra, self.k.ri, self.k.ro)[b].at[e]

    def keep(self, b):
        return pltpu.make_async_copy(self.chunk(b, self.z, self.e), self.result(b, self.e), self.k.sem_keep.at[b])

    def a1(self, b):
        return self.copy("a1", (b,), self.chunk(b, self.z, self.e), self.result(b, self.e), self.one)

    def a2(self, b, i):
        src = (self.chunk(b, self.z, self.e), self.result(b, self.e1))[i]
        return self.copy("a2", (b, i), src, self.result(b, (self.e, self.e1)[i]), self.two)

    def a3(self, b):
        ref = self.result(b, pl.ds(4 * self.c, 4))
        return self.copy("a3", (b,), ref, ref, self.core)

    def sg(self, i):
        device = (self.core, self.x, self.y, (self.dp, self.flip(1)), (self.dp, self.flip(2)))[i]
        return self.copy("sg", (i,), self.k.sg if i == 0 else self.k.sgs.at[i - 1], self.k.sgr.at[i], device)

    def flip(self, bit):
        return self.z + bit * (1 - 2 * ((self.z // bit) % 2))


def loop(n, fn):
    def go(i, _):
        fn(i)
        return 0
    lax.fori_loop(0, n, go, 0)


def when(condition, fn):
    @pl.when(condition)
    def _():
        fn()


PIECES = ((0, 1), (0, 2), (0, 3), (1, 1), (2, 1), (1, 2), (2, 2), (1, 3), (2, 3))
WINDOW = 3


def weight_step(net, t):
    if t < 9:
        b, d = PIECES[t]
        net.wz(b, d).wait_recv()
        net.w1(b, d).start()
        if t + WINDOW < 9:
            net.wz(*PIECES[t + WINDOW]).start()
    if 0 <= t - 1 < 9:
        b, d = PIECES[t - 1]
        net.w1(b, d).wait_recv()
        net.w2(b, d, 0).start()
        net.w2(b, d, 1).start()
    if 0 <= t - 2 < 9:
        b, d = PIECES[t - 2]
        net.w2(b, d, 0).wait_recv()
        net.w2(b, d, 1).wait_recv()
        net.w3(b, d).start()
    if 0 <= t - 3 < 9:
        net.w3(*PIECES[t - 3]).wait_recv()


def weights_sent(net):
    for b, d in PIECES:
        net.wz(b, d).wait_send()
        net.w1(b, d).wait_send()
        net.w2(b, d, 0).wait_send()
        net.w2(b, d, 1).wait_send()
        net.w3(b, d).wait_send()


def rows_step(net, a, j):
    for way in (0, 1):
        if j > 0:
            when(net.receives(way, j - 1), lambda: net.rows(a, way, j - 1).wait_recv())
        if j < 3:
            when(net.sends(way, j), lambda: net.rows(a, way, j).start())


def rows_sent(net, a):
    for j in range(3):
        for way in (0, 1):
            when(net.sends(way, j), lambda: net.rows(a, way, j).wait_send())


def add(net, b, p, e, ref):
    k = net.k
    if b == 0:
        k.wa[e // 2, p, e % 2] = k.wa[e // 2, p, e % 2] + ref[...]
    else:
        net.block(b)[p, e] = net.block(b)[p, e] + ref[...]


def halves(net, b, p):
    net.r1(b, p).wait_recv()
    for j in range(4):
        src = net.k.rb1a.at[p, j // 2, j % 2] if b == 0 else net.k.rb1.at[b - 1, p, j]
        add(net, b, p, 4 * net.c + j, src)
    net.r2(b, p, 1).start()
    net.r2(b, p, 0).start()


def quarters(net, b, p):
    net.r2(b, p, 1).wait_recv()
    add(net, b, p, net.e2, net.k.rb2.at[b, p, 1])
    net.r3(b, p).start()
    net.r2(b, p, 0).wait_recv()
    add(net, b, p, net.e, net.k.rb2.at[b, p, 0])


def eighths(net, b, i):
    p = net.ahead(1 + i)
    net.r3(b, p).wait_recv()
    add(net, b, p, net.e, net.k.rb3.at[b, p])
    if i < 3:
        net.r4(b, 1 + i).start()


def over_z(net, b):
    k = net.k
    for d in (1, 2, 3):
        net.r4(b, d).wait_recv()
    own = k.wa[net.e // 2, net.z, net.e % 2] if b == 0 else net.block(b)[net.z, net.e]
    total = (own.astype(f32) + k.rb4[b, 0].astype(f32)) + (k.rb4[b, 1].astype(f32) + k.rb4[b, 2].astype(f32))
    if b == 0:
        k.wa[net.e // 2, net.z, net.e % 2] = total.astype(bf16)
    else:
        net.block(b)[net.z, net.e] = total.astype(bf16)
    net.keep(b).start()
    net.a1(b).start()
    net.a2(b, 0).start()


def around(net, b):
    net.a1(b).wait_recv()
    net.a2(b, 1).start()


def to_core(net, b):
    net.keep(b).wait()
    net.a2(b, 0).wait_recv()
    net.a2(b, 1).wait_recv()
    net.a3(b).start()


def gradients_sent(net, b):
    net.a3(b).wait_recv()
    for p in range(4):
        net.r1(b, p).wait_send()
        net.r2(b, p, 0).wait_send()
        net.r2(b, p, 1).wait_send()
        net.r3(b, p).wait_send()
    for d in (1, 2, 3):
        net.r4(b, d).wait_send()
    net.a1(b).wait_send()
    net.a2(b, 0).wait_send()
    net.a2(b, 1).wait_send()
    net.a3(b).wait_send()


def small_step(net, i):
    k = net.k
    if i > 0:
        net.sg(i - 1).wait_recv()
        mine = k.sg[...] if i == 1 else k.sgs[i - 2]
        k.sgs[i - 1] = mine + k.sgr[i - 1]
    if i < 5:
        net.sg(i).start()


def kernel(names, *refs):
    k = K()
    for name, ref in zip(names, refs):
        setattr(k, name, ref)
    net = Net(k)
    z = net.z
    own_rows = pl.ds(pl.multiple_of(z * SEQ, 16), SEQ)
    moves = [
        (k.wq_hbm, k.wa.at[0, z]), (k.wk_hbm, k.wa.at[1, z]), (k.wv_hbm, k.wa.at[2, z]), (k.wout_hbm, k.wa.at[3, z]),
        (k.wi_hbm, k.wi.at[z]), (k.wo_hbm, k.wo.at[z]),
        (k.tok_hbm.at[own_rows], k.tok.at[pl.ds(0, SEQ)]), (k.cot_hbm.at[own_rows], k.cot.at[pl.ds(0, SEQ)]),
    ]
    local = [pltpu.make_async_copy(src, dst, k.sem_in.at[i]) for i, (src, dst) in enumerate(moves)]
    for c in local:
        c.start()
    net.greet()
    for c in local[0:4]:
        c.wait()
    for piece in PIECES[0:WINDOW]:
        net.wz(*piece).start()
    k.tok[SEQ:PAD] = jnp.zeros((PAD - SEQ, D), bf16)
    k.cot[SEQ:PAD] = jnp.zeros((PAD - SEQ, D), bf16)
    k.sg[...] = jnp.zeros((32, BIAS), f32)
    k.factor[...] = jnp.zeros((16, PAD), f32)
    own_small(k, z)
    for d in (1, 2, 3):
        net.sm(d).start()
    for c in local[4:8]:
        c.wait()
    weight_step(net, 0)
    mask_build(k, z)
    weight_step(net, 1)
    for d in (1, 2, 3):
        net.sm(d).wait_recv()
    gates(k)
    weight_step(net, 2)
    bias_tables(k)
    weight_step(net, 3)
    weight_step(net, 4)
    weight_step(net, 5)
    project(k)

    def forward(pr):
        attend(k, pr)
        when(pr == 1, lambda: weight_step(net, 6))
        when(pr == 4, lambda: weight_step(net, 7))
    loop(PAIRS, forward)
    norm_one(k)
    weight_step(net, 8)
    feed_init(k)

    def layer_two(i):
        when(i == 2, lambda: weight_step(net, 9))
        when(i == 3, lambda: (weight_step(net, 10), weight_step(net, 11)))
        feed(k, net.behind(i))
    loop(4, layer_two)
    norm_two(k)
    here = [
        pltpu.make_async_copy(k.out.at[pl.ds(0, SEQ)], k.out_hbm.at[own_rows], k.sem_in.at[0]),
        pltpu.make_async_copy(k.gtok.at[pl.ds(0, SEQ)], k.gtok_hbm.at[own_rows], k.sem_in.at[1]),
    ]
    here[0].start()
    rows_step(net, 0, 0)
    weights_sent(net)

    def layer_two_back(i):
        p = net.ahead(1 + i)
        feed_back(k, p)
        net.r1(2, p).start()
        net.r1(1, p).start()
        def last():
            before = net.ahead(i)
            halves(net, 2, before)
            halves(net, 1, before)
        when(i > 0, last)
    loop(4, layer_two_back)
    rows_step(net, 0, 1)
    norm_one_back(k)
    both = lambda fn, i: (fn(net, 2, net.ahead(1 + i)), fn(net, 1, net.ahead(1 + i)))
    pass_on = lambda i: (eighths(net, 2, i), eighths(net, 1, i))
    both(halves, 3)
    both(quarters, 0)

    def backward(pr):
        attend_back(k, pr)
        when(pr == 3, lambda: (both(quarters, 1), pass_on(0)))
        when(pr == 5, lambda: rows_step(net, 0, 2))
    loop(PAIRS, backward)
    grad_input(k)
    here[1].start()
    rows_step(net, 1, 0)
    both(quarters, 2)
    pass_on(1)
    grad_projections(k)
    for i in range(4):
        net.r1(0, net.ahead(1 + i)).start()
    small_step(net, 0)
    both(quarters, 3)
    pass_on(2)
    halves(net, 0, net.ahead(1))
    halves(net, 0, net.ahead(2))
    rows_step(net, 0, 3)
    small_step(net, 1)
    pass_on(3)
    halves(net, 0, net.ahead(3))
    halves(net, 0, net.ahead(4))
    rows_step(net, 1, 1)
    small_step(net, 2)
    quarters(net, 0, net.ahead(1))
    quarters(net, 0, net.ahead(2))
    eighths(net, 0, 0)
    small_step(net, 3)
    quarters(net, 0, net.ahead(3))
    eighths(net, 0, 1)
    over_z(net, 2)
    over_z(net, 1)
    quarters(net, 0, net.ahead(4))
    eighths(net, 0, 2)
    small_step(net, 4)
    eighths(net, 0, 3)
    around(net, 2)
    around(net, 1)
    rows_step(net, 1, 2)
    over_z(net, 0)
    to_core(net, 2)
    to_core(net, 1)
    small_step(net, 5)
    k.fin[...] = jnp.zeros((16, BIAS), f32)
    k.fin[0:6, :] = k.sgs[4, 0:6, :]
    k.fin[6:7, :] = k.sgs[4, pl.ds(6 + z, 1), :]
    for i in range(3):
        k.fin[8 + i : 9 + i, :] = k.sgs[4, pl.ds(12 + 3 * z + i, 1), :]
    k.fin[11:13, :] = k.sgs[4, 24:26, :]
    finish = pltpu.make_async_copy(k.fin, k.sg_hbm, k.sem_in.at[2])
    finish.start()
    around(net, 0)
    to_core(net, 0)
    rows_step(net, 1, 3)
    for b in (2, 1, 0):
        gradients_sent(net, b)
    for i in range(5):
        net.sg(i).wait_send()
    for d in (1, 2, 3):
        net.sm(d).wait_send()
    for a in (0, 1):
        rows_sent(net, a)
    here[0].wait()
    here[1].wait()
    finish.wait()


def finish_kernel(out, gtok, ra, ri, ro, sg, *rest):
    names = FINAL + ("stage", "wide", "sem")
    k = K()
    for name, ref in zip(names, rest):
        setattr(k, name, ref)
    copies = [pltpu.make_async_copy(out, k.output, k.sem.at[0]), pltpu.make_async_copy(gtok, k.grad_tokens, k.sem.at[1])]
    for c in copies:
        c.start()
    inward = [pltpu.make_async_copy(src, k.stage.at[i], k.sem.at[2 + i]) for i, src in enumerate((ri, ro, ra))]
    for c in inward:
        c.start()
    row = lambda r, lane, n: sg[r : r + 1, lane : lane + n].reshape(n)
    k.b_out[...], k.norm1_gain[...], k.norm1_bias[...] = row(0, 0, D), row(1, 0, D), row(2, 0, D)
    k.b_outer[...], k.norm2_gain[...], k.norm2_bias[...] = row(3, 0, D), row(4, 0, D), row(5, 0, D)
    k.b_inner[...], k.b_query[...], k.b_value[...] = row(6, 0, D), row(6, D, 192), row(8, 640, 192)
    k.rel_table[...] = sg[8:11, 0:NB]
    lane = lax.broadcasted_iota(jnp.int32, (1, 128), 1)
    cell = lambda r, at: sg[r : r + 1, at : at + 128]
    k.gate_scale[...] = jnp.where(lane == 0, cell(8, 512), jnp.where(lane == 1, cell(9, 512), cell(10, 512)))[:, 0:3]
    k.gate_bias[...] = jnp.where(lane < 4, cell(11, D), cell(12, D))[:, 0:8]
    for i in (0, 1):
        heads = cell(11 + i, 0)
        for pr in range(1, PAIRS):
            heads = heads + cell(11 + i, 128 * pr)
        k.gate_weight[4 * i : 4 * i + 4, :] = jnp.broadcast_to(heads[:, 0:HEAD] + heads[:, HEAD:128], (4, HEAD))
    outward = []
    for i, c in enumerate(inward):
        c.wait()
        def widen(j):
            k.wide[i, j] = k.stage[i, j].astype(f32)
        loop(8, widen)
        if i < 2:
            to = [(k.wide.at[i], (k.w_inner, k.w_outer)[i])]
        else:
            to = [(k.wide.at[i, pl.ds(2 * j, 2)], ref) for j, ref in enumerate((k.w_query, k.w_key, k.w_value, k.w_out))]
        for src, dst in to:
            copy = pltpu.make_async_copy(src, dst, k.sem.at[5 + len(outward)])
            copy.start()
            outward.append(copy)
    for c in copies + outward:
        c.wait()


FINAL = (
    "output", "grad_tokens", "w_query", "w_key", "w_value", "w_out", "w_inner", "w_outer", "b_query", "b_value", "b_out",
    "gate_weight", "gate_bias", "gate_scale", "rel_table", "norm1_gain", "norm1_bias", "b_inner", "b_outer", "norm2_gain",
    "norm2_bias",
)


def body(
    tokens, slot_kind, offset_bucket, w_query, b_query, w_key, w_value, b_value, w_out, b_out, gate_weight, gate_bias,
    gate_scale, rel_table, norm1_gain, norm1_bias, w_inner, b_inner, w_outer, b_outer, norm2_gain, norm2_bias, cotangent,
):
    n_dp = lax.axis_size("dp")
    rows = tokens.shape[0]
    shape = jax.ShapeDtypeStruct
    anywhere = pl.BlockSpec(memory_space=pl.ANY)
    vmem = pl.BlockSpec(memory_space=pltpu.VMEM)
    smem = pl.BlockSpec(memory_space=pltpu.SMEM)
    given = dict(
        kinds=(smem, slot_kind), bucket=(vmem, offset_bucket.reshape(1, OFFSETS)), rel=(vmem, rel_table.T),
        b_query=(vmem, b_query), b_value=(vmem, b_value), b_inner=(vmem, b_inner), scale=(vmem, gate_scale.reshape(1, 3)),
        gw=(vmem, gate_weight.T), gate_bias=(vmem, gate_bias), b_out=(vmem, b_out), b_outer=(vmem, b_outer),
        norm1_gain=(vmem, norm1_gain), norm1_bias=(vmem, norm1_bias), norm2_gain=(vmem, norm2_gain),
        norm2_bias=(vmem, norm2_bias), tok_hbm=(anywhere, tokens), cot_hbm=(anywhere, cotangent),
        wq_hbm=(anywhere, w_query.T.reshape(2, 96, D)), wk_hbm=(anywhere, w_key.T.reshape(2, 96, D)),
        wv_hbm=(anywhere, w_value.T.reshape(2, 96, D)), wout_hbm=(anywhere, w_out.reshape(2, 96, D)),
        wi_hbm=(anywhere, w_inner.reshape(8, 96, D)), wo_hbm=(anywhere, w_outer.reshape(8, 96, D)),
    )
    names = list(given) + ["out_hbm", "gtok_hbm", "ra", "ri", "ro", "sg_hbm"]
    scratch = []
    for name, (dims, dtype) in (COMPUTE_SCRATCH | COMM_SCRATCH).items():
        names.append(name)
        scratch.append(pltpu.VMEM(dims, dtype))
    for name, dims in SEMS.items():
        names.append("sem_" + name)
        scratch.append(pltpu.SemaphoreType.DMA((2, *dims)))
    for name, count in (("sem_in", 8), ("sem_keep", 3)):
        names.append(name)
        scratch.append(pltpu.SemaphoreType.DMA((count,)))
    whole = shape((8, 96, D), bf16)
    out, gtok, ra, ri, ro, sg = pl.pallas_call(
        functools.partial(kernel, names),
        in_specs=[spec for spec, _ in given.values()],
        out_specs=[anywhere] * 6,
        out_shape=[shape((rows, D), bf16), shape((rows, D), bf16), whole, whole, whole, shape((16, BIAS), f32)],
        scratch_shapes=scratch,
        compiler_params=pltpu.CompilerParams(collective_id=0, has_side_effects=True, vmem_limit_bytes=VMEM_LIMIT),
    )(*[value for _, value in given.values()])
    if n_dp > 8:
        groups = [list(range(g, n_dp, 8)) for g in range(8)]
        ra, ri, ro, sg = lax.psum((ra.astype(f32), ri.astype(f32), ro.astype(f32), sg), "dp", axis_index_groups=groups)
        ra, ri, ro = ra.astype(bf16), ri.astype(bf16), ro.astype(bf16)
    vector = shape((D,), f32)
    part = shape((2, 96, D), f32)
    final = dict(
        output=(anywhere, shape((rows, D), bf16)), grad_tokens=(anywhere, shape((rows, D), bf16)),
        w_query=(anywhere, part), w_key=(anywhere, part), w_value=(anywhere, part), w_out=(anywhere, part),
        w_inner=(anywhere, shape((8, 96, D), f32)), w_outer=(anywhere, shape((8, 96, D), f32)),
        b_query=(vmem, shape((192,), f32)), b_value=(vmem, shape((192,), f32)), gate_weight=(vmem, shape((8, HEAD), f32)),
        gate_bias=(vmem, shape((1, 8), f32)), gate_scale=(vmem, shape((1, 3), f32)), rel_table=(vmem, shape((3, NB), f32)),
    )
    specs, shapes = zip(*[final.get(name, (vmem, vector)) for name in FINAL])
    results = pl.pallas_call(
        finish_kernel,
        in_specs=[anywhere] * 5 + [vmem],
        out_specs=list(specs),
        out_shape=list(shapes),
        scratch_shapes=[pltpu.VMEM((3, 8, 96, D), bf16), pltpu.VMEM((3, 8, 96, D), f32), pltpu.SemaphoreType.DMA((11,))],
        compiler_params=pltpu.CompilerParams(vmem_limit_bytes=32 * 2**20),
    )(out, gtok, ra, ri, ro, sg)
    r = dict(zip(FINAL, results))
    for name in ("w_query", "w_key", "w_value"):
        r[name] = r[name].reshape(192, D).T
    r["w_out"] = r["w_out"].reshape(192, D)
    r["w_inner"] = r["w_inner"].reshape(D, D)
    r["w_outer"] = r["w_outer"].reshape(D, D)
    r["gate_weight"] = r["gate_weight"].T
    r["gate_bias"] = r["gate_bias"].reshape(8)
    r["gate_scale"] = r["gate_scale"].reshape(3)
    r["rel_table"] = r["rel_table"].T
    order = (
        "output", "grad_tokens", "w_query", "b_query", "w_key", "w_value", "b_value", "w_out", "b_out", "gate_weight",
        "gate_bias", "gate_scale", "rel_table", "norm1_gain", "norm1_bias", "w_inner", "b_inner", "w_outer", "b_outer",
        "norm2_gain", "norm2_bias",
    )
    return tuple(r[name] for name in order)


def solution(mesh):
    in_specs = (
        P("dp", None),
        P("dp"),
        P(),
        P(None, "tensor"),
        P("tensor"),
        P(None, "tensor"),
        P(None, "tensor"),
        P("tensor"),
        P("tensor", None),
        P(),
        P(),
        P(),
        P("tensor"),
        P(None, "tensor"),
        P(),
        P(),
        P(None, "tensor"),
        P("tensor"),
        P("tensor", None),
        P(),
        P(),
        P(),
        P("dp", None),
    )
    out_specs = (
        P("dp", None),
        P("dp", None),
        P(None, "tensor"),
        P("tensor"),
        P(None, "tensor"),
        P(None, "tensor"),
        P("tensor"),
        P("tensor", None),
        P(),
        P(),
        P(),
        P("tensor"),
        P(None, "tensor"),
        P(),
        P(),
        P(None, "tensor"),
        P("tensor"),
        P("tensor", None),
        P(),
        P(),
        P(),
    )
    return jax.shard_map(body, mesh=mesh, in_specs=in_specs, out_specs=out_specs, check_vma=False)
```

```python
import functools
import math

import jax
import jax.numpy as jnp
from jax import lax
from jax.experimental import pallas as pl
from jax.experimental.pallas import tpu as pltpu
from jax.sharding import PartitionSpec as P

HEAD = 64
SEQ = 496
PAD = 512
D = 768
PAIRS = 6
HEADS = 12
BIAS = 1024
NB = 320
VMEM_LIMIT = 64 * 2**20 - 2**16
OFFSETS = 991
HALF = SEQ // 2
f32 = jnp.float32
bf16 = jnp.bfloat16
residual_scale = 24.0**0.25
norm_epsilon = 1e-05
highest = lax.Precision.HIGHEST


def dot(a, b, precision=None):
    return lax.dot_general(a, b, (((1,), (0,)), ((), ())), preferred_element_type=f32, precision=precision)


def dot_t(a, b, precision=None):
    return lax.dot_general(a, b, (((1,), (1,)), ((), ())), preferred_element_type=f32, precision=precision)


def dot_l(a, b):
    return lax.dot_general(a, b, (((0,), (0,)), ((), ())), preferred_element_type=f32)


def fold(x):
    return jnp.sum(x.reshape(x.shape[0] // 8, 8, x.shape[1]), axis=0)


def stats(r):
    c = r - jnp.mean(r, -1, keepdims=True)
    inv = lax.rsqrt(jnp.mean(c * c, -1, keepdims=True) + norm_epsilon)
    return c * inv, inv


def norm_back(g, n, inv):
    return inv * (g - jnp.mean(g, -1, keepdims=True) - n * jnp.mean(g * n, -1, keepdims=True))


def wide(ref, i):
    return ref[i].reshape(D, D)


def rows_loop(step, body, carry, first=0, last=PAD):
    def go(c, carry):
        return body(pl.ds(pl.multiple_of(c * step, step), step), carry)
    return lax.fori_loop(first // step, last // step, go, carry)


class K:
    pass


def head_mask(hh):
    lane = lax.broadcasted_iota(jnp.int32, (1, 128), 1)
    return jnp.where((lane // HEAD) == hh, 1.0, 0.0).astype(bf16)


def line(ref):
    return ref[...].astype(f32).reshape(1, ref.shape[0])


def one_hot(k):
    k.row[...] = jnp.full((1, BIAS), -1, jnp.int32)
    k.row[:, 0:OFFSETS] = k.bucket[...]
    hot = jnp.where(lax.broadcasted_iota(jnp.int32, (NB, BIAS), 0) == k.row[...], 1.0, 0.0).astype(bf16)
    for n in range(4):
        m = lax.broadcasted_iota(jnp.int32, (BIAS, 256), 0) + lax.broadcasted_iota(jnp.int32, (BIAS, 256), 1) + 256 * n
        turn = jnp.where((m == 879) | (m == 1903), 1.0, 0.0).astype(bf16)
        k.hot[:, 256 * n : 256 * n + 256] = dot(hot, turn).astype(bf16)


def own_small(k, z):
    one_hot(k)
    k.sm[z, 0:3, :] = dot(k.rel[...], k.hot[...])
    k.sm[z, 3:4, 0:192] = line(k.b_query)
    k.sm[z, 3:4, 192:384] = line(k.b_value)
    k.sm[z, 4:5, 0:D] = line(k.b_inner)
    for i in range(3):
        k.sm[z, 5 + i : 6 + i, :] = jnp.broadcast_to(k.scale[:, i : i + 1].astype(f32), (1, BIAS))


def mask_build(k, z):
    kind = k.kinds[z].astype(f32)
    def go(rows, _):
        j = lax.broadcasted_iota(jnp.int32, (32, PAD), 0) + rows.start
        i = lax.broadcasted_iota(jnp.int32, (32, PAD), 1)
        far = jnp.where(j < HALF, 0, 1) != jnp.where(i < HALF, 0, 1)
        k.mask[rows, :] = jnp.where(j < SEQ, 0.0, -1e30) + jnp.where(far, -1e30, 0.0) * kind
        return 0
    rows_loop(32, go, 0)


def gate_weights(k):
    gw = k.gw[...].astype(f32)
    tile = lambda v: jnp.concatenate([jnp.concatenate([v, v], axis=1)] * PAIRS, axis=1)
    first = tile(jnp.sum(gw[0:4], axis=0, keepdims=True))
    second = tile(jnp.sum(gw[4:8], axis=0, keepdims=True))
    bias = line(k.gate_bias)
    own = (lax.broadcasted_iota(jnp.int32, (16, D), 1) // HEAD) == lax.broadcasted_iota(jnp.int32, (16, D), 0)
    both = jnp.concatenate([jnp.where(own, first, 0.0), jnp.where(own, second, 0.0)], axis=0)
    add = lambda v: jnp.sum(v, axis=1, keepdims=True)
    return both, add(bias[:, 0:4]), add(bias[:, 4:8]), own


def gates(k):
    weights, first_bias, second_bias, _ = gate_weights(k)
    logits = dot_t(weights, k.tok[...].astype(f32), precision=highest)
    first = jax.nn.sigmoid(logits[0:16] + first_bias)
    second = jax.nn.sigmoid(logits[16:32] + second_bias)
    k.first[...] = first
    k.second[...] = second
    for h in range(HEADS):
        k.factor[h : h + 1, :] = k.sm[h // 3, 5 + h % 3 : 6 + h % 3, 0:PAD]
    value = first * (second * k.factor[...] - 1.0) + 2.0
    for h in range(HEADS):
        k.gate[h] = value[h : h + 1, :]


def bias_tables(k):
    def go(p, _):
        for i in range(3):
            row = jnp.broadcast_to(k.sm[p, i : i + 1, :], (128, BIAS))
            k.bias[p * 3 + i] = pltpu.roll(row, 0, 1, stride=1, stride_axis=0)[:, 0:896].astype(bf16)
        return 0
    lax.fori_loop(0, 4, go, 0)


def small_row(k, row, start):
    return jnp.concatenate([k.sm[p, row : row + 1, start : start + 192] for p in range(4)], axis=1)


def project(k):
    bq = small_row(k, 3, 0)
    bv = small_row(k, 3, 192)
    for t, dest, bias, scale in ((0, k.q, bq, 0.125), (1, k.k, None, None), (2, k.v, bv, None)):
        r = dot_t(k.tok[...], wide(k.wa, t))
        if bias is not None:
            r = r + bias
        if scale is not None:
            r = r * scale
        r = r.astype(bf16)
        for pr in range(PAIRS):
            dest[pr] = r[:, 128 * pr : 128 * pr + 128]


def attend(k, pr):
    qp, kp, vp = k.q[pr], k.k[pr], k.v[pr]
    total = None
    for hh in range(2):
        h = pr * 2 + hh
        hm = head_mask(hh)
        km = kp * hm
        gate = k.gate[h]
        m8 = jnp.full((8, PAD), -3e38, f32)
        for c in range(4):
            s = dot_t(km[128 * c : 128 * c + 128], qp)
            k.s[128 * c : 128 * c + 128, :] = s
        for c in range(16):
            rows = slice(32 * c, 32 * c + 32)
            lane = 384 - 128 * (c // 4)
            t = k.bias[h, 32 * (c % 4) : 32 * (c % 4) + 32, lane : lane + PAD].astype(f32)
            s = k.s[rows, :] + t * gate + k.mask[rows, :]
            k.s[rows, :] = s
            m8 = jnp.maximum(m8, jnp.max(s.reshape(4, 8, PAD), axis=0))
        m = jnp.max(m8, axis=0, keepdims=True)
        l8 = jnp.zeros((8, PAD), f32)
        for c in range(16):
            rows = slice(32 * c, 32 * c + 32)
            e = jnp.exp(k.s[rows, :] - m)
            k.s[rows, :] = e
            l8 = l8 + fold(e)
        inv = 1.0 / jnp.sum(l8, axis=0, keepdims=True)
        for c in range(16):
            rows = slice(32 * c, 32 * c + 32)
            k.p[h, rows, :] = (k.s[rows, :] * inv).astype(bf16)
        part = dot_l(k.p[h], vp * hm)
        total = part if total is None else total + part
    k.mixed[pr] = total.astype(bf16)


def mixed_all(ref):
    return jnp.concatenate([ref[pr] for pr in range(PAIRS)], axis=1)


def norm_one(k):
    k.fa[...] = dot(mixed_all(k.mixed), wide(k.wa, 3))
    b_out, gain, shift = line(k.b_out), line(k.norm1_gain), line(k.norm1_bias)
    def go(rows, _):
        r = residual_scale * k.tok[rows, :].astype(f32) + k.fa[rows, :] + b_out
        n, inv = stats(r)
        k.n1[rows, :] = n
        k.inv1[rows, :] = jnp.broadcast_to(inv, (32, 128))
        k.hid[rows, :] = (n * gain + shift).astype(bf16)
        return 0
    rows_loop(32, go, 0)


def feed(k, p):
    k.fa[...] = dot(k.hid[...], wide(k.wi, p))
    b = k.sm[p, 4:5, 0:D]
    def go(rows, _):
        x = k.fa[rows, :] + b
        half = 0.5 * (1.0 + lax.erf(x * (1.0 / math.sqrt(2.0))))
        k.act[p, rows, :] = (x * half).astype(bf16)
        k.dg[p, rows, :] = (half + x * (jnp.exp(-0.5 * x * x) * (1.0 / math.sqrt(2.0 * math.pi)))).astype(bf16)
        return 0
    rows_loop(16, go, 0)
    k.fb[...] += dot(k.act[p], wide(k.wo, p))


def feed_init(k):
    k.fb[...] = jnp.zeros((PAD, D), f32)


def norm_two(k, part):
    b_outer, gain1, shift1 = line(k.b_outer), line(k.norm1_gain), line(k.norm1_bias)
    gain2, shift2 = line(k.norm2_gain), line(k.norm2_bias)
    def go(rows, carry):
        g_gain, g_shift, g_b = carry
        r = residual_scale * (k.n1[rows, :] * gain1 + shift1) + k.fb[rows, :] + b_outer
        n, inv = stats(r)
        k.out[rows, :] = (n * gain2 + shift2).astype(bf16)
        up = k.cot[rows, :].astype(f32)
        g2 = norm_back(up * gain2, n, inv)
        low = g2.astype(bf16)
        k.gb[rows, :] = low
        k.fb[rows, :] = residual_scale * g2
        return g_gain + fold(up * n), g_shift + fold(up), g_b + fold(low.astype(f32))
    zero = jnp.zeros((8, D), f32)
    g_gain, g_shift, g_b = rows_loop(32, go, (zero, zero, zero), 256 * part, 256 * part + 256)
    for row, v in ((3, g_b), (4, g_gain), (5, g_shift)):
        k.sg[row : row + 1, 0:D] += jnp.sum(v, axis=0, keepdims=True)


def feed_back(k, p):
    k.fa[...] = dot_t(k.gb[...], wide(k.wo, p))
    def go(rows, acc):
        gi = (k.fa[rows, :] * k.dg[p, rows, :].astype(f32)).astype(bf16)
        k.dg[p, rows, :] = gi
        return acc + fold(gi.astype(f32))
    acc = rows_loop(32, go, jnp.zeros((8, D), f32))
    k.sg[pl.ds(6 + p, 1), 0:D] = jnp.sum(acc, axis=0, keepdims=True)
    k.fb[...] += dot_t(k.dg[p], wide(k.wi, p))
    k.wo[p] = dot_l(k.act[p], k.gb[...]).astype(bf16).reshape(8, 96, D)
    k.wi[p] = dot_l(k.hid[...], k.dg[p]).astype(bf16).reshape(8, 96, D)


def norm_one_back(k):
    gain = line(k.norm1_gain)
    def go(rows, carry):
        g_gain, g_shift, g_b = carry
        gh = k.fb[rows, :]
        n = k.n1[rows, :]
        g1 = norm_back(gh * gain, n, k.inv1[rows, 0:1])
        low = g1.astype(bf16)
        k.gb[rows, :] = low
        k.fb[rows, :] = residual_scale * g1
        return g_gain + fold(gh * n), g_shift + fold(gh), g_b + fold(low.astype(f32))
    zero = jnp.zeros((8, D), f32)
    g_gain, g_shift, g_b = rows_loop(32, go, (zero, zero, zero))
    for row, v in ((0, g_b), (1, g_gain), (2, g_shift)):
        k.sg[row : row + 1, 0:D] = jnp.sum(v, axis=0, keepdims=True)
    gm = dot_t(k.gb[...], wide(k.wa, 3)).astype(bf16)
    for pr in range(PAIRS):
        k.gm[pr] = gm[:, 128 * pr : 128 * pr + 128]


def attend_back(k, pr):
    qp, kp, vp, gm = k.q[pr], k.k[pr], k.v[pr], k.gm[pr]
    tq = tk = tv = None
    for hh in range(2):
        h = pr * 2 + hh
        hm = head_mask(hh)
        vm = vp * hm
        gate = k.gate[h]
        for c in range(4):
            k.s[128 * c : 128 * c + 128, :] = dot_t(vm[128 * c : 128 * c + 128], gm)
        d8 = jnp.zeros((8, PAD), f32)
        for c in range(16):
            rows = slice(32 * c, 32 * c + 32)
            d8 = d8 + fold(k.s[rows, :] * k.p[h, rows, :].astype(f32))
        total = jnp.sum(d8, axis=0, keepdims=True)
        gg = jnp.zeros((8, PAD), f32)
        k.a[...] = jnp.zeros((128, BIAS), f32)
        for c in range(16):
            rows = slice(32 * c, 32 * c + 32)
            part = slice(32 * (c % 4), 32 * (c % 4) + 32)
            lane = 384 - 128 * (c // 4)
            low = (k.p[h, rows, :].astype(f32) * (k.s[rows, :] - total)).astype(bf16)
            k.gs[rows, :] = low
            g = low.astype(f32)
            gg = gg + fold(g * k.bias[h, part, lane : lane + PAD].astype(f32))
            k.a[part, lane : lane + PAD] += g * gate
        k.ggate[h] = jnp.sum(gg, axis=0, keepdims=True)
        acc = k.a[0:8, :]
        for c in range(1, 16):
            acc = acc + pltpu.roll(k.a[8 * c : 8 * c + 8, :], BIAS - 8 * c, 1)
        flat = acc[0:1]
        for b in range(1, 8):
            flat = flat + pltpu.roll(acc, BIAS - b, 1)[b : b + 1]
        k.goff[h] = flat
        gs = k.gs[...]
        pv = dot(k.p[h], gm * hm)
        pq = dot_l(gs, kp * hm)
        pk = dot(gs, qp * hm)
        tv, tq, tk = (pv, pq, pk) if tv is None else (tv + pv, tq + pq, tk + pk)
    k.q[pr] = (tq.astype(bf16) * 0.125).astype(bf16)
    k.k[pr] = tk.astype(bf16)
    k.v[pr] = tv.astype(bf16)


def gate_back(k):
    weights, _, _, own = gate_weights(k)
    ggate = jnp.concatenate([k.ggate[h] for h in range(HEADS)] + [jnp.zeros((4, PAD), f32)], axis=0)
    first, second, factor = k.first[...], k.second[...], k.factor[...]
    df = ggate * (second * factor - 1.0) * first * (1.0 - first)
    ds = ggate * first * factor * second * (1.0 - second)
    dz = jnp.concatenate([df, ds], axis=0)
    gscale = jnp.sum(ggate * first * second, axis=1, keepdims=True)
    gw = dot(dz, k.tok[...].astype(f32), precision=highest)
    pick = lambda v: jnp.sum(jnp.where(own, v, 0.0), axis=0, keepdims=True)
    k.sg[24:25, 0:D] = pick(gw[0:16])
    k.sg[25:26, 0:D] = pick(gw[16:32])
    k.sg[24:25, D:] = jnp.broadcast_to(jnp.sum(jnp.sum(df, axis=0, keepdims=True), axis=1, keepdims=True), (1, 256))
    k.sg[25:26, D:] = jnp.broadcast_to(jnp.sum(jnp.sum(ds, axis=0, keepdims=True), axis=1, keepdims=True), (1, 256))
    goff = jnp.concatenate([k.goff[h] for h in range(HEADS)] + [jnp.zeros((4, BIAS), f32)], axis=0)
    rel = dot_t(goff, k.hot[...].astype(f32), precision=highest)
    k.sg[12:24, 0:NB] = rel[0:HEADS]
    k.sg[12:24, 512:640] = jnp.broadcast_to(gscale, (16, 128))[0:HEADS]
    for t, src in ((0, k.q), (2, k.v)):
        row = jnp.sum(fold(mixed_all(src).astype(f32)), axis=0, keepdims=True)
        for p in range(4):
            at, lane = (6 + p, D) if t == 0 else (12 + 3 * p, 640)
            k.sg[at : at + 1, lane : lane + 192] = row[:, 192 * p : 192 * p + 192]
    k.fa[...] = dot(dz.T, weights)


def grad_input(k):
    for t, src in ((0, k.q), (1, k.k), (2, k.v)):
        k.fa[...] += dot(mixed_all(src), wide(k.wa, t))


def grad_rows(k, part):
    def go(rows, _):
        k.gtok[rows, :] = (k.fb[rows, :] + k.fa[rows, :]).astype(bf16)
        return 0
    rows_loop(32, go, 0, 256 * part, 256 * part + 256)


def grad_projections(k, part):
    own = lambda ref: jnp.concatenate([ref[3 * part + i] for i in range(3)], axis=1)
    for t, src, right in ((0, k.q, k.tok), (1, k.k, k.tok), (2, k.v, k.tok), (3, k.mixed, k.gb)):
        g = dot_l(own(src), right[...]).astype(bf16).reshape(2, 2, 96, D)
        for i in range(2):
            k.wa[t, 2 * part + i] = g[i]


def each(n, fn, k):
    def go(i, _):
        fn(k, i)
        return 0
    lax.fori_loop(0, n, go, 0)


COMPUTE_SCRATCH = dict(
    row=((1, BIAS), jnp.int32), hot=((NB, BIAS), bf16), tok=((PAD, D), bf16), cot=((PAD, D), bf16), sm=((4, 8, BIAS), f32), mask=((PAD, PAD), f32),
    first=((16, PAD), f32), second=((16, PAD), f32), factor=((16, PAD), f32), gate=((HEADS, 1, PAD), f32),
    bias=((HEADS, 128, 896), bf16), q=((PAIRS, PAD, 128), bf16), k=((PAIRS, PAD, 128), bf16),
    v=((PAIRS, PAD, 128), bf16), s=((PAD, PAD), f32), p=((HEADS, PAD, PAD), bf16), mixed=((PAIRS, PAD, 128), bf16),
    fa=((PAD, D), f32), fb=((PAD, D), f32), n1=((PAD, D), f32), inv1=((PAD, 128), f32), hid=((PAD, D), bf16),
    act=((4, PAD, D), bf16), dg=((4, PAD, D), bf16), out=((PAD, D), bf16), gb=((PAD, D), bf16),
    gm=((PAIRS, PAD, 128), bf16), gs=((PAD, PAD), bf16), a=((128, BIAS), f32), ggate=((HEADS, 1, PAD), f32),
    goff=((HEADS, 1, BIAS), f32), gtok=((PAD, D), bf16), sg=((32, BIAS), f32),
    wa=((4, 4, 2, 96, D), bf16), wi=((4, 8, 96, D), bf16), wo=((4, 8, 96, D), bf16),
)


MESH = pl.DeviceIdType.MESH
BLOCKS = (0, 1, 2)
SEMS = dict(
    wz=(3, 3), w1=(3, 3), w2=(3, 3, 2), w3=(3, 3), sm=(3,), rows=(2, 2, 6), r1=(3, 4), r2=(3, 4, 2), r3=(3, 4),
    r4=(3, 2, 3), a1=(3,), a2=(3, 2), a3=(3,), sg=(6,),
)
COMM_SCRATCH = dict(
    rb1a=((4, 2, 2, 96, D), bf16), rb1=((2, 4, 4, 96, D), bf16), rb2=((3, 4, 2, 96, D), bf16),
    rb3=((3, 4, 96, D), bf16), rb4=((3, 2, 3, 96, D), bf16), sgr=((5, 32, BIAS), f32), sgs=((6, 32, BIAS), f32), fin=((16, BIAS), f32),
)


class Net:
    def __init__(self, k):
        self.k = k
        dp, z = lax.axis_index("dp"), lax.axis_index("tensor")
        self.dp, self.z = dp, z
        c, x, y = dp % 2, (dp // 2) % 2, (dp // 4) % 2
        self.c = c
        across_x, across_y = dp + 2 * (1 - 2 * x), dp + 4 * (1 - 2 * y)
        self.core = (dp + 1 - 2 * c, z)
        self.x, self.y = (across_x, z), (across_y, z)
        self.one = ((1 - c) * across_x + c * across_y, z)
        self.two = (c * across_x + (1 - c) * across_y, z)
        at = lambda cc, yy, xx: 4 * cc + 2 * yy + xx
        ex, ey = at(c, y, 1 - x), at(c, 1 - y, x)
        self.e = at(c, y, x)
        self.e1 = (1 - c) * ex + c * ey
        self.e2 = c * ex + (1 - c) * ey
        self.e12 = at(c, 1 - y, 1 - x)

    def ahead(self, dz):
        return (self.z + dz) % 4

    def behind(self, dz):
        return (self.z + 4 - dz) % 4

    def copy(self, name, index, src, dst, device):
        sems = getattr(self.k, "sem_" + name)
        return pltpu.make_async_remote_copy(
            src_ref=src, dst_ref=dst, send_sem=sems.at[(0, *index)], recv_sem=sems.at[(1, *index)],
            device_id=device, device_id_type=MESH,
        )

    def greet(self):
        barrier = pltpu.get_barrier_semaphore()
        peers = [self.core, self.one, self.two] + [(self.dp, self.ahead(dz)) for dz in (1, 2, 3)]
        for peer in peers:
            pl.semaphore_signal(barrier, inc=1, device_id=peer, device_id_type=MESH)
        pl.semaphore_wait(barrier, len(peers))

    def block(self, b):
        return (self.k.wa, self.k.wi, self.k.wo)[b]

    def chunk(self, b, p, e):
        return self.block(b).at[e // 2, p, e % 2] if b == 0 else self.block(b).at[p, e]

    def side(self, b, p, c):
        return self.block(b).at[pl.ds(2 * c, 2), p] if b == 0 else self.block(b).at[p, pl.ds(4 * c, 4)]

    def wz(self, b, d):
        ref = self.chunk(b, self.z, self.e)
        return self.copy("wz", (b, d - 1), ref, ref, (self.dp, self.ahead(d)))

    def w1(self, b, d):
        ref = self.chunk(b, self.behind(d), self.e)
        return self.copy("w1", (b, d - 1), ref, ref, self.one)

    def w2(self, b, d, i):
        ref = self.chunk(b, self.behind(d), (self.e, self.e1)[i])
        return self.copy("w2", (b, d - 1, i), ref, ref, self.two)

    def w3(self, b, d):
        ref = self.side(b, self.behind(d), self.c)
        return self.copy("w3", (b, d - 1), ref, ref, self.core)

    def sm(self, d):
        ref = self.k.sm.at[self.z]
        return self.copy("sm", (d - 1,), ref, ref, (self.dp, self.ahead(d)))

    def rows(self, a, way, n):
        source, result = ((self.k.out, self.k.out_hbm), (self.k.gtok, self.k.gtok_hbm))[a]
        j, (start, size) = n // 2, PARTS[n % 2]
        slot = self.z - j if way == 0 else self.z + j
        to = self.z + 1 if way == 0 else self.z - 1
        at = result.at[pl.ds(pl.multiple_of(slot * SEQ + start, 16), size)]
        return self.copy("rows", (a, way, n), source.at[pl.ds(start, size)] if j == 0 else at, at, (self.dp, to))

    def sends(self, way, n):
        z, j = self.z, n // 2
        return (z <= 2) & (z >= j) if way == 0 else (z >= 1) & (z + j <= 3)

    def receives(self, way, n):
        z, j = self.z, n // 2
        return z >= 1 + j if way == 0 else z + 1 + j <= 3

    def r1(self, b, p):
        dst = self.k.rb1a.at[p] if b == 0 else self.k.rb1.at[b - 1, p]
        return self.copy("r1", (b, p), self.side(b, p, 1 - self.c), dst, self.core)

    def r2(self, b, p, i):
        return self.copy("r2", (b, p, i), self.chunk(b, p, (self.e1, self.e12)[i]), self.k.rb2.at[b, p, i], self.one)

    def r3(self, b, p):
        return self.copy("r3", (b, p), self.chunk(b, p, self.e2), self.k.rb3.at[b, p], self.two)

    def r4(self, b, way, p):
        to, i = (self.z + 1, p - 1) if way == 0 else (self.z - 1, p)
        return self.copy("r4", (b, way, i), self.chunk(b, p, self.e), self.k.rb4.at[b, way, i], (self.dp, to))

    def result(self, b, e):
        return (self.k.ra, self.k.ri, self.k.ro)[b].at[e]

    def keep(self, b):
        return pltpu.make_async_copy(self.chunk(b, self.z, self.e), self.result(b, self.e), self.k.sem_keep.at[b])

    def a1(self, b):
        return self.copy("a1", (b,), self.chunk(b, self.z, self.e), self.result(b, self.e), self.one)

    def a2(self, b, i):
        src = (self.chunk(b, self.z, self.e), self.result(b, self.e1))[i]
        return self.copy("a2", (b, i), src, self.result(b, (self.e, self.e1)[i]), self.two)

    def a3(self, b):
        ref = self.result(b, pl.ds(4 * self.c, 4))
        return self.copy("a3", (b,), ref, ref, self.core)

    def sg(self, i):
        k, half = self.k, pl.ds(16 * self.c, 16)
        if i < 3:
            return self.copy("sg", (i,), k.sgs.at[i], k.sgr.at[i], (self.core, self.x, self.y)[i])
        if i < 5:
            device = (self.dp, self.flip(1 if i == 3 else 2))
            return self.copy("sg", (i,), k.sgs.at[i, half], k.sgr.at[i, half], device)
        return self.copy("sg", (i,), k.sgs.at[5, half], k.sgs.at[5, half], self.core)

    def flip(self, bit):
        return self.z + bit * (1 - 2 * ((self.z // bit) % 2))


def loop(n, fn):
    def go(i, _):
        fn(i)
        return 0
    lax.fori_loop(0, n, go, 0)


def when(condition, fn):
    @pl.when(condition)
    def _():
        fn()


PIECES = ((0, 1), (0, 2), (0, 3), (1, 1), (2, 1), (1, 2), (2, 2), (1, 3), (2, 3))
WINDOW = 2
PARTS = ((0, 256), (256, 240))
ORDER = (3, 0, 2, 1)


def weight_step(net, t):
    if t < 9:
        b, d = PIECES[t]
        net.wz(b, d).wait_recv()
        net.w1(b, d).start()
        if t + WINDOW < 9:
            net.wz(*PIECES[t + WINDOW]).start()
    if 0 <= t - 1 < 9:
        b, d = PIECES[t - 1]
        net.w1(b, d).wait_recv()
        net.w2(b, d, 0).start()
        net.w2(b, d, 1).start()
    if 0 <= t - 3 < 9:
        b, d = PIECES[t - 3]
        net.w2(b, d, 0).wait_recv()
        net.w2(b, d, 1).wait_recv()
        net.w3(b, d).start()
    if 0 <= t - 4 < 9:
        net.w3(*PIECES[t - 4]).wait_recv()


def weights_sent(net):
    for b, d in PIECES:
        net.wz(b, d).wait_send()
        net.w1(b, d).wait_send()
        net.w2(b, d, 0).wait_send()
        net.w2(b, d, 1).wait_send()
        net.w3(b, d).wait_send()


def rows_own(net, a, part):
    for way in (0, 1):
        when(net.sends(way, part), lambda: net.rows(a, way, part).start())


def rows_next(net, a, way, n):
    when(net.receives(way, n - 1), lambda: net.rows(a, way, n - 1).wait_recv())
    if n + 1 < 6:
        when(net.sends(way, n + 1), lambda: net.rows(a, way, n + 1).start())


def rows_sent(net, a):
    for n in range(6):
        for way in (0, 1):
            when(net.sends(way, n), lambda: net.rows(a, way, n).wait_send())


def add(net, b, p, e, ref):
    k = net.k
    if b == 0:
        k.wa[e // 2, p, e % 2] = k.wa[e // 2, p, e % 2] + ref[...]
    else:
        net.block(b)[p, e] = net.block(b)[p, e] + ref[...]


def halves(net, b, p):
    net.r1(b, p).wait_recv()
    for j in range(4):
        src = net.k.rb1a.at[p, j // 2, j % 2] if b == 0 else net.k.rb1.at[b - 1, p, j]
        add(net, b, p, 4 * net.c + j, src)
    net.r2(b, p, 1).start()
    net.r2(b, p, 0).start()


def quarters(net, b, p):
    net.r2(b, p, 1).wait_recv()
    add(net, b, p, net.e2, net.k.rb2.at[b, p, 1])
    net.r3(b, p).start()
    net.r2(b, p, 0).wait_recv()
    add(net, b, p, net.e, net.k.rb2.at[b, p, 0])


def eighths(net, b, p):
    net.r3(b, p).wait_recv()
    add(net, b, p, net.e, net.k.rb3.at[b, p])
    if p > 0:
        when(net.z == 0, lambda: net.r4(b, 0, p).start())
    if p < 3:
        when(net.z == 3, lambda: net.r4(b, 1, p).start())


def chain(net, b, p):
    def link(way, i):
        net.r4(b, way, p).wait_recv()
        add(net, b, p, net.e, net.k.rb4.at[b, way, i])
        net.r4(b, way, p).start()
    if p > 1:
        when((net.z > 0) & (net.z < p), lambda: link(0, p - 1))
    if p < 2:
        when((net.z > p) & (net.z < 3), lambda: link(1, p))


def over_z(net, b):
    k, z = net.k, net.z
    def last(way, i):
        net.r4(b, way, z).wait_recv()
        add(net, b, z, net.e, k.rb4.at[b, way, i])
    when(z > 0, lambda: last(0, z - 1))
    when(z < 3, lambda: last(1, z))
    net.keep(b).start()
    net.a1(b).start()
    net.a2(b, 0).start()


def around(net, b):
    net.a1(b).wait_recv()
    net.a2(b, 1).start()


def to_core(net, b):
    net.keep(b).wait()
    net.a2(b, 0).wait_recv()
    net.a2(b, 1).wait_recv()
    net.a3(b).start()


def gradients_sent(net, b):
    net.a3(b).wait_recv()
    for p in range(4):
        net.r1(b, p).wait_send()
        net.r2(b, p, 0).wait_send()
        net.r2(b, p, 1).wait_send()
        net.r3(b, p).wait_send()
    for p in range(4):
        when(net.z < p, lambda: net.r4(b, 0, p).wait_send())
        when(net.z > p, lambda: net.r4(b, 1, p).wait_send())
    net.a1(b).wait_send()
    net.a2(b, 0).wait_send()
    net.a2(b, 1).wait_send()
    net.a3(b).wait_send()


def halves_out(net, b, p):
    net.r1(b, p).start()


def small_step(net, i):
    k, half = net.k, pl.ds(16 * net.c, 16)
    if i == 0:
        k.sgs[0] = k.sg[...]
    else:
        net.sg(i - 1).wait_recv()
    if 0 < i < 4:
        k.sgs[i] = k.sgs[i - 1] + k.sgr[i - 1]
    elif 3 < i < 6:
        k.sgs[i, half, :] = k.sgs[i - 1, half, :] + k.sgr[i - 1, half, :]
    if i < 6:
        net.sg(i).start()


STEPS = dict(
    rows_own=rows_own, rows_next=rows_next, halves_out=halves_out, halves=halves, quarters=quarters, eighths=eighths,
    chain=chain, over_z=over_z, around=around, to_core=to_core, small=small_step,
)
PLAN = {
    "n2a": [
        ("rows_own", 0, 0),
    ],
    "n2b": [
        ("rows_own", 0, 1),
    ],
    "fb0": [
        ("halves_out", 1, 3),
    ],
    "fb1": [
        ("halves_out", 2, 0), ("rows_next", 0, 0, 1), ("halves", 1, 3), ("halves_out", 1, 0),
    ],
    "fb2": [
        ("halves_out", 2, 2), ("halves", 2, 0), ("rows_next", 0, 1, 1), ("halves_out", 2, 3),
    ],
    "fb3": [
        ("halves_out", 1, 1), ("rows_next", 0, 1, 2), ("halves", 2, 2), ("halves", 1, 0), ("halves_out", 1, 2),
        ("halves_out", 2, 1), ("rows_next", 0, 0, 2), ("quarters", 2, 0),
    ],
    "ab0": [
        ("quarters", 2, 2), ("rows_next", 0, 1, 3), ("halves", 2, 3),
    ],
    "ab2": [
        ("halves", 1, 1), ("rows_next", 0, 0, 3), ("eighths", 2, 2), ("halves", 1, 2),
    ],
    "gateb": [
        ("chain", 2, 2),
    ],
    "gin": [
        ("rows_own", 1, 0), ("quarters", 2, 3), ("quarters", 1, 0),
    ],
    "gin2": [
        ("rows_next", 0, 1, 4), ("quarters", 1, 2),
    ],
    "gp0": [
        ("halves_out", 0, 0), ("eighths", 2, 0), ("halves_out", 0, 1), ("halves", 2, 1), ("quarters", 1, 3),
        ("small", 0), ("quarters", 1, 1), ("rows_own", 1, 1),
    ],
    "gp1": [
        ("halves_out", 0, 2), ("halves", 0, 1), ("halves_out", 0, 3), ("rows_next", 1, 0, 1), ("eighths", 1, 2),
        ("eighths", 1, 0), ("quarters", 2, 1), ("halves", 0, 3), ("rows_next", 1, 1, 1), ("rows_next", 1, 0, 2),
        ("halves", 0, 0), ("small", 1), ("eighths", 2, 1), ("quarters", 0, 3), ("quarters", 0, 1), ("eighths", 1, 1),
        ("halves", 0, 2), ("rows_next", 0, 1, 5), ("rows_next", 0, 1, 6), ("chain", 2, 0), ("chain", 1, 2),
        ("eighths", 2, 3), ("quarters", 0, 0), ("rows_next", 0, 0, 4), ("chain", 1, 0), ("eighths", 0, 3),
        ("small", 2), ("chain", 2, 1), ("eighths", 1, 3), ("rows_next", 1, 1, 2), ("eighths", 0, 1), ("chain", 2, 3),
        ("rows_next", 1, 1, 3), ("quarters", 0, 2), ("eighths", 0, 0), ("over_z", 2), ("chain", 1, 1),
        ("chain", 0, 3), ("chain", 0, 1), ("chain", 1, 3), ("eighths", 0, 2), ("around", 2), ("chain", 0, 2),
        ("over_z", 1), ("rows_next", 1, 0, 3), ("chain", 0, 0), ("small", 3), ("to_core", 2), ("around", 1),
        ("over_z", 0), ("small", 4), ("to_core", 1), ("rows_next", 1, 1, 4), ("rows_next", 1, 1, 5), ("around", 0),
        ("rows_next", 0, 0, 5), ("rows_next", 1, 0, 4), ("rows_next", 1, 0, 5), ("small", 5), ("to_core", 0),
        ("rows_next", 1, 1, 6), ("small", 6), ("rows_next", 1, 0, 6), ("rows_next", 0, 0, 6),
    ],
}


def kernel(names, *refs):
    k = K()
    for name, ref in zip(names, refs):
        setattr(k, name, ref)
    net = Net(k)
    z = net.z
    own_rows = pl.ds(pl.multiple_of(z * SEQ, 16), SEQ)
    moves = [
        (k.wq_hbm, k.wa.at[0, z]), (k.wk_hbm, k.wa.at[1, z]), (k.wv_hbm, k.wa.at[2, z]), (k.wout_hbm, k.wa.at[3, z]),
        (k.wi_hbm, k.wi.at[z]), (k.wo_hbm, k.wo.at[z]),
        (k.tok_hbm.at[own_rows], k.tok.at[pl.ds(0, SEQ)]), (k.cot_hbm.at[own_rows], k.cot.at[pl.ds(0, SEQ)]),
    ]
    local = [pltpu.make_async_copy(src, dst, k.sem_in.at[i]) for i, (src, dst) in enumerate(moves)]
    for c in local:
        c.start()
    net.greet()
    for c in local[0:4]:
        c.wait()
    for piece in PIECES[0:WINDOW]:
        net.wz(*piece).start()
    k.tok[SEQ:PAD] = jnp.zeros((PAD - SEQ, D), bf16)
    k.cot[SEQ:PAD] = jnp.zeros((PAD - SEQ, D), bf16)
    k.sg[...] = jnp.zeros((32, BIAS), f32)
    k.factor[...] = jnp.zeros((16, PAD), f32)
    own_small(k, z)
    for d in (1, 2, 3):
        net.sm(d).start()
    for c in local[4:8]:
        c.wait()
    weight_step(net, 0)
    mask_build(k, z)
    weight_step(net, 1)
    for d in (1, 2, 3):
        net.sm(d).wait_recv()
    gates(k)
    weight_step(net, 2)
    bias_tables(k)
    weight_step(net, 3)
    weight_step(net, 4)
    weight_step(net, 5)
    weight_step(net, 6)
    project(k)

    def forward(pr):
        attend(k, pr)
        when(pr == 1, lambda: weight_step(net, 7))
        when(pr == 4, lambda: weight_step(net, 8))
    loop(PAIRS, forward)
    norm_one(k)
    weight_step(net, 9)
    feed_init(k)

    def layer_two(i):
        when(i == 2, lambda: weight_step(net, 10))
        when(i == 3, lambda: (weight_step(net, 11), weight_step(net, 12)))
        feed(k, net.behind(i))
    loop(4, layer_two)
    here = [
        pltpu.make_async_copy(k.out.at[pl.ds(0, SEQ)], k.out_hbm.at[own_rows], k.sem_in.at[0]),
        pltpu.make_async_copy(k.gtok.at[pl.ds(0, SEQ)], k.gtok_hbm.at[own_rows], k.sem_in.at[1]),
    ]
    run = lambda key: [STEPS[name](net, *given) for name, *given in PLAN.get(key, ())]
    norm_two(k, 0)
    run("n2a")
    norm_two(k, 1)
    run("n2b")
    here[0].start()
    weights_sent(net)

    def layer_two_back(i):
        feed_back(k, (1 - i % 2) * (3 - i // 2) + (i % 2) * (i // 2))
        for n in range(4):
            when(i == n, lambda: run("fb" + str(n)))
    loop(4, layer_two_back)
    norm_one_back(k)
    run("n1b")

    def backward(pr):
        attend_back(k, pr)
        for n in range(PAIRS):
            when(pr == n, lambda: run("ab" + str(n)))
    loop(PAIRS, backward)
    gate_back(k)
    run("gateb")
    grad_input(k)
    grad_rows(k, 0)
    run("gin")
    grad_rows(k, 1)
    here[1].start()
    run("gin2")
    for part in (0, 1):
        grad_projections(k, part)
        run("gp" + str(part))
    k.fin[...] = jnp.zeros((16, BIAS), f32)
    k.fin[0:6, :] = k.sgs[5, 0:6, :]
    k.fin[6:7, :] = k.sgs[5, pl.ds(6 + z, 1), :]
    for i in range(3):
        k.fin[8 + i : 9 + i, :] = k.sgs[5, pl.ds(12 + 3 * z + i, 1), :]
    k.fin[11:13, :] = k.sgs[5, 24:26, :]
    finish = pltpu.make_async_copy(k.fin, k.sg_hbm, k.sem_in.at[2])
    finish.start()
    for b in (2, 1, 0):
        gradients_sent(net, b)
    for i in range(6):
        net.sg(i).wait_send()
    for d in (1, 2, 3):
        net.sm(d).wait_send()
    for a in (0, 1):
        rows_sent(net, a)
    here[0].wait()
    here[1].wait()
    finish.wait()


def finish_kernel(out, gtok, ra, ri, ro, sg, *rest):
    names = FINAL + ("stage", "wide", "rows", "sem")
    k = K()
    for name, ref in zip(names, rest):
        setattr(k, name, ref)
    inward = [pltpu.make_async_copy(src, k.stage.at[i], k.sem.at[2 + i]) for i, src in enumerate((ri, ro, ra))]
    for c in inward:
        c.start()
    pairs = [(out, k.rows.at[0], k.output), (gtok, k.rows.at[1], k.grad_tokens)]
    copies = [pltpu.make_async_copy(src, via, k.sem.at[i]) for i, (src, via, _) in enumerate(pairs)]
    for c in copies:
        c.start()
    row = lambda r, lane, n: sg[r : r + 1, lane : lane + n].reshape(n)
    k.b_out[...], k.norm1_gain[...], k.norm1_bias[...] = row(0, 0, D), row(1, 0, D), row(2, 0, D)
    k.b_outer[...], k.norm2_gain[...], k.norm2_bias[...] = row(3, 0, D), row(4, 0, D), row(5, 0, D)
    k.b_inner[...], k.b_query[...], k.b_value[...] = row(6, 0, D), row(6, D, 192), row(8, 640, 192)
    k.rel_table[...] = sg[8:11, 0:NB]
    lane = lax.broadcasted_iota(jnp.int32, (1, 128), 1)
    cell = lambda r, at: sg[r : r + 1, at : at + 128]
    k.gate_scale[...] = jnp.where(lane == 0, cell(8, 512), jnp.where(lane == 1, cell(9, 512), cell(10, 512)))[:, 0:3]
    k.gate_bias[...] = jnp.where(lane < 4, cell(11, D), cell(12, D))[:, 0:8]
    for i in (0, 1):
        heads = cell(11 + i, 0)
        for pr in range(1, PAIRS):
            heads = heads + cell(11 + i, 128 * pr)
        k.gate_weight[4 * i : 4 * i + 4, :] = jnp.broadcast_to(heads[:, 0:HEAD] + heads[:, HEAD:128], (4, HEAD))
    outward = []
    for i, c in enumerate(inward):
        c.wait()
        def widen(j):
            k.wide[i, j] = k.stage[i, j].astype(f32)
        loop(8, widen)
        if i < 2:
            to = [(k.wide.at[i], (k.w_inner, k.w_outer)[i])]
        else:
            to = [(k.wide.at[i, pl.ds(2 * j, 2)], ref) for j, ref in enumerate((k.w_query, k.w_key, k.w_value, k.w_out))]
        for src, dst in to:
            copy = pltpu.make_async_copy(src, dst, k.sem.at[5 + len(outward)])
            copy.start()
            outward.append(copy)
    for i, (c, (_, via, dst)) in enumerate(zip(copies, pairs)):
        c.wait()
        outward.append(pltpu.make_async_copy(via, dst, k.sem.at[i]))
        outward[-1].start()
    for c in outward:
        c.wait()


FINAL = (
    "output", "grad_tokens", "w_query", "w_key", "w_value", "w_out", "w_inner", "w_outer", "b_query", "b_value", "b_out",
    "gate_weight", "gate_bias", "gate_scale", "rel_table", "norm1_gain", "norm1_bias", "b_inner", "b_outer", "norm2_gain",
    "norm2_bias",
)


def body(
    tokens, slot_kind, offset_bucket, w_query, b_query, w_key, w_value, b_value, w_out, b_out, gate_weight, gate_bias,
    gate_scale, rel_table, norm1_gain, norm1_bias, w_inner, b_inner, w_outer, b_outer, norm2_gain, norm2_bias, cotangent,
):
    n_dp = lax.axis_size("dp")
    rows = tokens.shape[0]
    shape = jax.ShapeDtypeStruct
    anywhere = pl.BlockSpec(memory_space=pl.ANY)
    vmem = pl.BlockSpec(memory_space=pltpu.VMEM)
    smem = pl.BlockSpec(memory_space=pltpu.SMEM)
    given = dict(
        kinds=(smem, slot_kind), bucket=(vmem, offset_bucket.reshape(1, OFFSETS)), rel=(vmem, rel_table.T),
        b_query=(vmem, b_query), b_value=(vmem, b_value), b_inner=(vmem, b_inner), scale=(vmem, gate_scale.reshape(1, 3)),
        gw=(vmem, gate_weight.T), gate_bias=(vmem, gate_bias), b_out=(vmem, b_out), b_outer=(vmem, b_outer),
        norm1_gain=(vmem, norm1_gain), norm1_bias=(vmem, norm1_bias), norm2_gain=(vmem, norm2_gain),
        norm2_bias=(vmem, norm2_bias), tok_hbm=(anywhere, tokens), cot_hbm=(anywhere, cotangent),
        wq_hbm=(anywhere, w_query.T.reshape(2, 96, D)), wk_hbm=(anywhere, w_key.T.reshape(2, 96, D)),
        wv_hbm=(anywhere, w_value.T.reshape(2, 96, D)), wout_hbm=(anywhere, w_out.reshape(2, 96, D)),
        wi_hbm=(anywhere, w_inner.reshape(8, 96, D)), wo_hbm=(anywhere, w_outer.reshape(8, 96, D)),
    )
    names = list(given) + ["out_hbm", "gtok_hbm", "ra", "ri", "ro", "sg_hbm"]
    scratch = []
    for name, (dims, dtype) in (COMPUTE_SCRATCH | COMM_SCRATCH).items():
        names.append(name)
        scratch.append(pltpu.VMEM(dims, dtype))
    for name, dims in SEMS.items():
        names.append("sem_" + name)
        scratch.append(pltpu.SemaphoreType.DMA((2, *dims)))
    for name, count in (("sem_in", 8), ("sem_keep", 3)):
        names.append(name)
        scratch.append(pltpu.SemaphoreType.DMA((count,)))
    whole = shape((8, 96, D), bf16)
    out, gtok, ra, ri, ro, sg = pl.pallas_call(
        functools.partial(kernel, names),
        in_specs=[spec for spec, _ in given.values()],
        out_specs=[anywhere] * 6,
        out_shape=[shape((rows, D), bf16), shape((rows, D), bf16), whole, whole, whole, shape((16, BIAS), f32)],
        scratch_shapes=scratch,
        compiler_params=pltpu.CompilerParams(collective_id=0, has_side_effects=True, vmem_limit_bytes=VMEM_LIMIT),
    )(*[value for _, value in given.values()])
    if n_dp > 8:
        groups = [list(range(g, n_dp, 8)) for g in range(8)]
        ra, ri, ro, sg = lax.psum((ra.astype(f32), ri.astype(f32), ro.astype(f32), sg), "dp", axis_index_groups=groups)
        ra, ri, ro = ra.astype(bf16), ri.astype(bf16), ro.astype(bf16)
    vector = shape((D,), f32)
    part = shape((2, 96, D), f32)
    final = dict(
        output=(anywhere, shape((rows, D), bf16)), grad_tokens=(anywhere, shape((rows, D), bf16)),
        w_query=(anywhere, part), w_key=(anywhere, part), w_value=(anywhere, part), w_out=(anywhere, part),
        w_inner=(anywhere, shape((8, 96, D), f32)), w_outer=(anywhere, shape((8, 96, D), f32)),
        b_query=(vmem, shape((192,), f32)), b_value=(vmem, shape((192,), f32)), gate_weight=(vmem, shape((8, HEAD), f32)),
        gate_bias=(vmem, shape((1, 8), f32)), gate_scale=(vmem, shape((1, 3), f32)), rel_table=(vmem, shape((3, NB), f32)),
    )
    specs, shapes = zip(*[final.get(name, (vmem, vector)) for name in FINAL])
    results = pl.pallas_call(
        finish_kernel,
        in_specs=[anywhere] * 5 + [vmem],
        out_specs=list(specs),
        out_shape=list(shapes),
        scratch_shapes=[pltpu.VMEM((3, 8, 96, D), bf16), pltpu.VMEM((3, 8, 96, D), f32), pltpu.VMEM((2, rows, D), bf16), pltpu.SemaphoreType.DMA((11,))],
        compiler_params=pltpu.CompilerParams(vmem_limit_bytes=VMEM_LIMIT),
    )(out, gtok, ra, ri, ro, sg)
    r = dict(zip(FINAL, results))
    for name in ("w_query", "w_key", "w_value"):
        r[name] = r[name].reshape(192, D).T
    r["w_out"] = r["w_out"].reshape(192, D)
    r["w_inner"] = r["w_inner"].reshape(D, D)
    r["w_outer"] = r["w_outer"].reshape(D, D)
    r["gate_weight"] = r["gate_weight"].T
    r["gate_bias"] = r["gate_bias"].reshape(8)
    r["gate_scale"] = r["gate_scale"].reshape(3)
    r["rel_table"] = r["rel_table"].T
    order = (
        "output", "grad_tokens", "w_query", "b_query", "w_key", "w_value", "b_value", "w_out", "b_out", "gate_weight",
        "gate_bias", "gate_scale", "rel_table", "norm1_gain", "norm1_bias", "w_inner", "b_inner", "w_outer", "b_outer",
        "norm2_gain", "norm2_bias",
    )
    return tuple(r[name] for name in order)


def solution(mesh):
    in_specs = (
        P("dp", None),
        P("dp"),
        P(),
        P(None, "tensor"),
        P("tensor"),
        P(None, "tensor"),
        P(None, "tensor"),
        P("tensor"),
        P("tensor", None),
        P(),
        P(),
        P(),
        P("tensor"),
        P(None, "tensor"),
        P(),
        P(),
        P(None, "tensor"),
        P("tensor"),
        P("tensor", None),
        P(),
        P(),
        P(),
        P("dp", None),
    )
    out_specs = (
        P("dp", None),
        P("dp", None),
        P(None, "tensor"),
        P("tensor"),
        P(None, "tensor"),
        P(None, "tensor"),
        P("tensor"),
        P("tensor", None),
        P(),
        P(),
        P(),
        P("tensor"),
        P(None, "tensor"),
        P(),
        P(),
        P(None, "tensor"),
        P("tensor"),
        P("tensor", None),
        P(),
        P(),
        P(),
    )
    return jax.shard_map(body, mesh=mesh, in_specs=in_specs, out_specs=out_specs, check_vma=False)
```

```python
import functools
import math

import jax
import jax.numpy as jnp
from jax import lax
from jax.experimental import pallas as pl
from jax.experimental.pallas import tpu as pltpu
from jax.sharding import PartitionSpec as P

HEAD = 64
SEQ = 496
PAD = 512
D = 768
PAIRS = 6
HEADS = 12
BIAS = 1024
NB = 320
VMEM_LIMIT = 64 * 2**20 - 2**16
OFFSETS = 991
HALF = SEQ // 2
PARTS = ((0, 128), (128, 320), (320, PAD))
f32 = jnp.float32
bf16 = jnp.bfloat16
residual_scale = 24.0**0.25
norm_epsilon = 1e-05
highest = lax.Precision.HIGHEST


def dot(a, b, precision=None):
    return lax.dot_general(a, b, (((1,), (0,)), ((), ())), preferred_element_type=f32, precision=precision)


def dot_t(a, b, precision=None):
    return lax.dot_general(a, b, (((1,), (1,)), ((), ())), preferred_element_type=f32, precision=precision)


def dot_l(a, b):
    return lax.dot_general(a, b, (((0,), (0,)), ((), ())), preferred_element_type=f32)


def fold(x):
    return jnp.sum(x.reshape(x.shape[0] // 8, 8, x.shape[1]), axis=0)


def stats(r):
    c = r - jnp.mean(r, -1, keepdims=True)
    inv = lax.rsqrt(jnp.mean(c * c, -1, keepdims=True) + norm_epsilon)
    return c * inv, inv


def norm_back(g, n, inv):
    return inv * (g - jnp.mean(g, -1, keepdims=True) - n * jnp.mean(g * n, -1, keepdims=True))


def wide(ref, i):
    return ref[i].reshape(D, D)


def rows_loop(step, body, carry, first=0, last=PAD):
    def go(c, carry):
        return body(pl.ds(pl.multiple_of(c * step, step), step), carry)
    return lax.fori_loop(first // step, last // step, go, carry)


class K:
    pass


def head_mask(hh):
    lane = lax.broadcasted_iota(jnp.int32, (1, 128), 1)
    return jnp.where((lane // HEAD) == hh, 1.0, 0.0).astype(bf16)


def line(ref):
    return ref[...].astype(f32).reshape(1, ref.shape[0])


def one_hot(k):
    k.row[...] = jnp.full((1, BIAS), -1, jnp.int32)
    k.row[:, 0:OFFSETS] = k.bucket[...]
    hot = jnp.where(lax.broadcasted_iota(jnp.int32, (NB, BIAS), 0) == k.row[...], 1.0, 0.0).astype(bf16)
    for n in range(4):
        m = lax.broadcasted_iota(jnp.int32, (BIAS, 256), 0) + lax.broadcasted_iota(jnp.int32, (BIAS, 256), 1) + 256 * n
        turn = jnp.where((m == 879) | (m == 1903), 1.0, 0.0).astype(bf16)
        k.hot[:, 256 * n : 256 * n + 256] = dot(hot, turn).astype(bf16)


def own_small(k, z):
    one_hot(k)
    k.sm[z, 0:3, :] = dot(k.rel[...], k.hot[...])
    k.sm[z, 3:4, 0:192] = line(k.b_query)
    k.sm[z, 3:4, 192:384] = line(k.b_value)
    k.sm[z, 4:5, 0:D] = line(k.b_inner)
    for i in range(3):
        k.sm[z, 5 + i : 6 + i, :] = jnp.broadcast_to(k.scale[:, i : i + 1].astype(f32), (1, BIAS))


def mask_build(k, z):
    kind = k.kinds[z].astype(f32)
    def go(rows, _):
        j = lax.broadcasted_iota(jnp.int32, (32, PAD), 0) + rows.start
        i = lax.broadcasted_iota(jnp.int32, (32, PAD), 1)
        far = jnp.where(j < HALF, 0, 1) != jnp.where(i < HALF, 0, 1)
        k.mask[rows, :] = jnp.where(j < SEQ, 0.0, -1e30) + jnp.where(far, -1e30, 0.0) * kind
        return 0
    rows_loop(32, go, 0)


def gate_weights(k):
    gw = k.gw[...].astype(f32)
    tile = lambda v: jnp.concatenate([jnp.concatenate([v, v], axis=1)] * PAIRS, axis=1)
    first = tile(jnp.sum(gw[0:4], axis=0, keepdims=True))
    second = tile(jnp.sum(gw[4:8], axis=0, keepdims=True))
    bias = line(k.gate_bias)
    own = (lax.broadcasted_iota(jnp.int32, (16, D), 1) // HEAD) == lax.broadcasted_iota(jnp.int32, (16, D), 0)
    both = jnp.concatenate([jnp.where(own, first, 0.0), jnp.where(own, second, 0.0)], axis=0)
    add = lambda v: jnp.sum(v, axis=1, keepdims=True)
    return both, add(bias[:, 0:4]), add(bias[:, 4:8]), own


def gates(k):
    weights, first_bias, second_bias, _ = gate_weights(k)
    logits = dot_t(weights, k.tok[...].astype(f32), precision=highest)
    first = jax.nn.sigmoid(logits[0:16] + first_bias)
    second = jax.nn.sigmoid(logits[16:32] + second_bias)
    k.first[...] = first
    k.second[...] = second
    for h in range(HEADS):
        k.factor[h : h + 1, :] = k.sm[h // 3, 5 + h % 3 : 6 + h % 3, 0:PAD]
    value = first * (second * k.factor[...] - 1.0) + 2.0
    for h in range(HEADS):
        k.gate[h] = value[h : h + 1, :]


def bias_tables(k):
    def go(p, _):
        for i in range(3):
            row = jnp.broadcast_to(k.sm[p, i : i + 1, :], (128, BIAS))
            k.bias[p * 3 + i] = pltpu.roll(row, 0, 1, stride=1, stride_axis=0)[:, 0:896].astype(bf16)
        return 0
    lax.fori_loop(0, 4, go, 0)


def small_row(k, row, start):
    return jnp.concatenate([k.sm[p, row : row + 1, start : start + 192] for p in range(4)], axis=1)


def project(k):
    bq = small_row(k, 3, 0)
    bv = small_row(k, 3, 192)
    for t, dest, bias, scale in ((0, k.q, bq, 0.125), (1, k.k, None, None), (2, k.v, bv, None)):
        r = dot_t(k.tok[...], wide(k.wa, t))
        if bias is not None:
            r = r + bias
        if scale is not None:
            r = r * scale
        r = r.astype(bf16)
        for pr in range(PAIRS):
            dest[pr] = r[:, 128 * pr : 128 * pr + 128]


def attend(k, pr):
    qp, kp, vp = k.q[pr], k.k[pr], k.v[pr]
    total = None
    for hh in range(2):
        h = pr * 2 + hh
        hm = head_mask(hh)
        km = kp * hm
        gate = k.gate[h]
        m8 = jnp.full((8, PAD), -3e38, f32)
        for c in range(4):
            s = dot_t(km[128 * c : 128 * c + 128], qp)
            k.s[128 * c : 128 * c + 128, :] = s
        for c in range(16):
            rows = slice(32 * c, 32 * c + 32)
            lane = 384 - 128 * (c // 4)
            t = k.bias[h, 32 * (c % 4) : 32 * (c % 4) + 32, lane : lane + PAD].astype(f32)
            s = k.s[rows, :] + t * gate + k.mask[rows, :]
            k.s[rows, :] = s
            m8 = jnp.maximum(m8, jnp.max(s.reshape(4, 8, PAD), axis=0))
        m = jnp.max(m8, axis=0, keepdims=True)
        l8 = jnp.zeros((8, PAD), f32)
        for c in range(16):
            rows = slice(32 * c, 32 * c + 32)
            e = jnp.exp(k.s[rows, :] - m)
            k.s[rows, :] = e
            l8 = l8 + fold(e)
        inv = 1.0 / jnp.sum(l8, axis=0, keepdims=True)
        for c in range(16):
            rows = slice(32 * c, 32 * c + 32)
            k.p[h, rows, :] = (k.s[rows, :] * inv).astype(bf16)
        part = dot_l(k.p[h], vp * hm)
        total = part if total is None else total + part
    k.mixed[pr] = total.astype(bf16)


def mixed_all(ref):
    return jnp.concatenate([ref[pr] for pr in range(PAIRS)], axis=1)


def norm_one(k):
    k.fa[...] = dot(mixed_all(k.mixed), wide(k.wa, 3))
    b_out, gain, shift = line(k.b_out), line(k.norm1_gain), line(k.norm1_bias)
    def go(rows, _):
        r = residual_scale * k.tok[rows, :].astype(f32) + k.fa[rows, :] + b_out
        n, inv = stats(r)
        k.n1[rows, :] = n
        k.inv1[rows, :] = jnp.broadcast_to(inv, (32, 128))
        k.hid[rows, :] = (n * gain + shift).astype(bf16)
        return 0
    rows_loop(32, go, 0)


def feed_in(k, p):
    k.fa[...] = dot(k.hid[...], wide(k.wi, p))
    b = k.sm[p, 4:5, 0:D]
    def go(rows, _):
        x = k.fa[rows, :] + b
        half = 0.5 * (1.0 + lax.erf(x * (1.0 / math.sqrt(2.0))))
        k.act[p, rows, :] = (x * half).astype(bf16)
        k.dg[p, rows, :] = (half + x * (jnp.exp(-0.5 * x * x) * (1.0 / math.sqrt(2.0 * math.pi)))).astype(bf16)
        return 0
    rows_loop(16, go, 0)


def feed_out(k, p, first=0, last=PAD):
    k.fb[first:last, :] += dot(k.act[p, first:last, :], wide(k.wo, p))


def norm_two(k, part):
    b_outer, gain1, shift1 = line(k.b_outer), line(k.norm1_gain), line(k.norm1_bias)
    gain2, shift2 = line(k.norm2_gain), line(k.norm2_bias)
    def go(rows, carry):
        g_gain, g_shift, g_b = carry
        r = residual_scale * (k.n1[rows, :] * gain1 + shift1) + k.fb[rows, :] + b_outer
        n, inv = stats(r)
        k.out[rows, :] = (n * gain2 + shift2).astype(bf16)
        up = k.cot[rows, :].astype(f32)
        g2 = norm_back(up * gain2, n, inv)
        low = g2.astype(bf16)
        k.gb[rows, :] = low
        k.fb[rows, :] = residual_scale * g2
        return g_gain + fold(up * n), g_shift + fold(up), g_b + fold(low.astype(f32))
    zero = jnp.zeros((8, D), f32)
    g_gain, g_shift, g_b = rows_loop(32, go, (zero, zero, zero), *PARTS[part])
    for row, v in ((3, g_b), (4, g_gain), (5, g_shift)):
        k.sg[row : row + 1, 0:D] += jnp.sum(v, axis=0, keepdims=True)


def feed_back(k, p):
    k.fa[...] = dot_t(k.gb[...], wide(k.wo, p))
    def go(rows, acc):
        gi = (k.fa[rows, :] * k.dg[p, rows, :].astype(f32)).astype(bf16)
        k.dg[p, rows, :] = gi
        return acc + fold(gi.astype(f32))
    acc = rows_loop(32, go, jnp.zeros((8, D), f32))
    k.sg[pl.ds(6 + p, 1), 0:D] = jnp.sum(acc, axis=0, keepdims=True)
    k.fb[...] += dot_t(k.dg[p], wide(k.wi, p))
    k.wo[p] = dot_l(k.act[p], k.gb[...]).astype(bf16).reshape(8, 96, D)
    k.wi[p] = dot_l(k.hid[...], k.dg[p]).astype(bf16).reshape(8, 96, D)


def norm_one_back(k):
    gain = line(k.norm1_gain)
    def go(rows, carry):
        g_gain, g_shift, g_b = carry
        gh = k.fb[rows, :]
        n = k.n1[rows, :]
        g1 = norm_back(gh * gain, n, k.inv1[rows, 0:1])
        low = g1.astype(bf16)
        k.gb[rows, :] = low
        k.fb[rows, :] = residual_scale * g1
        return g_gain + fold(gh * n), g_shift + fold(gh), g_b + fold(low.astype(f32))
    zero = jnp.zeros((8, D), f32)
    g_gain, g_shift, g_b = rows_loop(32, go, (zero, zero, zero))
    for row, v in ((0, g_b), (1, g_gain), (2, g_shift)):
        k.sg[row : row + 1, 0:D] = jnp.sum(v, axis=0, keepdims=True)
    k.hid[...] = dot_t(k.gb[...], wide(k.wa, 3)).astype(bf16)


def attend_back(k, pr):
    qp, kp, vp = k.q[pr], k.k[pr], k.v[pr]
    gm = k.hid[:, pl.ds(pl.multiple_of(128 * pr, 128), 128)]
    tq = tk = tv = None
    for hh in range(2):
        h = pr * 2 + hh
        hm = head_mask(hh)
        vm = vp * hm
        gate = k.gate[h]
        for c in range(4):
            k.s[128 * c : 128 * c + 128, :] = dot_t(vm[128 * c : 128 * c + 128], gm)
        d8 = jnp.zeros((8, PAD), f32)
        for c in range(16):
            rows = slice(32 * c, 32 * c + 32)
            d8 = d8 + fold(k.s[rows, :] * k.p[h, rows, :].astype(f32))
        total = jnp.sum(d8, axis=0, keepdims=True)
        gg = jnp.zeros((8, PAD), f32)
        k.a[...] = jnp.zeros((128, BIAS), f32)
        for c in range(16):
            rows = slice(32 * c, 32 * c + 32)
            part = slice(32 * (c % 4), 32 * (c % 4) + 32)
            lane = 384 - 128 * (c // 4)
            low = (k.p[h, rows, :].astype(f32) * (k.s[rows, :] - total)).astype(bf16)
            k.gs[rows, :] = low
            g = low.astype(f32)
            gg = gg + fold(g * k.bias[h, part, lane : lane + PAD].astype(f32))
            k.a[part, lane : lane + PAD] += g * gate
        k.ggate[h] = jnp.sum(gg, axis=0, keepdims=True)
        acc = k.a[0:8, :]
        for c in range(1, 16):
            acc = acc + pltpu.roll(k.a[8 * c : 8 * c + 8, :], BIAS - 8 * c, 1)
        flat = acc[0:1]
        for b in range(1, 8):
            flat = flat + pltpu.roll(acc, BIAS - b, 1)[b : b + 1]
        k.goff[h] = flat
        gs = k.gs[...]
        pv = dot(k.p[h], gm * hm)
        pq = dot_l(gs, kp * hm)
        pk = dot(gs, qp * hm)
        tv, tq, tk = (pv, pq, pk) if tv is None else (tv + pv, tq + pq, tk + pk)
    k.q[pr] = (tq.astype(bf16) * 0.125).astype(bf16)
    k.k[pr] = tk.astype(bf16)
    k.v[pr] = tv.astype(bf16)


def gate_back(k):
    weights, _, _, own = gate_weights(k)
    ggate = jnp.concatenate([k.ggate[h] for h in range(HEADS)] + [jnp.zeros((4, PAD), f32)], axis=0)
    first, second, factor = k.first[...], k.second[...], k.factor[...]
    df = ggate * (second * factor - 1.0) * first * (1.0 - first)
    ds = ggate * first * factor * second * (1.0 - second)
    dz = jnp.concatenate([df, ds], axis=0)
    gscale = jnp.sum(ggate * first * second, axis=1, keepdims=True)
    gw = dot(dz, k.tok[...].astype(f32), precision=highest)
    pick = lambda v: jnp.sum(jnp.where(own, v, 0.0), axis=0, keepdims=True)
    k.sg[24:25, 0:D] = pick(gw[0:16])
    k.sg[25:26, 0:D] = pick(gw[16:32])
    k.sg[24:25, D:] = jnp.broadcast_to(jnp.sum(jnp.sum(df, axis=0, keepdims=True), axis=1, keepdims=True), (1, 256))
    k.sg[25:26, D:] = jnp.broadcast_to(jnp.sum(jnp.sum(ds, axis=0, keepdims=True), axis=1, keepdims=True), (1, 256))
    goff = jnp.concatenate([k.goff[h] for h in range(HEADS)] + [jnp.zeros((4, BIAS), f32)], axis=0)
    rel = dot_t(goff, k.hot[...].astype(f32), precision=highest)
    k.sg[12:24, 0:NB] = rel[0:HEADS]
    k.sg[12:24, 512:640] = jnp.broadcast_to(gscale, (16, 128))[0:HEADS]
    for t, src in ((0, k.q), (2, k.v)):
        row = jnp.sum(fold(mixed_all(src).astype(f32)), axis=0, keepdims=True)
        for p in range(4):
            at, lane = (6 + p, D) if t == 0 else (12 + 3 * p, 640)
            k.sg[at : at + 1, lane : lane + 192] = row[:, 192 * p : 192 * p + 192]
    k.fa[...] = dot(dz.T, weights)


def grad_input(k):
    for t, src in ((0, k.q), (1, k.k), (2, k.v)):
        k.fa[...] += dot(mixed_all(src), wide(k.wa, t))


def grad_rows(k, part):
    def go(rows, _):
        k.cot[rows, :] = (k.fb[rows, :] + k.fa[rows, :]).astype(bf16)
        return 0
    rows_loop(32, go, 0, *PARTS[part])


def grad_projections(k, part):
    own = lambda ref: jnp.concatenate([ref[3 * part + i] for i in range(3)], axis=1)
    for t, src, right in ((0, k.q, k.tok), (1, k.k, k.tok), (2, k.v, k.tok), (3, k.mixed, k.gb)):
        g = dot_l(own(src), right[...]).astype(bf16).reshape(2, 2, 96, D)
        for i in range(2):
            k.wa[t, 2 * part + i] = g[i]


def each(n, fn, k):
    def go(i, _):
        fn(k, i)
        return 0
    lax.fori_loop(0, n, go, 0)


COMPUTE_SCRATCH = dict(
    row=((1, BIAS), jnp.int32), hot=((NB, BIAS), bf16), tok=((PAD, D), bf16), cot=((PAD, D), bf16), sm=((4, 8, BIAS), f32), mask=((PAD, PAD), f32),
    first=((16, PAD), f32), second=((16, PAD), f32), factor=((16, PAD), f32), gate=((HEADS, 1, PAD), f32),
    bias=((HEADS, 128, 896), bf16), q=((PAIRS, PAD, 128), bf16), k=((PAIRS, PAD, 128), bf16),
    v=((PAIRS, PAD, 128), bf16), s=((PAD, PAD), f32), p=((HEADS, PAD, PAD), bf16), mixed=((PAIRS, PAD, 128), bf16),
    fa=((PAD, D), f32), fb=((PAD, D), f32), n1=((PAD, D), f32), inv1=((PAD, 128), f32), hid=((PAD, D), bf16),
    act=((4, PAD, D), bf16), dg=((4, PAD, D), bf16), out=((PAD, D), bf16), gb=((PAD, D), bf16),
    gs=((PAD, PAD), bf16), a=((128, BIAS), f32), ggate=((HEADS, 1, PAD), f32),
    goff=((HEADS, 1, BIAS), f32), sg=((32, BIAS), f32),
    wa=((4, 4, 2, 96, D), bf16), wi=((4, 8, 96, D), bf16), wo=((4, 8, 96, D), bf16),
)


MESH = pl.DeviceIdType.MESH
BLOCKS = (0, 1, 2)
SEMS = dict(
    wz=(3, 2, 3), w1=(3, 2, 3), w2=(3, 2, 3, 2), w3=(3, 2, 3), sm=(3,), rows=(2, 2, 9), r1=(3, 4), r2=(3, 4, 2), r3=(3, 4),
    r4=(3, 2, 3), a1=(3,), a2=(3, 2), a3=(3,), sg=(6,),
)
COMM_SCRATCH = dict(
    rb1a=((4, 2, 2, 96, D), bf16), rb1=((2, 4, 4, 96, D), bf16), rb2=((3, 4, 2, 96, D), bf16),
    rb3=((3, 4, 96, D), bf16), rb4=((3, 2, 3, 96, D), bf16), sgr=((5, 32, BIAS), f32), sgs=((6, 32, BIAS), f32), fin=((16, BIAS), f32),
)


class Net:
    def __init__(self, k):
        self.k = k
        dp, z = lax.axis_index("dp"), lax.axis_index("tensor")
        self.dp, self.z = dp, z
        c, x, y = dp % 2, (dp // 2) % 2, (dp // 4) % 2
        self.c = c
        across_x, across_y = dp + 2 * (1 - 2 * x), dp + 4 * (1 - 2 * y)
        self.core = (dp + 1 - 2 * c, z)
        self.x, self.y = (across_x, z), (across_y, z)
        self.one = ((1 - c) * across_x + c * across_y, z)
        self.two = (c * across_x + (1 - c) * across_y, z)
        at = lambda cc, yy, xx: 4 * cc + 2 * yy + xx
        ex, ey = at(c, y, 1 - x), at(c, 1 - y, x)
        self.e = at(c, y, x)
        self.e1 = (1 - c) * ex + c * ey
        self.e2 = c * ex + (1 - c) * ey
        self.e12 = at(c, 1 - y, 1 - x)

    def ahead(self, dz):
        return (self.z + dz) % 4

    def behind(self, dz):
        return (self.z + 4 - dz) % 4

    def copy(self, name, index, src, dst, device):
        sems = getattr(self.k, "sem_" + name)
        return pltpu.make_async_remote_copy(
            src_ref=src, dst_ref=dst, send_sem=sems.at[(0, *index)], recv_sem=sems.at[(1, *index)],
            device_id=device, device_id_type=MESH,
        )

    def greet(self):
        barrier = pltpu.get_barrier_semaphore()
        peers = [self.core, self.one, self.two] + [(self.dp, self.ahead(dz)) for dz in (1, 2, 3)]
        for peer in peers:
            pl.semaphore_signal(barrier, inc=1, device_id=peer, device_id_type=MESH)

    def all_here(self):
        pl.semaphore_wait(pltpu.get_barrier_semaphore(), 6)

    def block(self, b):
        return (self.k.wa, self.k.wi, self.k.wo)[b]

    def chunk(self, b, p, e):
        return self.block(b).at[e // 2, p, e % 2] if b == 0 else self.block(b).at[p, e]

    def side(self, b, p, c):
        return self.block(b).at[pl.ds(2 * c, 2), p] if b == 0 else self.block(b).at[p, pl.ds(4 * c, 4)]

    def plane(self, way, j):
        return self.z - 1 - j if way == 0 else self.z + 1 + j

    def wz(self, b, way, j):
        ref = self.chunk(b, self.plane(way, j - 1), self.e)
        return self.copy("wz", (b, way, j), ref, ref, (self.dp, self.z + 1 if way == 0 else self.z - 1))

    def w1(self, b, way, j):
        ref = self.chunk(b, self.plane(way, j), self.e)
        return self.copy("w1", (b, way, j), ref, ref, self.one)

    def w2(self, b, way, j, i):
        ref = self.chunk(b, self.plane(way, j), (self.e, self.e1)[i])
        return self.copy("w2", (b, way, j, i), ref, ref, self.two)

    def w3(self, b, way, j):
        ref = self.side(b, self.plane(way, j), self.c)
        return self.copy("w3", (b, way, j), ref, ref, self.core)

    def sm(self, d):
        ref = self.k.sm.at[self.z]
        return self.copy("sm", (d - 1,), ref, ref, (self.dp, self.ahead(d)))

    def rows(self, a, way, n):
        source, result = ((self.k.out, self.k.out_hbm), (self.k.cot, self.k.gtok_hbm))[a]
        j, (start, stop) = n // 3, PARTS[n % 3]
        size = min(stop, SEQ) - start
        slot = self.z - j if way == 0 else self.z + j
        to = self.z + 1 if way == 0 else self.z - 1
        at = result.at[pl.ds(pl.multiple_of(slot * SEQ + start, 16), size)]
        return self.copy("rows", (a, way, n), source.at[pl.ds(start, size)] if j == 0 else at, at, (self.dp, to))

    def sends(self, way, j):
        return (self.z <= 2) & (self.z >= j) if way == 0 else (self.z >= 1) & (self.z + j <= 3)

    def receives(self, way, j):
        return self.z >= 1 + j if way == 0 else self.z + 1 + j <= 3

    def r1(self, b, p):
        dst = self.k.rb1a.at[p] if b == 0 else self.k.rb1.at[b - 1, p]
        return self.copy("r1", (b, p), self.side(b, p, 1 - self.c), dst, self.core)

    def r2(self, b, p, i):
        return self.copy("r2", (b, p, i), self.chunk(b, p, (self.e1, self.e12)[i]), self.k.rb2.at[b, p, i], self.one)

    def r3(self, b, p):
        return self.copy("r3", (b, p), self.chunk(b, p, self.e2), self.k.rb3.at[b, p], self.two)

    def r4(self, b, way, p):
        to, i = (self.z + 1, p - 1) if way == 0 else (self.z - 1, p)
        return self.copy("r4", (b, way, i), self.chunk(b, p, self.e), self.k.rb4.at[b, way, i], (self.dp, to))

    def result(self, b, e):
        return (self.k.ra, self.k.ri, self.k.ro)[b].at[e]

    def keep(self, b):
        return pltpu.make_async_copy(self.chunk(b, self.z, self.e), self.result(b, self.e), self.k.sem_keep.at[b])

    def a1(self, b):
        return self.copy("a1", (b,), self.chunk(b, self.z, self.e), self.result(b, self.e), self.one)

    def a2(self, b, i):
        src = (self.chunk(b, self.z, self.e), self.result(b, self.e1))[i]
        return self.copy("a2", (b, i), src, self.result(b, (self.e, self.e1)[i]), self.two)

    def a3(self, b):
        ref = self.result(b, pl.ds(4 * self.c, 4))
        return self.copy("a3", (b,), ref, ref, self.core)

    def sg(self, i):
        k, half = self.k, pl.ds(16 * self.c, 16)
        if i < 3:
            return self.copy("sg", (i,), k.sgs.at[i], k.sgr.at[i], (self.core, self.x, self.y)[i])
        if i < 5:
            device = (self.dp, self.flip(1 if i == 3 else 2))
            return self.copy("sg", (i,), k.sgs.at[i, half], k.sgr.at[i, half], device)
        return self.copy("sg", (i,), k.sgs.at[5, half], k.sgs.at[5, half], self.core)

    def flip(self, bit):
        return self.z + bit * (1 - 2 * ((self.z // bit) % 2))


def loop(n, fn):
    def go(i, _):
        fn(i)
        return 0
    lax.fori_loop(0, n, go, 0)


def when(condition, fn):
    @pl.when(condition)
    def _():
        fn()


ORDER = (3, 0, 2, 1)


def weight_own(net, b):
    for way in (0, 1):
        when(net.sends(way, 0), lambda: net.wz(b, way, 0).start())


def weight_one(net, b, way, j):
    def step():
        net.wz(b, way, j).wait_recv()
        if j < 2:
            when(net.sends(way, j + 1), lambda: net.wz(b, way, j + 1).start())
        net.w1(b, way, j).start()
    when(net.receives(way, j), step)


def weight_two(net, b, way, j):
    def step():
        net.w1(b, way, j).wait_recv()
        net.w2(b, way, j, 0).start()
        net.w2(b, way, j, 1).start()
    when(net.receives(way, j), step)


def weight_core(net, b, way, j):
    def step():
        net.w2(b, way, j, 0).wait_recv()
        net.w2(b, way, j, 1).wait_recv()
        net.w3(b, way, j).start()
    when(net.receives(way, j), step)


def weight_there(net, b, way, j):
    when(net.receives(way, j), lambda: net.w3(b, way, j).wait_recv())


def weights_sent(net):
    for b in BLOCKS:
        for way in (0, 1):
            for j in range(3):
                def step():
                    net.w1(b, way, j).wait_send()
                    net.w2(b, way, j, 0).wait_send()
                    net.w2(b, way, j, 1).wait_send()
                    net.w3(b, way, j).wait_send()
                when(net.sends(way, j), lambda: net.wz(b, way, j).wait_send())
                when(net.receives(way, j), step)


def rows_own(net, a, part):
    for way in (0, 1):
        when(net.sends(way, 0), lambda: net.rows(a, way, part).start())


def rows_next(net, a, way, n):
    when(net.receives(way, (n - 1) // 3), lambda: net.rows(a, way, n - 1).wait_recv())
    if n + 2 < 9:
        when(net.sends(way, (n + 2) // 3), lambda: net.rows(a, way, n + 2).start())


def rows_sent(net, a):
    for n in range(9):
        for way in (0, 1):
            when(net.sends(way, n // 3), lambda: net.rows(a, way, n).wait_send())


def add(net, b, p, e, ref):
    k = net.k
    if b == 0:
        k.wa[e // 2, p, e % 2] = k.wa[e // 2, p, e % 2] + ref[...]
    else:
        net.block(b)[p, e] = net.block(b)[p, e] + ref[...]


def halves(net, b, p):
    net.r1(b, p).wait_recv()
    for j in range(4):
        src = net.k.rb1a.at[p, j // 2, j % 2] if b == 0 else net.k.rb1.at[b - 1, p, j]
        add(net, b, p, 4 * net.c + j, src)
    net.r2(b, p, 1).start()
    net.r2(b, p, 0).start()


def quarters(net, b, p):
    net.r2(b, p, 1).wait_recv()
    add(net, b, p, net.e2, net.k.rb2.at[b, p, 1])
    net.r3(b, p).start()
    net.r2(b, p, 0).wait_recv()
    add(net, b, p, net.e, net.k.rb2.at[b, p, 0])


def eighths(net, b, p):
    net.r3(b, p).wait_recv()
    add(net, b, p, net.e, net.k.rb3.at[b, p])
    if p > 0:
        when(net.z == 0, lambda: net.r4(b, 0, p).start())
    if p < 3:
        when(net.z == 3, lambda: net.r4(b, 1, p).start())


def chain(net, b, p):
    def link(way, i):
        net.r4(b, way, p).wait_recv()
        add(net, b, p, net.e, net.k.rb4.at[b, way, i])
        net.r4(b, way, p).start()
    if p > 1:
        when((net.z > 0) & (net.z < p), lambda: link(0, p - 1))
    if p < 2:
        when((net.z > p) & (net.z < 3), lambda: link(1, p))


def over_z(net, b):
    k, z = net.k, net.z
    def last(way, i):
        net.r4(b, way, z).wait_recv()
        add(net, b, z, net.e, k.rb4.at[b, way, i])
    when(z > 0, lambda: last(0, z - 1))
    when(z < 3, lambda: last(1, z))
    net.keep(b).start()
    net.a1(b).start()
    net.a2(b, 0).start()


def around(net, b):
    net.a1(b).wait_recv()
    net.a2(b, 1).start()


def to_core(net, b):
    net.keep(b).wait()
    net.a2(b, 0).wait_recv()
    net.a2(b, 1).wait_recv()
    net.a3(b).start()


def gradients_sent(net, b):
    net.a3(b).wait_recv()
    for p in range(4):
        net.r1(b, p).wait_send()
        net.r2(b, p, 0).wait_send()
        net.r2(b, p, 1).wait_send()
        net.r3(b, p).wait_send()
    for p in range(4):
        when(net.z < p, lambda: net.r4(b, 0, p).wait_send())
        when(net.z > p, lambda: net.r4(b, 1, p).wait_send())
    net.a1(b).wait_send()
    net.a2(b, 0).wait_send()
    net.a2(b, 1).wait_send()
    net.a3(b).wait_send()


def halves_out(net, b, p):
    net.r1(b, p).start()


def small_sum(net, i):
    k, half = net.k, pl.ds(16 * net.c, 16)
    if i == 0:
        k.sgs[0] = k.sg[...]
    else:
        net.sg(i - 1).wait_recv()
    if 0 < i < 4:
        k.sgs[i] = k.sgs[i - 1] + k.sgr[i - 1]
    elif 3 < i < 6:
        k.sgs[i, half, :] = k.sgs[i - 1, half, :] + k.sgr[i - 1, half, :]
    if i < 6:
        net.sg(i).start()


PLAN = (
    (
        (weight_own, 0), (weight_own, 2), (weight_one, 0, 0, 0), (weight_one, 0, 1, 0), (weight_own, 1),
        (weight_two, 0, 0, 0),
    ),
    (
        (weight_one, 0, 1, 1), (weight_one, 0, 0, 1), (weight_two, 0, 1, 0), (weight_core, 0, 0, 0),
        (weight_two, 0, 1, 1), (weight_one, 1, 0, 0), (weight_one, 0, 1, 2), (weight_one, 0, 0, 2),
        (weight_two, 0, 0, 1), (weight_one, 1, 1, 0), (weight_two, 0, 0, 2), (weight_one, 2, 0, 0),
        (weight_core, 0, 1, 0),
    ),
    (
        (weight_one, 2, 0, 1), (weight_core, 0, 0, 1), (weight_there, 0, 0, 0), (weight_core, 0, 1, 1),
        (weight_two, 0, 1, 2), (weight_core, 0, 0, 2), (weight_one, 1, 1, 1), (weight_one, 1, 1, 2),
        (weight_one, 2, 1, 0), (weight_one, 1, 0, 1), (weight_two, 1, 0, 0), (weight_core, 0, 1, 2),
    ),
    (
        (weight_there, 0, 1, 0),
    ),
    (
        (weight_one, 2, 0, 2), (weight_two, 1, 1, 1), (weight_two, 2, 0, 0), (weight_there, 0, 0, 1),
        (weight_two, 1, 1, 2), (weight_there, 0, 0, 2), (weight_one, 2, 1, 1), (weight_there, 0, 1, 1),
        (weight_there, 0, 1, 2),
    ),
    (),
    (),
    (
        (weight_core, 1, 0, 0), (weight_two, 2, 1, 0), (weight_two, 1, 1, 0), (weight_two, 2, 0, 2),
        (weight_core, 1, 1, 1), (weight_one, 1, 0, 2), (weight_two, 1, 0, 1), (weight_two, 2, 0, 1),
    ),
    (),
    (
        (weight_core, 1, 1, 2),
    ),
    (),
    (
        (weight_core, 2, 0, 2), (weight_two, 1, 0, 2), (weight_core, 2, 0, 0), (weight_one, 2, 1, 2),
        (weight_core, 2, 1, 0), (weight_two, 2, 1, 1),
    ),
    (
        (weight_there, 2, 0, 2), (weight_there, 1, 0, 0), (weight_core, 1, 1, 0), (weight_two, 2, 1, 2),
        (weight_core, 1, 0, 1), (weight_there, 1, 1, 2),
    ),
    (
        (weight_there, 2, 0, 0), (weight_core, 2, 1, 1),
    ),
    (
        (weight_there, 2, 1, 0), (weight_there, 1, 1, 1), (weight_core, 2, 0, 1),
    ),
    (
        (weight_there, 1, 1, 0), (weight_core, 1, 0, 2),
    ),
    (),
    (),
    (
        (weight_there, 1, 0, 1),
    ),
    (
        (weight_there, 2, 1, 1), (weight_there, 2, 0, 1),
    ),
    (
        (weight_core, 2, 1, 2),
    ),
    (),
    (
        (weight_there, 1, 0, 2),
    ),
    (),
    (),
    (
        (weight_there, 2, 1, 2),
    ),
    (),
    (
        (rows_own, 0, 0),
    ),
    (
        (rows_own, 0, 1),
    ),
    (),
    (
        (halves_out, 2, 3), (rows_own, 0, 2), (halves_out, 1, 3), (rows_next, 0, 0, 1),
    ),
    (
        (halves_out, 1, 0), (rows_next, 0, 1, 1), (halves_out, 2, 0), (halves, 2, 3),
    ),
    (
        (halves_out, 2, 2), (rows_next, 0, 0, 2), (halves_out, 1, 2), (halves, 1, 0), (halves, 1, 3),
        (rows_next, 0, 1, 2),
    ),
    (
        (rows_next, 0, 1, 3), (halves_out, 2, 1), (rows_next, 0, 1, 4), (halves_out, 1, 1), (rows_next, 0, 0, 3),
        (rows_next, 0, 0, 4), (halves, 2, 0), (halves, 1, 2),
    ),
    (),
    (
        (quarters, 2, 0), (quarters, 2, 3),
    ),
    (),
    (
        (halves, 2, 1), (rows_next, 0, 1, 5),
    ),
    (),
    (
        (rows_next, 0, 1, 6), (rows_next, 0, 0, 5),
    ),
    (),
    (),
    (
        (rows_own, 1, 0), (quarters, 1, 2), (small_sum, 0), (eighths, 2, 3), (halves, 2, 2),
    ),
    (
        (rows_next, 0, 1, 7), (rows_own, 1, 1),
    ),
    (
        (rows_own, 1, 2), (halves, 1, 1),
    ),
    (),
    (
        (halves_out, 0, 2), (quarters, 1, 0), (halves_out, 0, 3), (halves_out, 0, 0), (quarters, 1, 3),
        (eighths, 2, 0), (rows_next, 0, 1, 8), (rows_next, 1, 1, 1), (quarters, 1, 1), (eighths, 1, 2),
        (quarters, 2, 1), (halves, 0, 3), (rows_next, 1, 0, 1), (rows_next, 1, 1, 2), (eighths, 1, 0), (halves, 0, 2),
        (eighths, 2, 1), (rows_next, 1, 0, 2), (quarters, 0, 3), (rows_next, 1, 0, 3), (halves, 0, 0),
        (eighths, 1, 3), (halves_out, 0, 1), (rows_next, 1, 0, 4), (small_sum, 1), (eighths, 1, 1), (quarters, 2, 2),
        (quarters, 0, 2), (chain, 2, 0), (eighths, 0, 3), (chain, 1, 2), (halves, 0, 1), (chain, 1, 0),
        (rows_next, 0, 0, 6), (rows_next, 1, 1, 3), (chain, 1, 3), (quarters, 0, 0), (rows_next, 0, 1, 9),
        (small_sum, 2), (chain, 1, 1), (chain, 2, 3), (chain, 2, 1), (eighths, 2, 2), (rows_next, 1, 1, 4),
        (eighths, 0, 2), (quarters, 0, 1), (rows_next, 0, 0, 7), (chain, 0, 3), (chain, 2, 2), (rows_next, 1, 1, 5),
        (chain, 0, 2), (eighths, 0, 0), (rows_next, 1, 0, 5), (over_z, 1), (chain, 0, 0), (eighths, 0, 1),
        (over_z, 2), (around, 1), (chain, 0, 1), (small_sum, 3), (rows_next, 0, 0, 8), (around, 2), (over_z, 0),
        (small_sum, 4), (to_core, 1), (rows_next, 1, 1, 6), (rows_next, 1, 1, 7), (around, 0), (rows_next, 0, 0, 9),
        (rows_next, 1, 0, 6), (rows_next, 1, 1, 8), (to_core, 2), (rows_next, 1, 0, 7), (small_sum, 5), (to_core, 0),
        (small_sum, 6), (rows_next, 1, 1, 9), (rows_next, 1, 0, 8), (rows_next, 1, 0, 9),
    ),
)


def kernel(names, *refs):
    k = K()
    for name, ref in zip(names, refs):
        setattr(k, name, ref)
    net = Net(k)
    z = net.z
    own_rows = pl.ds(pl.multiple_of(z * SEQ, 16), SEQ)
    moves = [
        (k.wq_hbm, k.wa.at[0, z]), (k.wk_hbm, k.wa.at[1, z]), (k.wv_hbm, k.wa.at[2, z]), (k.wout_hbm, k.wa.at[3, z]),
        (k.wi_hbm, k.wi.at[z]), (k.wo_hbm, k.wo.at[z]),
        (k.tok_hbm.at[own_rows], k.tok.at[pl.ds(0, SEQ)]), (k.cot_hbm.at[own_rows], k.cot.at[pl.ds(0, SEQ)]),
    ]
    local = [pltpu.make_async_copy(src, dst, k.sem_in.at[i]) for i, (src, dst) in enumerate(moves)]
    for c in local:
        c.start()
    run = lambda n: [step(net, *given) for step, *given in PLAN[n]]
    net.greet()
    k.tok[SEQ:PAD] = jnp.zeros((PAD - SEQ, D), bf16)
    k.cot[SEQ:PAD] = jnp.zeros((PAD - SEQ, D), bf16)
    k.sg[...] = jnp.zeros((32, BIAS), f32)
    k.factor[...] = jnp.zeros((16, PAD), f32)
    k.fb[...] = jnp.zeros((PAD, D), f32)
    for c in local[0:6]:
        c.wait()
    net.all_here()
    run(0)
    own_small(k, z)
    for d in (1, 2, 3):
        net.sm(d).start()
    run(1)
    mask_build(k, z)
    run(2)
    for d in (1, 2, 3):
        net.sm(d).wait_recv()
    for c in local[6:8]:
        c.wait()
    gates(k)
    run(3)
    bias_tables(k)
    run(4)
    project(k)
    run(5)

    def forward(pr):
        attend(k, pr)
        for n in range(PAIRS):
            when(pr == n, lambda: run(6 + n))
    loop(PAIRS, forward)
    norm_one(k)
    run(12)

    feed_in(k, z)
    run(13)
    feed_out(k, z)
    run(14)
    last = 3 - 3 * (z // 2)

    def layer_two(n):
        p = z + (2 * (n % 2) - 1) * (1 + n // 2)
        when((p >= 0) & (p <= 3), lambda: feed_in(k, p))
        for i in range(6):
            when(n == i, lambda: run(15 + 2 * i))
        when((p >= 0) & (p <= 3) & (p != last), lambda: feed_out(k, p))
        for i in range(6):
            when(n == i, lambda: run(16 + 2 * i))
    loop(6, layer_two)
    here = [
        pltpu.make_async_copy(k.out.at[pl.ds(0, SEQ)], k.out_hbm.at[own_rows], k.sem_in.at[0]),
        pltpu.make_async_copy(k.cot.at[pl.ds(0, SEQ)], k.gtok_hbm.at[own_rows], k.sem_in.at[1]),
    ]
    for part in range(3):
        feed_out(k, last, *PARTS[part])
        norm_two(k, part)
        run(27 + part)
    here[0].start()
    weights_sent(net)

    def layer_two_back(i):
        feed_back(k, (1 - i % 2) * (3 - i // 2) + (i % 2) * (i // 2))
        for n in range(4):
            when(i == n, lambda: run(30 + n))
    loop(4, layer_two_back)
    norm_one_back(k)
    run(34)

    def backward(pr):
        attend_back(k, pr)
        for n in range(PAIRS):
            when(pr == n, lambda: run(35 + n))
    loop(PAIRS, backward)
    gate_back(k)
    run(41)
    grad_input(k)
    for part in range(3):
        grad_rows(k, part)
        run(42 + part)
    here[1].start()
    for part in (0, 1):
        grad_projections(k, part)
        run(45 + part)
    k.fin[...] = jnp.zeros((16, BIAS), f32)
    k.fin[0:6, :] = k.sgs[5, 0:6, :]
    k.fin[6:7, :] = k.sgs[5, pl.ds(6 + z, 1), :]
    for i in range(3):
        k.fin[8 + i : 9 + i, :] = k.sgs[5, pl.ds(12 + 3 * z + i, 1), :]
    k.fin[11:13, :] = k.sgs[5, 24:26, :]
    finish = pltpu.make_async_copy(k.fin, k.sg_hbm, k.sem_in.at[2])
    finish.start()
    for b in (2, 1, 0):
        gradients_sent(net, b)
    for i in range(6):
        net.sg(i).wait_send()
    for d in (1, 2, 3):
        net.sm(d).wait_send()
    for a in (0, 1):
        rows_sent(net, a)
    here[0].wait()
    here[1].wait()
    finish.wait()


def finish_kernel(out, gtok, ra, ri, ro, sg, *rest):
    names = FINAL + ("stage", "wide", "rows", "sem")
    k = K()
    for name, ref in zip(names, rest):
        setattr(k, name, ref)
    count = iter(range(64))
    def copy(src, dst):
        c = pltpu.make_async_copy(src, dst, k.sem.at[next(count)])
        c.start()
        return c
    parts = [pl.ds(4 * i, 4) for i in (0, 1)]
    size = out.shape[0] // 4
    inward = [[copy(src.at[part], k.stage.at[i, part]) for part in parts] for i, src in enumerate((ri, ro, ra))]
    pairs = [(src, k.rows.at[i], dst) for i, (src, dst) in enumerate(((out, k.output), (gtok, k.grad_tokens)))]
    moves = [(src.at[at], via.at[at], dst.at[at]) for src, via, dst in pairs for at in [pl.ds(size * i, size) for i in range(4)]]
    copies = [copy(src, via) for src, via, _ in moves]
    row = lambda r, lane, n: sg[r : r + 1, lane : lane + n].reshape(n)
    k.b_out[...], k.norm1_gain[...], k.norm1_bias[...] = row(0, 0, D), row(1, 0, D), row(2, 0, D)
    k.b_outer[...], k.norm2_gain[...], k.norm2_bias[...] = row(3, 0, D), row(4, 0, D), row(5, 0, D)
    k.b_inner[...], k.b_query[...], k.b_value[...] = row(6, 0, D), row(6, D, 192), row(8, 640, 192)
    k.rel_table[...] = sg[8:11, 0:NB]
    lane = lax.broadcasted_iota(jnp.int32, (1, 128), 1)
    cell = lambda r, at: sg[r : r + 1, at : at + 128]
    k.gate_scale[...] = jnp.where(lane == 0, cell(8, 512), jnp.where(lane == 1, cell(9, 512), cell(10, 512)))[:, 0:3]
    k.gate_bias[...] = jnp.where(lane < 4, cell(11, D), cell(12, D))[:, 0:8]
    for i in (0, 1):
        heads = cell(11 + i, 0)
        for pr in range(1, PAIRS):
            heads = heads + cell(11 + i, 128 * pr)
        k.gate_weight[4 * i : 4 * i + 4, :] = jnp.broadcast_to(heads[:, 0:HEAD] + heads[:, HEAD:128], (4, HEAD))
    outward = []
    def pass_rows(n):
        copies[n].wait()
        outward.append(copy(moves[n][1], moves[n][2]))
    for i in range(3):
        for j in (0, 1):
            inward[i][j].wait()
            def widen(n):
                k.wide[i, 4 * j + n] = k.stage[i, 4 * j + n].astype(f32)
            loop(4, widen)
            if i < 2:
                outward.append(copy(k.wide.at[i, parts[j]], (k.w_inner, k.w_outer)[i].at[parts[j]]))
            else:
                for n, ref in enumerate(((k.w_query, k.w_key), (k.w_value, k.w_out))[j]):
                    outward.append(copy(k.wide.at[i, pl.ds(4 * j + 2 * n, 2)], ref))
            pass_rows(2 * i + j)
    pass_rows(6)
    pass_rows(7)
    for c in outward:
        c.wait()


FINAL = (
    "output", "grad_tokens", "w_query", "w_key", "w_value", "w_out", "w_inner", "w_outer", "b_query", "b_value", "b_out",
    "gate_weight", "gate_bias", "gate_scale", "rel_table", "norm1_gain", "norm1_bias", "b_inner", "b_outer", "norm2_gain",
    "norm2_bias",
)


def body(
    tokens, slot_kind, offset_bucket, w_query, b_query, w_key, w_value, b_value, w_out, b_out, gate_weight, gate_bias,
    gate_scale, rel_table, norm1_gain, norm1_bias, w_inner, b_inner, w_outer, b_outer, norm2_gain, norm2_bias, cotangent,
):
    n_dp = lax.axis_size("dp")
    rows = tokens.shape[0]
    shape = jax.ShapeDtypeStruct
    anywhere = pl.BlockSpec(memory_space=pl.ANY)
    vmem = pl.BlockSpec(memory_space=pltpu.VMEM)
    smem = pl.BlockSpec(memory_space=pltpu.SMEM)
    given = dict(
        kinds=(smem, slot_kind), bucket=(vmem, offset_bucket.reshape(1, OFFSETS)), rel=(vmem, rel_table.T),
        b_query=(vmem, b_query), b_value=(vmem, b_value), b_inner=(vmem, b_inner), scale=(vmem, gate_scale.reshape(1, 3)),
        gw=(vmem, gate_weight.T), gate_bias=(vmem, gate_bias), b_out=(vmem, b_out), b_outer=(vmem, b_outer),
        norm1_gain=(vmem, norm1_gain), norm1_bias=(vmem, norm1_bias), norm2_gain=(vmem, norm2_gain),
        norm2_bias=(vmem, norm2_bias), tok_hbm=(anywhere, tokens), cot_hbm=(anywhere, cotangent),
        wq_hbm=(anywhere, w_query.T.reshape(2, 96, D)), wk_hbm=(anywhere, w_key.T.reshape(2, 96, D)),
        wv_hbm=(anywhere, w_value.T.reshape(2, 96, D)), wout_hbm=(anywhere, w_out.reshape(2, 96, D)),
        wi_hbm=(anywhere, w_inner.reshape(8, 96, D)), wo_hbm=(anywhere, w_outer.reshape(8, 96, D)),
    )
    names = list(given) + ["out_hbm", "gtok_hbm", "ra", "ri", "ro", "sg_hbm"]
    scratch = []
    for name, (dims, dtype) in (COMPUTE_SCRATCH | COMM_SCRATCH).items():
        names.append(name)
        scratch.append(pltpu.VMEM(dims, dtype))
    for name, dims in SEMS.items():
        names.append("sem_" + name)
        scratch.append(pltpu.SemaphoreType.DMA((2, *dims)))
    for name, count in (("sem_in", 8), ("sem_keep", 3)):
        names.append(name)
        scratch.append(pltpu.SemaphoreType.DMA((count,)))
    whole = shape((8, 96, D), bf16)
    out, gtok, ra, ri, ro, sg = pl.pallas_call(
        functools.partial(kernel, names),
        in_specs=[spec for spec, _ in given.values()],
        out_specs=[anywhere] * 6,
        out_shape=[shape((rows, D), bf16), shape((rows, D), bf16), whole, whole, whole, shape((16, BIAS), f32)],
        scratch_shapes=scratch,
        compiler_params=pltpu.CompilerParams(collective_id=0, has_side_effects=True, vmem_limit_bytes=VMEM_LIMIT),
    )(*[value for _, value in given.values()])
    if n_dp > 8:
        groups = [list(range(g, n_dp, 8)) for g in range(8)]
        ra, ri, ro, sg = lax.psum((ra.astype(f32), ri.astype(f32), ro.astype(f32), sg), "dp", axis_index_groups=groups)
        ra, ri, ro = ra.astype(bf16), ri.astype(bf16), ro.astype(bf16)
    vector = shape((D,), f32)
    part = shape((2, 96, D), f32)
    final = dict(
        output=(anywhere, shape((rows, D), bf16)), grad_tokens=(anywhere, shape((rows, D), bf16)),
        w_query=(anywhere, part), w_key=(anywhere, part), w_value=(anywhere, part), w_out=(anywhere, part),
        w_inner=(anywhere, shape((8, 96, D), f32)), w_outer=(anywhere, shape((8, 96, D), f32)),
        b_query=(vmem, shape((192,), f32)), b_value=(vmem, shape((192,), f32)), gate_weight=(vmem, shape((8, HEAD), f32)),
        gate_bias=(vmem, shape((1, 8), f32)), gate_scale=(vmem, shape((1, 3), f32)), rel_table=(vmem, shape((3, NB), f32)),
    )
    specs, shapes = zip(*[final.get(name, (vmem, vector)) for name in FINAL])
    results = pl.pallas_call(
        finish_kernel,
        in_specs=[anywhere] * 5 + [vmem],
        out_specs=list(specs),
        out_shape=list(shapes),
        scratch_shapes=[pltpu.VMEM((3, 8, 96, D), bf16), pltpu.VMEM((3, 8, 96, D), f32), pltpu.VMEM((2, rows, D), bf16), pltpu.SemaphoreType.DMA((40,))],
        compiler_params=pltpu.CompilerParams(vmem_limit_bytes=VMEM_LIMIT),
    )(out, gtok, ra, ri, ro, sg)
    r = dict(zip(FINAL, results))
    for name in ("w_query", "w_key", "w_value"):
        r[name] = r[name].reshape(192, D).T
    r["w_out"] = r["w_out"].reshape(192, D)
    r["w_inner"] = r["w_inner"].reshape(D, D)
    r["w_outer"] = r["w_outer"].reshape(D, D)
    r["gate_weight"] = r["gate_weight"].T
    r["gate_bias"] = r["gate_bias"].reshape(8)
    r["gate_scale"] = r["gate_scale"].reshape(3)
    r["rel_table"] = r["rel_table"].T
    order = (
        "output", "grad_tokens", "w_query", "b_query", "w_key", "w_value", "b_value", "w_out", "b_out", "gate_weight",
        "gate_bias", "gate_scale", "rel_table", "norm1_gain", "norm1_bias", "w_inner", "b_inner", "w_outer", "b_outer",
        "norm2_gain", "norm2_bias",
    )
    return tuple(r[name] for name in order)


def solution(mesh):
    in_specs = (
        P("dp", None),
        P("dp"),
        P(),
        P(None, "tensor"),
        P("tensor"),
        P(None, "tensor"),
        P(None, "tensor"),
        P("tensor"),
        P("tensor", None),
        P(),
        P(),
        P(),
        P("tensor"),
        P(None, "tensor"),
        P(),
        P(),
        P(None, "tensor"),
        P("tensor"),
        P("tensor", None),
        P(),
        P(),
        P(),
        P("dp", None),
    )
    out_specs = (
        P("dp", None),
        P("dp", None),
        P(None, "tensor"),
        P("tensor"),
        P(None, "tensor"),
        P(None, "tensor"),
        P("tensor"),
        P("tensor", None),
        P(),
        P(),
        P(),
        P("tensor"),
        P(None, "tensor"),
        P(),
        P(),
        P(None, "tensor"),
        P("tensor"),
        P("tensor", None),
        P(),
        P(),
        P(),
    )
    return jax.shard_map(body, mesh=mesh, in_specs=in_specs, out_specs=out_specs, check_vma=False)
```

```python
import functools
import math

import jax
import jax.numpy as jnp
from jax import lax
from jax.experimental import pallas as pl
from jax.experimental.pallas import tpu as pltpu
from jax.sharding import PartitionSpec as P

HEAD = 64
SEQ = 496
PAD = 512
D = 768
PAIRS = 6
HEADS = 12
BIAS = 1024
NB = 320
VMEM_LIMIT = 64 * 2**20 - 2**16
OFFSETS = 991
HALF = SEQ // 2
PARTS = ((0, 128), (128, 320), (320, PAD))
f32 = jnp.float32
bf16 = jnp.bfloat16
residual_scale = 24.0**0.25
norm_epsilon = 1e-05
highest = lax.Precision.HIGHEST


def dot(a, b, precision=None):
    return lax.dot_general(a, b, (((1,), (0,)), ((), ())), preferred_element_type=f32, precision=precision)


def dot_t(a, b, precision=None):
    return lax.dot_general(a, b, (((1,), (1,)), ((), ())), preferred_element_type=f32, precision=precision)


def dot_l(a, b):
    return lax.dot_general(a, b, (((0,), (0,)), ((), ())), preferred_element_type=f32)


def fold(x):
    return jnp.sum(x.reshape(x.shape[0] // 8, 8, x.shape[1]), axis=0)


def stats(r):
    c = r - jnp.mean(r, -1, keepdims=True)
    inv = lax.rsqrt(jnp.mean(c * c, -1, keepdims=True) + norm_epsilon)
    return c * inv, inv


def norm_back(g, n, inv):
    return inv * (g - jnp.mean(g, -1, keepdims=True) - n * jnp.mean(g * n, -1, keepdims=True))


def wide(ref, i):
    return ref[i].reshape(D, D)


def rows_loop(step, body, carry, first=0, last=PAD):
    def go(c, carry):
        return body(pl.ds(pl.multiple_of(c * step, step), step), carry)
    return lax.fori_loop(first // step, last // step, go, carry)


class K:
    pass


def head_mask(hh):
    lane = lax.broadcasted_iota(jnp.int32, (1, 128), 1)
    return jnp.where((lane // HEAD) == hh, 1.0, 0.0).astype(bf16)


def line(ref):
    return ref[...].astype(f32).reshape(1, ref.shape[0])


def one_hot(k):
    k.row[...] = jnp.full((1, BIAS), -1, jnp.int32)
    k.row[:, 0:OFFSETS] = k.bucket[...]
    hot = jnp.where(lax.broadcasted_iota(jnp.int32, (NB, BIAS), 0) == k.row[...], 1.0, 0.0).astype(bf16)
    for n in range(4):
        m = lax.broadcasted_iota(jnp.int32, (BIAS, 256), 0) + lax.broadcasted_iota(jnp.int32, (BIAS, 256), 1) + 256 * n
        turn = jnp.where((m == 879) | (m == 1903), 1.0, 0.0).astype(bf16)
        k.hot[:, 256 * n : 256 * n + 256] = dot(hot, turn).astype(bf16)


def own_small(k, z):
    one_hot(k)
    k.sm[z, 0:3, :] = dot(k.rel[...], k.hot[...])
    k.sm[z, 3:4, 0:192] = line(k.b_query)
    k.sm[z, 3:4, 192:384] = line(k.b_value)
    k.sm[z, 4:5, 0:D] = line(k.b_inner)
    for i in range(3):
        k.sm[z, 5 + i : 6 + i, :] = jnp.broadcast_to(k.scale[:, i : i + 1].astype(f32), (1, BIAS))


def mask_build(k, z):
    kind = k.kinds[z].astype(f32)
    def go(rows, _):
        j = lax.broadcasted_iota(jnp.int32, (32, PAD), 0) + rows.start
        i = lax.broadcasted_iota(jnp.int32, (32, PAD), 1)
        far = jnp.where(j < HALF, 0, 1) != jnp.where(i < HALF, 0, 1)
        k.mask[rows, :] = jnp.where(j < SEQ, 0.0, -1e30) + jnp.where(far, -1e30, 0.0) * kind
        return 0
    rows_loop(32, go, 0)


def gate_weights(k):
    gw = k.gw[...].astype(f32)
    tile = lambda v: jnp.concatenate([jnp.concatenate([v, v], axis=1)] * PAIRS, axis=1)
    first = tile(jnp.sum(gw[0:4], axis=0, keepdims=True))
    second = tile(jnp.sum(gw[4:8], axis=0, keepdims=True))
    bias = line(k.gate_bias)
    own = (lax.broadcasted_iota(jnp.int32, (16, D), 1) // HEAD) == lax.broadcasted_iota(jnp.int32, (16, D), 0)
    both = jnp.concatenate([jnp.where(own, first, 0.0), jnp.where(own, second, 0.0)], axis=0)
    add = lambda v: jnp.sum(v, axis=1, keepdims=True)
    return both, add(bias[:, 0:4]), add(bias[:, 4:8]), own


def gates(k):
    weights, first_bias, second_bias, _ = gate_weights(k)
    logits = dot_t(weights, k.tok[...].astype(f32), precision=highest)
    first = jax.nn.sigmoid(logits[0:16] + first_bias)
    second = jax.nn.sigmoid(logits[16:32] + second_bias)
    k.first[...] = first
    k.second[...] = second
    for h in range(HEADS):
        k.factor[h : h + 1, :] = k.sm[h // 3, 5 + h % 3 : 6 + h % 3, 0:PAD]
    value = first * (second * k.factor[...] - 1.0) + 2.0
    for h in range(HEADS):
        k.gate[h] = value[h : h + 1, :]


def bias_tables(k):
    def go(p, _):
        for i in range(3):
            row = jnp.broadcast_to(k.sm[p, i : i + 1, :], (128, BIAS))
            k.bias[p * 3 + i] = pltpu.roll(row, 0, 1, stride=1, stride_axis=0)[:, 0:896].astype(bf16)
        return 0
    lax.fori_loop(0, 4, go, 0)


def small_row(k, row, start):
    return jnp.concatenate([k.sm[p, row : row + 1, start : start + 192] for p in range(4)], axis=1)


def project(k):
    bq = small_row(k, 3, 0)
    bv = small_row(k, 3, 192)
    for t, dest, bias, scale in ((0, k.q, bq, 0.125), (1, k.k, None, None), (2, k.v, bv, None)):
        r = dot_t(k.tok[...], wide(k.wa, t))
        if bias is not None:
            r = r + bias
        if scale is not None:
            r = r * scale
        r = r.astype(bf16)
        for pr in range(PAIRS):
            dest[pr] = r[:, 128 * pr : 128 * pr + 128]


def attend(k, pr):
    qp, kp, vp = k.q[pr], k.k[pr], k.v[pr]
    total = None
    for hh in range(2):
        h = pr * 2 + hh
        hm = head_mask(hh)
        km = kp * hm
        gate = k.gate[h]
        m8 = jnp.full((8, PAD), -3e38, f32)
        for c in range(4):
            s = dot_t(km[128 * c : 128 * c + 128], qp)
            k.s[128 * c : 128 * c + 128, :] = s
        for c in range(16):
            rows = slice(32 * c, 32 * c + 32)
            lane = 384 - 128 * (c // 4)
            t = k.bias[h, 32 * (c % 4) : 32 * (c % 4) + 32, lane : lane + PAD].astype(f32)
            s = k.s[rows, :] + t * gate + k.mask[rows, :]
            k.s[rows, :] = s
            m8 = jnp.maximum(m8, jnp.max(s.reshape(4, 8, PAD), axis=0))
        m = jnp.max(m8, axis=0, keepdims=True)
        l8 = jnp.zeros((8, PAD), f32)
        for c in range(16):
            rows = slice(32 * c, 32 * c + 32)
            e = jnp.exp(k.s[rows, :] - m)
            k.s[rows, :] = e
            l8 = l8 + fold(e)
        inv = 1.0 / jnp.sum(l8, axis=0, keepdims=True)
        for c in range(16):
            rows = slice(32 * c, 32 * c + 32)
            k.p[h, rows, :] = (k.s[rows, :] * inv).astype(bf16)
        part = dot_l(k.p[h], vp * hm)
        total = part if total is None else total + part
    k.mixed[pr] = total.astype(bf16)


def mixed_all(ref):
    return jnp.concatenate([ref[pr] for pr in range(PAIRS)], axis=1)


def norm_one(k):
    k.fa[...] = dot(mixed_all(k.mixed), wide(k.wa, 3))
    b_out, gain, shift = line(k.b_out), line(k.norm1_gain), line(k.norm1_bias)
    def go(rows, _):
        r = residual_scale * k.tok[rows, :].astype(f32) + k.fa[rows, :] + b_out
        n, inv = stats(r)
        k.n1[rows, :] = n
        k.inv1[rows, :] = jnp.broadcast_to(inv, (32, 128))
        k.hid[rows, :] = (n * gain + shift).astype(bf16)
        return 0
    rows_loop(32, go, 0)


def feed_in(k, p):
    k.fa[...] = dot(k.hid[...], wide(k.wi, p))
    b = k.sm[p, 4:5, 0:D]
    def go(rows, _):
        x = k.fa[rows, :] + b
        half = 0.5 * (1.0 + lax.erf(x * (1.0 / math.sqrt(2.0))))
        k.act[p, rows, :] = (x * half).astype(bf16)
        k.dg[p, rows, :] = (half + x * (jnp.exp(-0.5 * x * x) * (1.0 / math.sqrt(2.0 * math.pi)))).astype(bf16)
        return 0
    rows_loop(16, go, 0)


def feed_out(k, p, first=0, last=PAD):
    k.fb[first:last, :] += dot(k.act[p, first:last, :], wide(k.wo, p))


def norm_two(k, part):
    b_outer, gain1, shift1 = line(k.b_outer), line(k.norm1_gain), line(k.norm1_bias)
    gain2, shift2 = line(k.norm2_gain), line(k.norm2_bias)
    def go(rows, carry):
        g_gain, g_shift, g_b = carry
        r = residual_scale * (k.n1[rows, :] * gain1 + shift1) + k.fb[rows, :] + b_outer
        n, inv = stats(r)
        k.out[rows, :] = (n * gain2 + shift2).astype(bf16)
        up = k.cot[rows, :].astype(f32)
        g2 = norm_back(up * gain2, n, inv)
        low = g2.astype(bf16)
        k.gb[rows, :] = low
        k.fb[rows, :] = residual_scale * g2
        return g_gain + fold(up * n), g_shift + fold(up), g_b + fold(low.astype(f32))
    zero = jnp.zeros((8, D), f32)
    g_gain, g_shift, g_b = rows_loop(32, go, (zero, zero, zero), *PARTS[part])
    for row, v in ((3, g_b), (4, g_gain), (5, g_shift)):
        k.sg[row : row + 1, 0:D] += jnp.sum(v, axis=0, keepdims=True)


def feed_back(k, p):
    k.fa[...] = dot_t(k.gb[...], wide(k.wo, p))
    def go(rows, acc):
        gi = (k.fa[rows, :] * k.dg[p, rows, :].astype(f32)).astype(bf16)
        k.dg[p, rows, :] = gi
        return acc + fold(gi.astype(f32))
    acc = rows_loop(32, go, jnp.zeros((8, D), f32))
    k.sg[pl.ds(6 + p, 1), 0:D] = jnp.sum(acc, axis=0, keepdims=True)
    k.fb[...] += dot_t(k.dg[p], wide(k.wi, p))
    k.wo[p] = dot_l(k.act[p], k.gb[...]).astype(bf16).reshape(8, 96, D)
    k.wi[p] = dot_l(k.hid[...], k.dg[p]).astype(bf16).reshape(8, 96, D)


def norm_one_back(k):
    gain = line(k.norm1_gain)
    def go(rows, carry):
        g_gain, g_shift, g_b = carry
        gh = k.fb[rows, :]
        n = k.n1[rows, :]
        g1 = norm_back(gh * gain, n, k.inv1[rows, 0:1])
        low = g1.astype(bf16)
        k.gb[rows, :] = low
        k.fb[rows, :] = residual_scale * g1
        return g_gain + fold(gh * n), g_shift + fold(gh), g_b + fold(low.astype(f32))
    zero = jnp.zeros((8, D), f32)
    g_gain, g_shift, g_b = rows_loop(32, go, (zero, zero, zero))
    for row, v in ((0, g_b), (1, g_gain), (2, g_shift)):
        k.sg[row : row + 1, 0:D] = jnp.sum(v, axis=0, keepdims=True)
    k.hid[...] = dot_t(k.gb[...], wide(k.wa, 3)).astype(bf16)


def attend_back(k, pr):
    qp, kp, vp = k.q[pr], k.k[pr], k.v[pr]
    gm = k.hid[:, pl.ds(pl.multiple_of(128 * pr, 128), 128)]
    tq = tk = tv = None
    for hh in range(2):
        h = pr * 2 + hh
        hm = head_mask(hh)
        vm = vp * hm
        gate = k.gate[h]
        for c in range(4):
            k.s[128 * c : 128 * c + 128, :] = dot_t(vm[128 * c : 128 * c + 128], gm)
        d8 = jnp.zeros((8, PAD), f32)
        for c in range(16):
            rows = slice(32 * c, 32 * c + 32)
            d8 = d8 + fold(k.s[rows, :] * k.p[h, rows, :].astype(f32))
        total = jnp.sum(d8, axis=0, keepdims=True)
        gg = jnp.zeros((8, PAD), f32)
        k.a[...] = jnp.zeros((128, BIAS), f32)
        for c in range(16):
            rows = slice(32 * c, 32 * c + 32)
            part = slice(32 * (c % 4), 32 * (c % 4) + 32)
            lane = 384 - 128 * (c // 4)
            low = (k.p[h, rows, :].astype(f32) * (k.s[rows, :] - total)).astype(bf16)
            k.gs[rows, :] = low
            g = low.astype(f32)
            gg = gg + fold(g * k.bias[h, part, lane : lane + PAD].astype(f32))
            k.a[part, lane : lane + PAD] += g * gate
        k.ggate[h] = jnp.sum(gg, axis=0, keepdims=True)
        acc = k.a[0:8, :]
        for c in range(1, 16):
            acc = acc + pltpu.roll(k.a[8 * c : 8 * c + 8, :], BIAS - 8 * c, 1)
        flat = acc[0:1]
        for b in range(1, 8):
            flat = flat + pltpu.roll(acc, BIAS - b, 1)[b : b + 1]
        k.goff[h] = flat
        gs = k.gs[...]
        pv = dot(k.p[h], gm * hm)
        pq = dot_l(gs, kp * hm)
        pk = dot(gs, qp * hm)
        tv, tq, tk = (pv, pq, pk) if tv is None else (tv + pv, tq + pq, tk + pk)
    k.q[pr] = (tq.astype(bf16) * 0.125).astype(bf16)
    k.k[pr] = tk.astype(bf16)
    k.v[pr] = tv.astype(bf16)


def gate_back(k):
    weights, _, _, own = gate_weights(k)
    ggate = jnp.concatenate([k.ggate[h] for h in range(HEADS)] + [jnp.zeros((4, PAD), f32)], axis=0)
    first, second, factor = k.first[...], k.second[...], k.factor[...]
    df = ggate * (second * factor - 1.0) * first * (1.0 - first)
    ds = ggate * first * factor * second * (1.0 - second)
    dz = jnp.concatenate([df, ds], axis=0)
    gscale = jnp.sum(ggate * first * second, axis=1, keepdims=True)
    gw = dot(dz, k.tok[...].astype(f32), precision=highest)
    pick = lambda v: jnp.sum(jnp.where(own, v, 0.0), axis=0, keepdims=True)
    k.sg[14:15, 0:D] = pick(gw[0:16])
    k.sg[15:16, 0:D] = pick(gw[16:32])
    k.sg[14:15, D:] = jnp.broadcast_to(jnp.sum(jnp.sum(df, axis=0, keepdims=True), axis=1, keepdims=True), (1, 256))
    k.sg[15:16, D:] = jnp.broadcast_to(jnp.sum(jnp.sum(ds, axis=0, keepdims=True), axis=1, keepdims=True), (1, 256))
    goff = jnp.concatenate([k.goff[h] for h in range(HEADS)] + [jnp.zeros((4, BIAS), f32)], axis=0)
    rel = dot_t(goff, k.hot[...].astype(f32), precision=highest)
    for h in range(HEADS):
        at, i = 10 + h // 3, h % 3
        k.sg[at : at + 1, NB * i : NB * i + NB] = rel[h : h + 1]
        k.sg[at : at + 1, 960 + i : 961 + i] = gscale[h : h + 1]
    for t, src in ((0, k.q), (2, k.v)):
        row = jnp.sum(fold(mixed_all(src).astype(f32)), axis=0, keepdims=True)
        for p in range(4):
            at = 6 + p if t == 0 else p
            k.sg[at : at + 1, D : D + 192] = row[:, 192 * p : 192 * p + 192]
    k.fa[...] = dot(dz.T, weights)


def grad_input(k):
    for t, src in ((0, k.q), (1, k.k), (2, k.v)):
        k.fa[...] += dot(mixed_all(src), wide(k.wa, t))


def grad_rows(k, part):
    def go(rows, _):
        k.cot[rows, :] = (k.fb[rows, :] + k.fa[rows, :]).astype(bf16)
        return 0
    rows_loop(32, go, 0, *PARTS[part])


def grad_projections(k, part):
    own = lambda ref: jnp.concatenate([ref[3 * part + i] for i in range(3)], axis=1)
    for t, src, right in ((0, k.q, k.tok), (1, k.k, k.tok), (2, k.v, k.tok), (3, k.mixed, k.gb)):
        g = dot_l(own(src), right[...]).astype(bf16).reshape(2, 2, 96, D)
        for i in range(2):
            k.wa[t, 2 * part + i] = g[i]


def each(n, fn, k):
    def go(i, _):
        fn(k, i)
        return 0
    lax.fori_loop(0, n, go, 0)


COMPUTE_SCRATCH = dict(
    row=((1, BIAS), jnp.int32), hot=((NB, BIAS), bf16), tok=((PAD, D), bf16), cot=((PAD, D), bf16), sm=((4, 8, BIAS), f32), mask=((PAD, PAD), f32),
    first=((16, PAD), f32), second=((16, PAD), f32), factor=((16, PAD), f32), gate=((HEADS, 1, PAD), f32),
    bias=((HEADS, 128, 896), bf16), q=((PAIRS, PAD, 128), bf16), k=((PAIRS, PAD, 128), bf16),
    v=((PAIRS, PAD, 128), bf16), s=((PAD, PAD), f32), p=((HEADS, PAD, PAD), bf16), mixed=((PAIRS, PAD, 128), bf16),
    fa=((PAD, D), f32), fb=((PAD, D), f32), n1=((PAD, D), f32), inv1=((PAD, 128), f32), hid=((PAD, D), bf16),
    act=((4, PAD, D), bf16), dg=((4, PAD, D), bf16), out=((PAD, D), bf16), gb=((PAD, D), bf16),
    gs=((PAD, PAD), bf16), a=((128, BIAS), f32), ggate=((HEADS, 1, PAD), f32),
    goff=((HEADS, 1, BIAS), f32), sg=((16, BIAS), f32),
    wa=((4, 4, 2, 96, D), bf16), wi=((4, 8, 96, D), bf16), wo=((4, 8, 96, D), bf16),
)


MESH = pl.DeviceIdType.MESH
BLOCKS = (0, 1, 2)
WIDE = (2,)
SEMS = dict(
    wz=(3, 2, 3, 2), w1=(3, 2, 3), w2=(3, 2, 3, 2), w3=(3, 2, 3), sm=(3,), rows=(2, 2, 9), r1=(3, 4), r2=(3, 4, 2), r3=(3, 4),
    r4=(3, 2, 3), a1=(3,), a2=(3, 2), a3=(3,), sg=(6,),
)
COMM_SCRATCH = dict(
    rb1a=((4, 2, 2, 96, D), bf16), rb1=((2, 4, 4, 96, D), bf16), rb2=((3, 4, 2, 96, D), bf16),
    rb3=((3, 4, 96, D), bf16), rb4=((3, 2, 3, 96, D), bf16), sgr=((5, 16, BIAS), f32), sgs=((6, 16, BIAS), f32), fin=((16, BIAS), f32),
)


class Net:
    def __init__(self, k):
        self.k = k
        dp, z = lax.axis_index("dp"), lax.axis_index("tensor")
        self.dp, self.z = dp, z
        c, x, y = dp % 2, (dp // 2) % 2, (dp // 4) % 2
        self.c = c
        across_x, across_y = dp + 2 * (1 - 2 * x), dp + 4 * (1 - 2 * y)
        self.core = (dp + 1 - 2 * c, z)
        self.x, self.y = (across_x, z), (across_y, z)
        self.one = ((1 - c) * across_x + c * across_y, z)
        self.two = (c * across_x + (1 - c) * across_y, z)
        at = lambda cc, yy, xx: 4 * cc + 2 * yy + xx
        ex, ey = at(c, y, 1 - x), at(c, 1 - y, x)
        self.e = at(c, y, x)
        self.e1 = (1 - c) * ex + c * ey
        self.e2 = c * ex + (1 - c) * ey
        self.e12 = at(c, 1 - y, 1 - x)

    def ahead(self, dz):
        return (self.z + dz) % 4

    def behind(self, dz):
        return (self.z + 4 - dz) % 4

    def copy(self, name, index, src, dst, device):
        sems = getattr(self.k, "sem_" + name)
        return pltpu.make_async_remote_copy(
            src_ref=src, dst_ref=dst, send_sem=sems.at[(0, *index)], recv_sem=sems.at[(1, *index)],
            device_id=device, device_id_type=MESH,
        )

    def greet(self):
        barrier = pltpu.get_barrier_semaphore()
        peers = [self.core, self.one, self.two] + [(self.dp, self.ahead(dz)) for dz in (1, 2, 3)]
        for peer in peers:
            pl.semaphore_signal(barrier, inc=1, device_id=peer, device_id_type=MESH)

    def all_here(self):
        pl.semaphore_wait(pltpu.get_barrier_semaphore(), 6)

    def block(self, b):
        return (self.k.wa, self.k.wi, self.k.wo)[b]

    def chunk(self, b, p, e):
        return self.block(b).at[e // 2, p, e % 2] if b == 0 else self.block(b).at[p, e]

    def side(self, b, p, c):
        return self.block(b).at[pl.ds(2 * c, 2), p] if b == 0 else self.block(b).at[p, pl.ds(4 * c, 4)]

    def plane(self, way, j):
        return self.z - 1 - j if way == 0 else self.z + 1 + j

    def wz(self, b, way, j, i=0):
        ref = self.chunk(b, self.plane(way, j - 1), (self.e, self.e1)[i])
        return self.copy("wz", (b, way, j, i), ref, ref, (self.dp, self.z + 1 if way == 0 else self.z - 1))

    def w1(self, b, way, j):
        ref = self.chunk(b, self.plane(way, j), self.e)
        return self.copy("w1", (b, way, j), ref, ref, self.one)

    def w2(self, b, way, j, i):
        ref = self.chunk(b, self.plane(way, j), (self.e, self.e1)[i])
        return self.copy("w2", (b, way, j, i), ref, ref, self.two)

    def w3(self, b, way, j):
        ref = self.side(b, self.plane(way, j), self.c)
        return self.copy("w3", (b, way, j), ref, ref, self.core)

    def sm(self, d):
        ref = self.k.sm.at[self.z]
        return self.copy("sm", (d - 1,), ref, ref, (self.dp, self.ahead(d)))

    def rows(self, a, way, n):
        source, result = ((self.k.out, self.k.out_hbm), (self.k.cot, self.k.gtok_hbm))[a]
        j, (start, stop) = n // 3, PARTS[n % 3]
        size = min(stop, SEQ) - start
        slot = self.z - j if way == 0 else self.z + j
        to = self.z + 1 if way == 0 else self.z - 1
        at = result.at[pl.ds(pl.multiple_of(slot * SEQ + start, 16), size)]
        return self.copy("rows", (a, way, n), source.at[pl.ds(start, size)] if j == 0 else at, at, (self.dp, to))

    def sends(self, way, j):
        return (self.z <= 2) & (self.z >= j) if way == 0 else (self.z >= 1) & (self.z + j <= 3)

    def receives(self, way, j):
        return self.z >= 1 + j if way == 0 else self.z + 1 + j <= 3

    def r1(self, b, p):
        dst = self.k.rb1a.at[p] if b == 0 else self.k.rb1.at[b - 1, p]
        return self.copy("r1", (b, p), self.side(b, p, 1 - self.c), dst, self.core)

    def r2(self, b, p, i):
        return self.copy("r2", (b, p, i), self.chunk(b, p, (self.e1, self.e12)[i]), self.k.rb2.at[b, p, i], self.one)

    def r3(self, b, p):
        return self.copy("r3", (b, p), self.chunk(b, p, self.e2), self.k.rb3.at[b, p], self.two)

    def r4(self, b, way, p):
        to, i = (self.z + 1, p - 1) if way == 0 else (self.z - 1, p)
        return self.copy("r4", (b, way, i), self.chunk(b, p, self.e), self.k.rb4.at[b, way, i], (self.dp, to))

    def result(self, b, e):
        return (self.k.ra, self.k.ri, self.k.ro)[b].at[e]

    def keep(self, b):
        return pltpu.make_async_copy(self.chunk(b, self.z, self.e), self.result(b, self.e), self.k.sem_keep.at[b])

    def a1(self, b):
        return self.copy("a1", (b,), self.chunk(b, self.z, self.e), self.result(b, self.e), self.one)

    def a2(self, b, i):
        src = (self.chunk(b, self.z, self.e), self.result(b, self.e1))[i]
        return self.copy("a2", (b, i), src, self.result(b, (self.e, self.e1)[i]), self.two)

    def a3(self, b):
        ref = self.result(b, pl.ds(4 * self.c, 4))
        return self.copy("a3", (b,), ref, ref, self.core)

    def sg(self, i):
        k, half = self.k, pl.ds(8 * self.c, 8)
        if i < 3:
            return self.copy("sg", (i,), k.sgs.at[i], k.sgr.at[i], (self.core, self.x, self.y)[i])
        if i < 5:
            device = (self.dp, self.flip(1 if i == 3 else 2))
            return self.copy("sg", (i,), k.sgs.at[i, half], k.sgr.at[i, half], device)
        return self.copy("sg", (i,), k.sgs.at[5, half], k.sgs.at[5, half], self.core)

    def flip(self, bit):
        return self.z + bit * (1 - 2 * ((self.z // bit) % 2))


def loop(n, fn):
    def go(i, _):
        fn(i)
        return 0
    lax.fori_loop(0, n, go, 0)


def when(condition, fn):
    @pl.when(condition)
    def _():
        fn()


ORDER = (3, 0, 2, 1)


def weight_own(net, b):
    for way in (0, 1):
        for i in range(1 + (b in WIDE)):
            when(net.sends(way, 0), lambda: net.wz(b, way, 0, i).start())


def weight_one(net, b, way, j):
    def step():
        for i in range(1 + (b in WIDE)):
            net.wz(b, way, j, i).wait_recv()
            if j < 2:
                when(net.sends(way, j + 1), lambda: net.wz(b, way, j + 1, i).start())
        if b not in WIDE:
            net.w1(b, way, j).start()
    when(net.receives(way, j), step)


def weight_two(net, b, way, j):
    def step():
        if b not in WIDE:
            net.w1(b, way, j).wait_recv()
        net.w2(b, way, j, 0).start()
        net.w2(b, way, j, 1).start()
    when(net.receives(way, j), step)


def weight_core(net, b, way, j):
    def step():
        net.w2(b, way, j, 0).wait_recv()
        net.w2(b, way, j, 1).wait_recv()
        net.w3(b, way, j).start()
    when(net.receives(way, j), step)


def weight_there(net, b, way, j):
    when(net.receives(way, j), lambda: net.w3(b, way, j).wait_recv())


def weights_sent(net):
    for b in BLOCKS:
        for way in (0, 1):
            for j in range(3):
                def along():
                    for i in range(1 + (b in WIDE)):
                        net.wz(b, way, j, i).wait_send()
                def inside():
                    if b not in WIDE:
                        net.w1(b, way, j).wait_send()
                    net.w2(b, way, j, 0).wait_send()
                    net.w2(b, way, j, 1).wait_send()
                    net.w3(b, way, j).wait_send()
                when(net.sends(way, j), along)
                when(net.receives(way, j), inside)


def rows_own(net, a, part):
    for way in (0, 1):
        when(net.sends(way, 0), lambda: net.rows(a, way, part).start())


def rows_next(net, a, way, n):
    when(net.receives(way, (n - 1) // 3), lambda: net.rows(a, way, n - 1).wait_recv())
    if n + 2 < 9:
        when(net.sends(way, (n + 2) // 3), lambda: net.rows(a, way, n + 2).start())


def rows_sent(net, a):
    for n in range(9):
        for way in (0, 1):
            when(net.sends(way, n // 3), lambda: net.rows(a, way, n).wait_send())


def add(net, b, p, e, ref):
    k = net.k
    if b == 0:
        k.wa[e // 2, p, e % 2] = k.wa[e // 2, p, e % 2] + ref[...]
    else:
        net.block(b)[p, e] = net.block(b)[p, e] + ref[...]


def halves(net, b, p):
    net.r1(b, p).wait_recv()
    for j in range(4):
        src = net.k.rb1a.at[p, j // 2, j % 2] if b == 0 else net.k.rb1.at[b - 1, p, j]
        add(net, b, p, 4 * net.c + j, src)
    net.r2(b, p, 1).start()
    net.r2(b, p, 0).start()


def quarters(net, b, p):
    net.r2(b, p, 1).wait_recv()
    add(net, b, p, net.e2, net.k.rb2.at[b, p, 1])
    net.r3(b, p).start()
    net.r2(b, p, 0).wait_recv()
    add(net, b, p, net.e, net.k.rb2.at[b, p, 0])


def eighths(net, b, p):
    net.r3(b, p).wait_recv()
    add(net, b, p, net.e, net.k.rb3.at[b, p])
    if p > 0:
        when(net.z == 0, lambda: net.r4(b, 0, p).start())
    if p < 3:
        when(net.z == 3, lambda: net.r4(b, 1, p).start())


def chain(net, b, p):
    def link(way, i):
        net.r4(b, way, p).wait_recv()
        add(net, b, p, net.e, net.k.rb4.at[b, way, i])
        net.r4(b, way, p).start()
    if p > 1:
        when((net.z > 0) & (net.z < p), lambda: link(0, p - 1))
    if p < 2:
        when((net.z > p) & (net.z < 3), lambda: link(1, p))


def over_z(net, b):
    k, z = net.k, net.z
    def last(way, i):
        net.r4(b, way, z).wait_recv()
        add(net, b, z, net.e, k.rb4.at[b, way, i])
    when(z > 0, lambda: last(0, z - 1))
    when(z < 3, lambda: last(1, z))
    net.keep(b).start()
    net.a1(b).start()
    net.a2(b, 0).start()


def around(net, b):
    net.a1(b).wait_recv()
    net.a2(b, 1).start()


def to_core(net, b):
    net.keep(b).wait()
    net.a2(b, 0).wait_recv()
    net.a2(b, 1).wait_recv()
    net.a3(b).start()


def gradients_sent(net, b):
    net.a3(b).wait_recv()
    for p in range(4):
        net.r1(b, p).wait_send()
        net.r2(b, p, 0).wait_send()
        net.r2(b, p, 1).wait_send()
        net.r3(b, p).wait_send()
    for p in range(4):
        when(net.z < p, lambda: net.r4(b, 0, p).wait_send())
        when(net.z > p, lambda: net.r4(b, 1, p).wait_send())
    net.a1(b).wait_send()
    net.a2(b, 0).wait_send()
    net.a2(b, 1).wait_send()
    net.a3(b).wait_send()


def halves_out(net, b, p):
    net.r1(b, p).start()


def small_sum(net, i):
    k, half = net.k, pl.ds(8 * net.c, 8)
    if i == 0:
        k.sgs[0] = k.sg[...]
    else:
        net.sg(i - 1).wait_recv()
    if 0 < i < 4:
        k.sgs[i] = k.sgs[i - 1] + k.sgr[i - 1]
    elif 3 < i < 6:
        k.sgs[i, half, :] = k.sgs[i - 1, half, :] + k.sgr[i - 1, half, :]
    if i < 6:
        net.sg(i).start()


PLAN = (
    (
        (weight_own, 0), (weight_own, 1),
    ),
    (),
    (
        (weight_one, 0, 1, 0), (weight_one, 0, 0, 0), (weight_one, 1, 0, 0), (weight_two, 0, 1, 0),
        (weight_one, 0, 1, 1), (weight_one, 0, 0, 1), (weight_one, 1, 1, 0), (weight_two, 0, 0, 0), (weight_own, 2),
        (weight_core, 0, 1, 0), (weight_one, 0, 1, 2), (weight_two, 0, 1, 1), (weight_two, 0, 0, 1),
        (weight_one, 0, 0, 2), (weight_two, 1, 0, 0), (weight_two, 0, 1, 2),
    ),
    (
        (weight_core, 0, 0, 0), (weight_two, 0, 0, 2), (weight_one, 1, 0, 1), (weight_there, 0, 1, 0),
    ),
    (
        (weight_one, 1, 1, 1), (weight_two, 1, 1, 0), (weight_core, 0, 0, 1), (weight_core, 0, 1, 1),
        (weight_one, 2, 0, 0), (weight_one, 2, 1, 0), (weight_core, 0, 1, 2), (weight_there, 0, 1, 1),
        (weight_one, 1, 0, 2), (weight_core, 0, 0, 2), (weight_there, 0, 0, 1), (weight_two, 2, 1, 0),
        (weight_there, 0, 0, 0), (weight_there, 0, 1, 2), (weight_core, 1, 0, 0), (weight_one, 1, 1, 2),
        (weight_two, 2, 0, 0), (weight_two, 1, 0, 2), (weight_two, 1, 0, 1), (weight_there, 0, 0, 2),
    ),
    (
        (weight_two, 1, 1, 1),
    ),
    (
        (weight_core, 1, 1, 0),
    ),
    (
        (weight_one, 2, 1, 1), (weight_two, 2, 1, 1), (weight_one, 2, 0, 1), (weight_two, 1, 1, 2),
    ),
    (
        (weight_core, 1, 0, 2), (weight_core, 2, 1, 0), (weight_two, 2, 0, 1),
    ),
    (),
    (),
    (
        (weight_one, 2, 1, 2), (weight_two, 2, 1, 2), (weight_core, 1, 0, 1), (weight_one, 2, 0, 2),
        (weight_two, 2, 0, 2), (weight_core, 2, 0, 0), (weight_there, 1, 0, 2), (weight_core, 1, 1, 1),
    ),
    (
        (weight_there, 1, 0, 1), (weight_core, 2, 0, 1), (weight_core, 2, 1, 1),
    ),
    (),
    (
        (weight_core, 2, 0, 2), (weight_there, 1, 0, 0), (weight_there, 1, 1, 0), (weight_there, 2, 1, 0),
    ),
    (
        (weight_core, 2, 1, 2), (weight_there, 1, 1, 1), (weight_there, 2, 0, 0),
    ),
    (
        (weight_core, 1, 1, 2), (weight_there, 2, 0, 1),
    ),
    (),
    (),
    (
        (weight_there, 2, 0, 2),
    ),
    (
        (weight_there, 2, 1, 1),
    ),
    (),
    (),
    (),
    (
        (weight_there, 1, 1, 2),
    ),
    (
        (weight_there, 2, 1, 2),
    ),
    (),
    (
        (rows_own, 0, 0),
    ),
    (
        (rows_own, 0, 1),
    ),
    (),
    (
        (rows_own, 0, 2), (halves_out, 2, 3), (halves_out, 1, 3),
    ),
    (
        (halves_out, 2, 0), (rows_next, 0, 1, 1), (rows_next, 0, 0, 1), (halves_out, 1, 0), (halves, 2, 3),
    ),
    (
        (halves_out, 1, 2), (halves_out, 2, 2), (rows_next, 0, 1, 2), (halves, 1, 3), (halves, 2, 0),
        (rows_next, 0, 0, 2),
    ),
    (
        (rows_next, 0, 0, 3), (halves_out, 1, 1), (halves, 1, 0), (halves, 2, 2), (rows_next, 0, 1, 3),
    ),
    (
        (rows_next, 0, 1, 4), (halves, 1, 2), (rows_next, 0, 1, 5),
    ),
    (),
    (
        (rows_next, 0, 0, 4),
    ),
    (
        (halves, 1, 1), (rows_next, 0, 1, 6),
    ),
    (
        (rows_next, 0, 0, 5),
    ),
    (),
    (),
    (),
    (
        (rows_own, 1, 0), (quarters, 2, 0), (small_sum, 0),
    ),
    (
        (rows_next, 0, 0, 6), (quarters, 1, 0), (halves_out, 2, 1), (rows_own, 1, 1), (quarters, 2, 3),
    ),
    (),
    (
        (halves_out, 0, 0), (quarters, 1, 3), (quarters, 1, 1), (halves_out, 0, 1),
    ),
    (
        (halves_out, 0, 2), (rows_own, 1, 2), (quarters, 1, 2), (halves, 0, 0), (rows_next, 1, 0, 1), (eighths, 1, 0),
        (halves, 2, 1), (rows_next, 1, 1, 1), (rows_next, 1, 1, 2), (halves_out, 0, 3), (rows_next, 0, 0, 7),
        (quarters, 0, 0), (eighths, 2, 3), (eighths, 2, 0), (eighths, 1, 3), (halves, 0, 1), (quarters, 2, 2),
        (quarters, 2, 1), (eighths, 1, 1), (small_sum, 1), (eighths, 0, 0), (rows_next, 1, 0, 2), (halves, 0, 3),
        (eighths, 1, 2), (rows_next, 1, 0, 3), (rows_next, 0, 1, 7), (quarters, 0, 1), (chain, 2, 0),
        (rows_next, 1, 0, 4), (halves, 0, 2), (chain, 1, 0), (chain, 1, 2), (eighths, 2, 1), (eighths, 2, 2),
        (small_sum, 2), (chain, 0, 0), (chain, 1, 1), (chain, 2, 1), (chain, 1, 3), (quarters, 0, 3), (eighths, 0, 1),
        (rows_next, 1, 1, 3), (rows_next, 1, 1, 4), (quarters, 0, 2), (over_z, 1), (chain, 2, 3), (small_sum, 3),
        (chain, 0, 1), (rows_next, 0, 0, 8), (eighths, 0, 3), (eighths, 0, 2), (chain, 2, 2), (rows_next, 1, 1, 5),
        (over_z, 2), (around, 1), (chain, 0, 3), (rows_next, 1, 0, 5), (rows_next, 1, 0, 6), (around, 2),
        (small_sum, 4), (chain, 0, 2), (over_z, 0), (rows_next, 1, 1, 6), (rows_next, 1, 1, 7), (rows_next, 0, 1, 8),
        (to_core, 1), (rows_next, 0, 1, 9), (to_core, 2), (around, 0), (rows_next, 1, 1, 8), (rows_next, 0, 0, 9),
        (small_sum, 5), (to_core, 0), (small_sum, 6), (rows_next, 1, 0, 7), (rows_next, 1, 1, 9),
        (rows_next, 1, 0, 8), (rows_next, 1, 0, 9),
    ),
)


def kernel(names, *refs):
    k = K()
    for name, ref in zip(names, refs):
        setattr(k, name, ref)
    net = Net(k)
    z = net.z
    own_rows = pl.ds(pl.multiple_of(z * SEQ, 16), SEQ)
    moves = [
        (k.wq_hbm, k.wa.at[0, z]), (k.wk_hbm, k.wa.at[1, z]), (k.wv_hbm, k.wa.at[2, z]), (k.wout_hbm, k.wa.at[3, z]),
        (k.wi_hbm, k.wi.at[z]), (k.wo_hbm, k.wo.at[z]),
        (k.tok_hbm.at[own_rows], k.tok.at[pl.ds(0, SEQ)]), (k.cot_hbm.at[own_rows], k.cot.at[pl.ds(0, SEQ)]),
    ]
    local = [pltpu.make_async_copy(src, dst, k.sem_in.at[i]) for i, (src, dst) in enumerate(moves)]
    for c in local:
        c.start()
    run = lambda n: [step(net, *given) for step, *given in PLAN[n]]
    net.greet()
    k.tok[SEQ:PAD] = jnp.zeros((PAD - SEQ, D), bf16)
    k.cot[SEQ:PAD] = jnp.zeros((PAD - SEQ, D), bf16)
    k.sg[...] = jnp.zeros((16, BIAS), f32)
    k.factor[...] = jnp.zeros((16, PAD), f32)
    k.fb[...] = jnp.zeros((PAD, D), f32)
    for c in local[0:6]:
        c.wait()
    net.all_here()
    run(0)
    own_small(k, z)
    for d in (1, 2, 3):
        net.sm(d).start()
    run(1)
    mask_build(k, z)
    run(2)
    for d in (1, 2, 3):
        net.sm(d).wait_recv()
    for c in local[6:8]:
        c.wait()
    gates(k)
    run(3)
    bias_tables(k)
    run(4)
    project(k)
    run(5)

    def forward(pr):
        attend(k, pr)
        for n in range(PAIRS):
            when(pr == n, lambda: run(6 + n))
    loop(PAIRS, forward)
    norm_one(k)
    run(12)

    feed_in(k, z)
    run(13)
    feed_out(k, z)
    run(14)
    last = 3 - 3 * (z // 2)

    def layer_two(n):
        p = z + (2 * (n % 2) - 1) * (1 + n // 2)
        when((p >= 0) & (p <= 3), lambda: feed_in(k, p))
        for i in range(6):
            when(n == i, lambda: run(15 + 2 * i))
        when((p >= 0) & (p <= 3) & (p != last), lambda: feed_out(k, p))
        for i in range(6):
            when(n == i, lambda: run(16 + 2 * i))
    loop(6, layer_two)
    here = [
        pltpu.make_async_copy(k.out.at[pl.ds(0, SEQ)], k.out_hbm.at[own_rows], k.sem_in.at[0]),
        pltpu.make_async_copy(k.cot.at[pl.ds(0, SEQ)], k.gtok_hbm.at[own_rows], k.sem_in.at[1]),
    ]
    for part in range(3):
        feed_out(k, last, *PARTS[part])
        norm_two(k, part)
        run(27 + part)
    here[0].start()
    weights_sent(net)

    def layer_two_back(i):
        feed_back(k, (1 - i % 2) * (3 - i // 2) + (i % 2) * (i // 2))
        for n in range(4):
            when(i == n, lambda: run(30 + n))
    loop(4, layer_two_back)
    norm_one_back(k)
    run(34)

    def backward(pr):
        attend_back(k, pr)
        for n in range(PAIRS):
            when(pr == n, lambda: run(35 + n))
    loop(PAIRS, backward)
    gate_back(k)
    run(41)
    grad_input(k)
    for part in range(3):
        grad_rows(k, part)
        run(42 + part)
    here[1].start()
    for part in (0, 1):
        grad_projections(k, part)
        run(45 + part)
    k.fin[...] = jnp.zeros((16, BIAS), f32)
    k.fin[0:6, :] = k.sgs[5, 0:6, :]
    for at, start in ((6, 6), (7, 10), (8, 0)):
        k.fin[at : at + 1, :] = k.sgs[5, pl.ds(start + z, 1), :]
    k.fin[9:11, :] = k.sgs[5, 14:16, :]
    finish = pltpu.make_async_copy(k.fin, k.sg_hbm, k.sem_in.at[2])
    finish.start()
    for b in (2, 1, 0):
        gradients_sent(net, b)
    for i in range(6):
        net.sg(i).wait_send()
    for d in (1, 2, 3):
        net.sm(d).wait_send()
    for a in (0, 1):
        rows_sent(net, a)
    here[0].wait()
    here[1].wait()
    finish.wait()


def finish_kernel(out, gtok, ra, ri, ro, sg, *rest):
    names = FINAL + ("stage", "wide", "rows", "sem")
    k = K()
    for name, ref in zip(names, rest):
        setattr(k, name, ref)
    count = iter(range(64))
    def copy(src, dst):
        c = pltpu.make_async_copy(src, dst, k.sem.at[next(count)])
        c.start()
        return c
    parts = [pl.ds(4 * i, 4) for i in (0, 1)]
    size = out.shape[0] // 4
    inward = [[copy(src.at[part], k.stage.at[i, part]) for part in parts] for i, src in enumerate((ri, ro, ra))]
    pairs = [(src, k.rows.at[i], dst) for i, (src, dst) in enumerate(((out, k.output), (gtok, k.grad_tokens)))]
    moves = [(src.at[at], via.at[at], dst.at[at]) for src, via, dst in pairs for at in [pl.ds(size * i, size) for i in range(4)]]
    copies = [copy(src, via) for src, via, _ in moves]
    row = lambda r, lane, n: sg[r : r + 1, lane : lane + n].reshape(n)
    k.b_out[...], k.norm1_gain[...], k.norm1_bias[...] = row(0, 0, D), row(1, 0, D), row(2, 0, D)
    k.b_outer[...], k.norm2_gain[...], k.norm2_bias[...] = row(3, 0, D), row(4, 0, D), row(5, 0, D)
    k.b_inner[...], k.b_query[...], k.b_value[...] = row(6, 0, D), row(6, D, 192), row(8, D, 192)
    for i in range(3):
        k.rel_table[i : i + 1, :] = sg[7:8, NB * i : NB * i + NB]
    lane = lax.broadcasted_iota(jnp.int32, (1, 128), 1)
    cell = lambda r, at: sg[r : r + 1, at : at + 128]
    k.gate_scale[...] = sg[7:8, 960:963]
    k.gate_bias[...] = jnp.where(lane < 4, cell(9, D), cell(10, D))[:, 0:8]
    for i in (0, 1):
        heads = cell(9 + i, 0)
        for pr in range(1, PAIRS):
            heads = heads + cell(9 + i, 128 * pr)
        k.gate_weight[4 * i : 4 * i + 4, :] = jnp.broadcast_to(heads[:, 0:HEAD] + heads[:, HEAD:128], (4, HEAD))
    outward = []
    def pass_rows(n):
        copies[n].wait()
        outward.append(copy(moves[n][1], moves[n][2]))
    for i in range(3):
        for j in (0, 1):
            inward[i][j].wait()
            def widen(n):
                k.wide[i, 4 * j + n] = k.stage[i, 4 * j + n].astype(f32)
            loop(4, widen)
            if i < 2:
                outward.append(copy(k.wide.at[i, parts[j]], (k.w_inner, k.w_outer)[i].at[parts[j]]))
            else:
                for n, ref in enumerate(((k.w_query, k.w_key), (k.w_value, k.w_out))[j]):
                    outward.append(copy(k.wide.at[i, pl.ds(4 * j + 2 * n, 2)], ref))
            pass_rows(2 * i + j)
    pass_rows(6)
    pass_rows(7)
    for c in outward:
        c.wait()


FINAL = (
    "output", "grad_tokens", "w_query", "w_key", "w_value", "w_out", "w_inner", "w_outer", "b_query", "b_value", "b_out",
    "gate_weight", "gate_bias", "gate_scale", "rel_table", "norm1_gain", "norm1_bias", "b_inner", "b_outer", "norm2_gain",
    "norm2_bias",
)


def body(
    tokens, slot_kind, offset_bucket, w_query, b_query, w_key, w_value, b_value, w_out, b_out, gate_weight, gate_bias,
    gate_scale, rel_table, norm1_gain, norm1_bias, w_inner, b_inner, w_outer, b_outer, norm2_gain, norm2_bias, cotangent,
):
    n_dp = lax.axis_size("dp")
    rows = tokens.shape[0]
    shape = jax.ShapeDtypeStruct
    anywhere = pl.BlockSpec(memory_space=pl.ANY)
    vmem = pl.BlockSpec(memory_space=pltpu.VMEM)
    smem = pl.BlockSpec(memory_space=pltpu.SMEM)
    given = dict(
        kinds=(smem, slot_kind), bucket=(vmem, offset_bucket.reshape(1, OFFSETS)), rel=(vmem, rel_table.T),
        b_query=(vmem, b_query), b_value=(vmem, b_value), b_inner=(vmem, b_inner), scale=(vmem, gate_scale.reshape(1, 3)),
        gw=(vmem, gate_weight.T), gate_bias=(vmem, gate_bias), b_out=(vmem, b_out), b_outer=(vmem, b_outer),
        norm1_gain=(vmem, norm1_gain), norm1_bias=(vmem, norm1_bias), norm2_gain=(vmem, norm2_gain),
        norm2_bias=(vmem, norm2_bias), tok_hbm=(anywhere, tokens), cot_hbm=(anywhere, cotangent),
        wq_hbm=(anywhere, w_query.T.reshape(2, 96, D)), wk_hbm=(anywhere, w_key.T.reshape(2, 96, D)),
        wv_hbm=(anywhere, w_value.T.reshape(2, 96, D)), wout_hbm=(anywhere, w_out.reshape(2, 96, D)),
        wi_hbm=(anywhere, w_inner.reshape(8, 96, D)), wo_hbm=(anywhere, w_outer.reshape(8, 96, D)),
    )
    names = list(given) + ["out_hbm", "gtok_hbm", "ra", "ri", "ro", "sg_hbm"]
    scratch = []
    for name, (dims, dtype) in (COMPUTE_SCRATCH | COMM_SCRATCH).items():
        names.append(name)
        scratch.append(pltpu.VMEM(dims, dtype))
    for name, dims in SEMS.items():
        names.append("sem_" + name)
        scratch.append(pltpu.SemaphoreType.DMA((2, *dims)))
    for name, count in (("sem_in", 8), ("sem_keep", 3)):
        names.append(name)
        scratch.append(pltpu.SemaphoreType.DMA((count,)))
    whole = shape((8, 96, D), bf16)
    out, gtok, ra, ri, ro, sg = pl.pallas_call(
        functools.partial(kernel, names),
        in_specs=[spec for spec, _ in given.values()],
        out_specs=[anywhere] * 6,
        out_shape=[shape((rows, D), bf16), shape((rows, D), bf16), whole, whole, whole, shape((16, BIAS), f32)],
        scratch_shapes=scratch,
        compiler_params=pltpu.CompilerParams(collective_id=0, has_side_effects=True, vmem_limit_bytes=VMEM_LIMIT),
    )(*[value for _, value in given.values()])
    if n_dp > 8:
        groups = [list(range(g, n_dp, 8)) for g in range(8)]
        ra, ri, ro, sg = lax.psum((ra.astype(f32), ri.astype(f32), ro.astype(f32), sg), "dp", axis_index_groups=groups)
        ra, ri, ro = ra.astype(bf16), ri.astype(bf16), ro.astype(bf16)
    vector = shape((D,), f32)
    part = shape((2, 96, D), f32)
    final = dict(
        output=(anywhere, shape((rows, D), bf16)), grad_tokens=(anywhere, shape((rows, D), bf16)),
        w_query=(anywhere, part), w_key=(anywhere, part), w_value=(anywhere, part), w_out=(anywhere, part),
        w_inner=(anywhere, shape((8, 96, D), f32)), w_outer=(anywhere, shape((8, 96, D), f32)),
        b_query=(vmem, shape((192,), f32)), b_value=(vmem, shape((192,), f32)), gate_weight=(vmem, shape((8, HEAD), f32)),
        gate_bias=(vmem, shape((1, 8), f32)), gate_scale=(vmem, shape((1, 3), f32)), rel_table=(vmem, shape((3, NB), f32)),
    )
    specs, shapes = zip(*[final.get(name, (vmem, vector)) for name in FINAL])
    results = pl.pallas_call(
        finish_kernel,
        in_specs=[anywhere] * 5 + [vmem],
        out_specs=list(specs),
        out_shape=list(shapes),
        scratch_shapes=[pltpu.VMEM((3, 8, 96, D), bf16), pltpu.VMEM((3, 8, 96, D), f32), pltpu.VMEM((2, rows, D), bf16), pltpu.SemaphoreType.DMA((40,))],
        compiler_params=pltpu.CompilerParams(vmem_limit_bytes=VMEM_LIMIT),
    )(out, gtok, ra, ri, ro, sg)
    r = dict(zip(FINAL, results))
    for name in ("w_query", "w_key", "w_value"):
        r[name] = r[name].reshape(192, D).T
    r["w_out"] = r["w_out"].reshape(192, D)
    r["w_inner"] = r["w_inner"].reshape(D, D)
    r["w_outer"] = r["w_outer"].reshape(D, D)
    r["gate_weight"] = r["gate_weight"].T
    r["gate_bias"] = r["gate_bias"].reshape(8)
    r["gate_scale"] = r["gate_scale"].reshape(3)
    r["rel_table"] = r["rel_table"].T
    order = (
        "output", "grad_tokens", "w_query", "b_query", "w_key", "w_value", "b_value", "w_out", "b_out", "gate_weight",
        "gate_bias", "gate_scale", "rel_table", "norm1_gain", "norm1_bias", "w_inner", "b_inner", "w_outer", "b_outer",
        "norm2_gain", "norm2_bias",
    )
    return tuple(r[name] for name in order)


def solution(mesh):
    in_specs = (
        P("dp", None),
        P("dp"),
        P(),
        P(None, "tensor"),
        P("tensor"),
        P(None, "tensor"),
        P(None, "tensor"),
        P("tensor"),
        P("tensor", None),
        P(),
        P(),
        P(),
        P("tensor"),
        P(None, "tensor"),
        P(),
        P(),
        P(None, "tensor"),
        P("tensor"),
        P("tensor", None),
        P(),
        P(),
        P(),
        P("dp", None),
    )
    out_specs = (
        P("dp", None),
        P("dp", None),
        P(None, "tensor"),
        P("tensor"),
        P(None, "tensor"),
        P(None, "tensor"),
        P("tensor"),
        P("tensor", None),
        P(),
        P(),
        P(),
        P("tensor"),
        P(None, "tensor"),
        P(),
        P(),
        P(None, "tensor"),
        P("tensor"),
        P("tensor", None),
        P(),
        P(),
        P(),
    )
    return jax.shard_map(body, mesh=mesh, in_specs=in_specs, out_specs=out_specs, check_vma=False)
```
